32 devices in a mesh: rows: 8 (over y, x, core), mlp: 4 (over z).
Axes of the slice: x: 2, y: 2, z: 4, core: 2. Of those that a mesh axis runs over, the one named last changes fastest.
Arguments:
- tokens: bfloat16 [65536, 1024], P(('rows', 'mlp')), may hold values from -6 to 6
- doc_lengths: int32 [64, 4], P(('rows', 'mlp')), may hold values from 1 to 512, 1024 in all within a row
- cotangent: bfloat16 [65536, 1024], P(('rows', 'mlp')), may hold values from -6 to 6
- norm_gain_mix: bfloat16 [1024], P(('rows', 'mlp')), may hold values from 0.5 to 1.5
- w_query: bfloat16 [1024, 512], P(('rows', 'mlp')), may hold values from -0.1875 to 0.1875
- w_key: bfloat16 [1024, 512], P(('rows', 'mlp')), may hold values from -0.1875 to 0.1875
- w_value: bfloat16 [1024, 1024], P(('rows', 'mlp')), may hold values from -0.1875 to 0.1875
- w_outgate: bfloat16 [1024, 1024], P(('rows', 'mlp')), may hold values from -0.1875 to 0.1875
- w_rank: bfloat16 [1024, 16], P(('rows', 'mlp')), may hold values from -0.1875 to 0.1875
- w_decay: bfloat16 [16, 512], replicated, may hold values from -1.5 to 1.5
- decay_bias: bfloat16 [512], replicated, may hold values from 0.5 to 5
- head_gain: bfloat16 [256], replicated, may hold values from 0.5 to 1.5
- w_output: bfloat16 [1024, 1024], P(None, ('rows', 'mlp')), may hold values from -0.375 to 0.375
- norm_gain_mlp: bfloat16 [1024], P(('rows', 'mlp')), may hold values from 0.5 to 1.5
- w_gate: bfloat16 [1024, 2816], P('rows', 'mlp'), may hold values from -0.1875 to 0.1875
- w_up: bfloat16 [1024, 2816], P('rows', 'mlp'), may hold values from -0.1875 to 0.1875
- w_down: bfloat16 [2816, 1024], P('mlp', 'rows'), may hold values from -0.21875 to 0.21875
Outputs:
- block_out: bfloat16 [65536, 1024], P(('rows', 'mlp'))
- grad_tokens: float32 [65536, 1024], P(('rows', 'mlp'))
- grad_norm_mix: float32 [1024], P(('rows', 'mlp'))
- grad_w_query: float32 [1024, 512], P(('rows', 'mlp'))
- grad_w_key: float32 [1024, 512], P(('rows', 'mlp'))
- grad_w_value: float32 [1024, 1024], P(('rows', 'mlp'))
- grad_w_outgate: float32 [1024, 1024], P(('rows', 'mlp'))
- grad_w_rank: float32 [1024, 16], P(('rows', 'mlp'))
- grad_w_decay: float32 [16, 512], replicated
- grad_decay_bias: float32 [512], replicated
- grad_head_gain: float32 [256], replicated
- grad_w_output: float32 [1024, 1024], P(None, ('rows', 'mlp'))
- grad_norm_mlp: float32 [1024], P(('rows', 'mlp'))
- grad_w_gate: float32 [1024, 2816], P('rows', 'mlp')
- grad_w_up: float32 [1024, 2816], P('rows', 'mlp')
- grad_w_down: float32 [2816, 1024], P('mlp', 'rows')
The draws below stay inside these ranges and needn't reach their ends.
Inputs may be any that keep to these rules, and one draw needn't show every extreme that they name: `doc_lengths`: each row holds the lengths of 4 documents that fill one sequence of 1024 tokens in order; the longest is 512.
All inputs are finite; a program needn't handle non-finite values.
Results may differ from the reference program's by a relative error of at most 0.019.
Values may be sent and summed in bfloat16 or wider, within the bound.
No kernel may reach another device: no remote copies, remote signals or barrier semaphores. Data moves between devices by JAX's collectives and lax.ppermute only.
A program may use at most 448 MiB of HBM per device.

```python
import math
import jax
import jax.numpy as jnp
import numpy as np
from jax import lax

D = 1024
H = 4
DK = 512
DV = 1024
R = 16
FF = 2816
BLOCK = 64
LEN = 1024
NDOC = 4
HK = 128
HV = 256
NC = 16
SEQUENCES = 64
TOKENS = 65536


def block_scale(rng, extent, shards, smallest, top_value):
    factor_of = 1.0
    for axis_at, shards_of in shards:
        steps = jax.random.uniform(jax.random.fold_in(jax.random.fold_in(rng, 6), axis_at), (shards_of,), jnp.float32, smallest / len(shards), top_value / len(shards))
        factor_of = factor_of * jnp.repeat(jnp.exp(steps), extent[axis_at] // shards_of).reshape((-1,) + (1,) * (len(extent) - 1 - axis_at))
    return factor_of


def profile(number_of, total, limit, lean):
    portions = [(1 << 20) // math.isqrt(grade ** lean) + 1 for grade in range(2, number_of + 1)]
    spare, given = total - limit - (number_of - 1), [1] * (number_of - 1)
    while spare > 0:
        free = [i for i in range(number_of - 1) if given[i] < limit]
        mass, left = sum([portions[i] for i in free]), spare
        for i in free:
            addition = min(limit - given[i], max(1, left * portions[i] // mass), spare)
            given[i] = given[i] + addition
            spare = spare - addition
    return np.array([limit] + given)


def uneven_parts(own_key, number_of, total, bound, lean):
    if number_of == 2:
        one = jax.random.randint(own_key, (), max(1, total - bound), min(bound, total - 1) + 1)
        return jnp.stack([one, total - one])
    sizes = jnp.asarray(profile(number_of, total, bound, lean), jnp.int32)
    pairs = (number_of - 1) // 2
    donor, sink = sizes[1:1 + 2 * pairs:2], sizes[2:2 + 2 * pairs:2]
    slack = jnp.minimum(donor - 1, bound - sink)
    moved = jax.random.randint(jax.random.fold_in(own_key, 1), (pairs,), 0, 1 << 20) % (slack + 1)
    sizes = sizes.at[1:1 + 2 * pairs:2].set(donor - moved).at[2:2 + 2 * pairs:2].set(sink + moved)
    return sizes[jax.random.permutation(jax.random.fold_in(own_key, 2), number_of)]


def scatter_about(stream_key, dims, spread, most, cuts=(), kind=jnp.bfloat16):
    factor_of = block_scale(stream_key, dims, cuts, -0.22, 0.18) if cuts else 1.0
    drawn = jax.random.normal(stream_key, dims, jnp.float32) * spread * factor_of
    return jnp.minimum(jnp.maximum(drawn, -most), most).astype(kind)


def setup_inputs(seed: int = 0) -> dict:
    key_of = jax.random.split(jax.random.key(seed), 18)
    return {
        "tokens": scatter_about(key_of[0], (TOKENS, D), 1.0, 6.0, ((0, 32),)),
        "doc_lengths": jax.vmap(lambda own: uneven_parts(own, NDOC, LEN, LEN // 2, 0))(jax.random.split(key_of[1], SEQUENCES)).reshape((SEQUENCES, NDOC)).astype(jnp.int32),
        "cotangent": scatter_about(key_of[2], (TOKENS, D), 1.0, 6.0, ((0, 32),)),
        "norm_gain_mix": jnp.clip(1.0 + 0.1 * jax.random.normal(key_of[3], (D,), jnp.float32), 0.5, 1.5).astype(jnp.bfloat16),
        "w_query": scatter_about(key_of[4], (D, DK), D ** -0.5, 0.1875, ((0, 32),)),
        "w_key": scatter_about(key_of[5], (D, DK), D ** -0.5, 0.1875, ((0, 32),)),
        "w_value": scatter_about(key_of[6], (D, DV), D ** -0.5, 0.1875, ((0, 32),)),
        "w_outgate": scatter_about(key_of[7], (D, DV), D ** -0.5, 0.1875, ((0, 32),)),
        "w_rank": scatter_about(key_of[8], (D, R), D ** -0.5, 0.1875, ((0, 32),)),
        "w_decay": scatter_about(key_of[9], (R, DK), R ** -0.5, 1.5),
        "decay_bias": jnp.clip(jax.random.uniform(key_of[10], (DK,), jnp.float32, 0.5, 5.0), 0.5, 5.0).astype(jnp.bfloat16),
        "head_gain": jnp.clip(1.0 + 0.1 * jax.random.normal(key_of[11], (HV,), jnp.float32), 0.5, 1.5).astype(jnp.bfloat16),
        "w_output": scatter_about(key_of[12], (DV, D), (DV // 4) ** -0.5, 0.375, ((1, 32),)),
        "norm_gain_mlp": jnp.clip(1.0 + 0.1 * jax.random.normal(key_of[13], (D,), jnp.float32), 0.5, 1.5).astype(jnp.bfloat16),
        "w_gate": scatter_about(key_of[14], (D, FF), D ** -0.5, 0.1875, ((0, 8), (1, 4))),
        "w_up": scatter_about(key_of[15], (D, FF), D ** -0.5, 0.1875, ((0, 8), (1, 4))),
        "w_down": scatter_about(key_of[16], (FF, D), (FF // 4) ** -0.5, 0.21875, ((0, 4), (1, 8))),
    }


EPSILON = 1e-05
HIGHEST = lax.Precision.HIGHEST

@jax.custom_vjp
def low(v):
    return lax.optimization_barrier(v.astype(jnp.bfloat16)).astype(jnp.float32)

@jax.custom_vjp
def low_back(v):
    return v

def low_keep(v):
    return (low(v), None)

def low_pass(kept, grad):
    return (grad,)

def back_keep(v):
    return (v, None)

def back_low(kept, grad):
    return (low(grad),)
low.defvjp(low_keep, low_pass)
low_back.defvjp(back_keep, back_low)

def matmul(left, right):
    return jnp.dot(left, right, precision=HIGHEST)

def rms_scale(values):
    return lax.rsqrt(lax.optimization_barrier(jnp.mean(values * values, axis=-1, keepdims=True)) + EPSILON)

def head_scale(values):
    return lax.rsqrt(jnp.maximum(lax.optimization_barrier(jnp.mean(values * values, axis=-1, keepdims=True)), 1.0))

def doc_masks(lengths_row):
    starts = (jnp.cumsum(lengths_row) - lengths_row).astype(jnp.int32)
    places = jnp.arange(LEN, dtype=jnp.int32)
    doc_ids = lax.optimization_barrier(jnp.sum((places[:, None] >= starts[None, 1:]).astype(jnp.int32), axis=1)).astype(jnp.int32)
    blocks = doc_ids.reshape(NC, BLOCK)
    final_ids = blocks[:, -1]
    prior_ids = jnp.concatenate([jnp.full((1,), -1, jnp.int32), final_ids[:-1]])
    within = jnp.arange(BLOCK, dtype=jnp.int32)
    causal = within[:, None] >= within[None, :]
    intra_mask = ((blocks[:, :, None] == blocks[:, None, :]) & causal[None]).astype(jnp.float32)
    inter_mask = (blocks == prior_ids[:, None]).astype(jnp.float32)
    keep_last = (final_ids == prior_ids).astype(jnp.float32)
    reach_last = (blocks == final_ids[:, None]).astype(jnp.float32)
    return (intra_mask, inter_mask, keep_last, reach_last)

def mixer(inputs, masking, gain_mix, w_query, w_key, w_value, w_outgate, w_rank, w_decay, decay_bias, head_gain, w_output):
    intra_mask, inter_mask, keep_last, reach_last = masking
    normed_in = low(inputs * rms_scale(inputs) * gain_mix)
    queries = low_back(matmul(normed_in, w_query)) * HK ** (-0.5)
    keys_proj = low_back(matmul(normed_in, w_key))
    values = low(low_back(matmul(normed_in, w_value)))
    gate_pre = low_back(matmul(normed_in, w_outgate))
    rank_proj = low(low_back(matmul(normed_in, w_rank)))
    decay_log = jax.nn.log_sigmoid(low_back(matmul(rank_proj, w_decay) + decay_bias)) / 16.0
    key_shape = (NC, BLOCK, H, HK)
    val_shape = (NC, BLOCK, H, HV)
    cumulative = jnp.cumsum(decay_log.reshape(key_shape), axis=1)
    block_end = cumulative[:, -1:]
    query_gated = low(queries.reshape(key_shape) * jnp.exp(cumulative))
    key_gated = low(keys_proj.reshape(key_shape) * jnp.exp(-cumulative))
    key_carry = low(keys_proj.reshape(key_shape) * jnp.exp(block_end - cumulative))
    value_heads = values.reshape(val_shape)
    scores = low(low_back(jnp.einsum('ntha,nsha->nhts', query_gated, key_gated, precision=HIGHEST) * intra_mask[:, None]))
    update = jnp.einsum('nsha,nshb->nhab', key_carry, value_heads * reach_last[:, :, None, None], precision=HIGHEST)
    keep_factor = jnp.exp(block_end[:, 0]) * keep_last[:, None, None]

    def advance(carry_state, pieces):
        factor, added_term = pieces
        return (low_back(carry_state * factor[..., None] + added_term), carry_state)
    _, before = lax.scan(advance, jnp.zeros((H, HK, HV), jnp.float32), (keep_factor, update))
    local_part = jnp.einsum('nhts,nshb->nthb', scores, value_heads, precision=HIGHEST)
    carried = jnp.einsum('ntha,nhab->nthb', query_gated, low(before), precision=HIGHEST)
    mixer_out = low_back(local_part + carried * inter_mask[:, :, None, None])
    normed_out = mixer_out * head_scale(mixer_out) * head_gain
    mixed_in = low((normed_out * jax.nn.silu(gate_pre.reshape(val_shape))).reshape(LEN, DV))
    return low_back(matmul(mixed_in, w_output))

def group_block(inputs, masking, params):
    gain_mix, w_query, w_key, w_value, w_outgate, w_rank, w_decay, decay_bias, head_gain, w_output, gain_mlp, w_gate, w_up, w_down = params
    mixed_out = jax.vmap(mixer, in_axes=(0, 0) + (None,) * 10)(inputs, masking, gain_mix, w_query, w_key, w_value, w_outgate, w_rank, w_decay, decay_bias, head_gain, w_output)
    residual = (inputs + mixed_out).reshape(-1, D)
    normed_mid = low(residual * rms_scale(residual) * gain_mlp)
    gate_proj = low_back(matmul(normed_mid, w_gate))
    up_proj = low_back(matmul(normed_mid, w_up))
    hidden = low(jax.nn.silu(gate_proj) * up_proj)
    return (residual + low_back(matmul(hidden, w_down))).reshape(inputs.shape)

def reference(tokens, doc_lengths, cotangent, norm_gain_mix, w_query, w_key, w_value, w_outgate, w_rank, w_decay, decay_bias, head_gain, w_output, norm_gain_mlp, w_gate, w_up, w_down):
    params = tuple((item.astype(jnp.float32) for item in (norm_gain_mix, w_query, w_key, w_value, w_outgate, w_rank, w_decay, decay_bias, head_gain, w_output, norm_gain_mlp, w_gate, w_up, w_down)))
    group_seqs = 4
    group_count = SEQUENCES // group_seqs
    inputs_all = tokens.astype(jnp.float32).reshape(group_count, group_seqs, LEN, D)
    grads_all = cotangent.astype(jnp.float32).reshape(group_count, group_seqs, LEN, D)
    lengths_all = doc_lengths.reshape(group_count, group_seqs, NDOC)

    def one_group(totals, pieces):
        inputs, grad_rows, lengths = pieces
        masking = jax.vmap(doc_masks)(lengths)

        def forward(values_in, *weights):
            return group_block(values_in, masking, weights)
        result, pullback = jax.vjp(forward, inputs, *params)
        gradients = pullback(grad_rows)
        totals = tuple((earlier + fresh for earlier, fresh in zip(totals, gradients[1:])))
        return (totals, (result.astype(jnp.bfloat16), gradients[0]))
    totals, (results, input_grads) = lax.scan(one_group, tuple((jnp.zeros_like(item) for item in params)), (inputs_all, grads_all, lengths_all))
    return (results.reshape(TOKENS, D), input_grads.reshape(TOKENS, D), totals[0], totals[1], totals[2], totals[3], totals[4], totals[5], totals[6], totals[7], totals[8], totals[9], totals[10], totals[11], totals[12], totals[13])
```

```python
import jax
import jax.numpy as jnp
from jax import lax
from jax.sharding import PartitionSpec as P

H = 4
BLOCK = 64
LEN = 1024
HK = 128
HV = 256
NC = 16


EPSILON = 1e-05


def rms_scale(values):
    return lax.rsqrt(jnp.mean(values * values, axis=-1, keepdims=True) + EPSILON)


def head_scale(values):
    return lax.rsqrt(jnp.maximum(jnp.mean(values * values, axis=-1, keepdims=True), 1.0))


def rounded(values):
    return lax.optimization_barrier(values.astype(jnp.bfloat16)).astype(jnp.float32)


def product(left, right):
    return jnp.dot(left, right, preferred_element_type=jnp.float32)


def product_left(left, right):
    return lax.dot_general(
        left, right, (((0,), (0,)), ((), ())), preferred_element_type=jnp.float32
    )


def product_right(left, right):
    return lax.dot_general(
        left, right, (((1,), (1,)), ((), ())), preferred_element_type=jnp.float32
    )


def norm_back(grad_norm, values, scale, gain, active=1.0):
    scaled = grad_norm * gain
    inner = jnp.mean(scaled * values, axis=-1, keepdims=True) * active
    return (scale * scaled - values * scale**3 * inner, grad_norm * values * scale)


def doc_masks(lengths, length, block_len):
    starts = jnp.cumsum(lengths, axis=-1) - lengths
    places = jnp.arange(length, dtype=jnp.int32)
    doc_ids = jnp.sum((places[None, :, None] >= starts[:, None, 1:]).astype(jnp.int32), axis=-1)
    blocks = doc_ids.reshape(lengths.shape[0], length // block_len, block_len)
    final_ids = blocks[:, :, -1]
    prior_ids = jnp.concatenate(
        [jnp.full((blocks.shape[0], 1), -1, jnp.int32), final_ids[:, :-1]], axis=1
    )
    within = jnp.arange(block_len, dtype=jnp.int32)
    causal = within[:, None] >= within[None, :]
    intra_mask = ((blocks[..., :, None] == blocks[..., None, :]) & causal).astype(jnp.float32)
    inter_mask = (blocks == prior_ids[..., None]).astype(jnp.float32)
    keep_last = (final_ids == prior_ids).astype(jnp.float32)
    reach_last = (blocks == final_ids[..., None]).astype(jnp.float32)
    return (intra_mask, inter_mask, keep_last, reach_last)


def mixer_forward(inputs, masking, weights, small_params):
    gain_mix, w_query, w_key, w_value, w_outgate, w_rank, w_output = weights
    w_decay, decay_bias, head_gain = small_params
    intra_mask, inter_mask, keep_last, reach_last = masking
    seq_count = inputs.shape[0] // LEN
    key_shape = (seq_count, NC, BLOCK, H, HK)
    val_shape = (seq_count, NC, BLOCK, H, HV)
    scale_in = rms_scale(inputs)
    normed_in = (inputs * scale_in * gain_mix.astype(jnp.float32)).astype(jnp.bfloat16)
    queries = product(normed_in, w_query).reshape(key_shape) * HK ** (-0.5)
    keys_proj = product(normed_in, w_key).reshape(key_shape)
    values = product(normed_in, w_value).astype(jnp.bfloat16).reshape(val_shape)
    gate_pre = product(normed_in, w_outgate).reshape(val_shape)
    rank_proj = product(normed_in, w_rank).astype(jnp.bfloat16)
    decay_pre = product(rank_proj, w_decay) + decay_bias.astype(jnp.float32)
    cumulative = jnp.cumsum((jax.nn.log_sigmoid(decay_pre) / 16.0).reshape(key_shape), axis=2)
    block_end = cumulative[:, :, -1:]
    grow_exp = jnp.exp(cumulative)
    shrink_exp = jnp.exp(-cumulative)
    carry_exp = jnp.exp(block_end - cumulative)
    query_scaled = queries * grow_exp
    key_scaled = keys_proj * shrink_exp
    key_decayed = keys_proj * carry_exp
    query_gated = query_scaled.astype(jnp.bfloat16)
    key_gated = key_scaled.astype(jnp.bfloat16)
    key_carry = key_decayed.astype(jnp.bfloat16)
    scores = (
        jnp.einsum("pntha,pnsha->pnhts", query_gated, key_gated, preferred_element_type=jnp.float32)
        * intra_mask[:, :, None]
    ).astype(jnp.bfloat16)
    value_kept = values * reach_last[..., None, None].astype(jnp.bfloat16)
    update = jnp.einsum(
        "pnsha,pnshb->pnhab", key_carry, value_kept, preferred_element_type=jnp.float32
    )
    keep_factor = jnp.exp(block_end[:, :, 0]) * keep_last[:, :, None, None]

    def advance(carry_state, pieces):
        factor, added_term = pieces
        return (carry_state * factor[..., None] + added_term, carry_state)

    _, before = lax.scan(
        advance,
        jnp.zeros((seq_count, H, HK, HV), jnp.float32),
        (jnp.moveaxis(keep_factor, 1, 0), jnp.moveaxis(update, 1, 0)),
    )
    before = jnp.moveaxis(before, 0, 1)
    before_low = before.astype(jnp.bfloat16)
    mixer_out = jnp.einsum("pnhts,pnshb->pnthb", scores, values, preferred_element_type=jnp.float32)
    mixer_out = (
        mixer_out
        + jnp.einsum(
            "pntha,pnhab->pnthb", query_gated, before_low, preferred_element_type=jnp.float32
        )
        * inter_mask[..., None, None]
    )
    scale_out = head_scale(mixer_out)
    normed_out = mixer_out * scale_out * head_gain.astype(jnp.float32)
    gate_act = jax.nn.silu(gate_pre)
    mixed_in = (normed_out * gate_act).reshape(inputs.shape[0], -1).astype(jnp.bfloat16)
    mixed_out = product(mixed_in, w_output)
    stored = dict(
        scale_in=scale_in,
        normed_in=normed_in,
        values=values,
        gate_pre=gate_pre,
        rank_proj=rank_proj,
        decay_pre=decay_pre,
        grow_exp=grow_exp,
        shrink_exp=shrink_exp,
        carry_exp=carry_exp,
        query_scaled=query_scaled,
        key_scaled=key_scaled,
        key_decayed=key_decayed,
        query_gated=query_gated,
        key_gated=key_gated,
        key_carry=key_carry,
        scores=scores,
        value_kept=value_kept,
        keep_factor=keep_factor,
        before=before,
        before_low=before_low,
        mixer_out=mixer_out,
        scale_out=scale_out,
        normed_out=normed_out,
        gate_act=gate_act,
        mixed_in=mixed_in,
    )
    return (mixed_out, stored)


def mixer_backward(grad_mixed, inputs, masking, weights, small_params, stored):
    gain_mix, w_query, w_key, w_value, w_outgate, w_rank, w_output = weights
    w_decay, decay_bias, head_gain = small_params
    intra_mask, inter_mask, keep_last, reach_last = masking
    row_count = inputs.shape[0]
    seq_count = row_count // LEN
    val_shape = (seq_count, NC, BLOCK, H, HV)
    grad_w_output = product_left(grad_mixed, stored["mixed_in"])
    grad_input = product_right(grad_mixed, w_output).reshape(val_shape)
    gate_pre = stored["gate_pre"]
    gate_sig = jax.nn.sigmoid(gate_pre)
    grad_gate = grad_input * stored["normed_out"] * gate_sig * (1.0 + gate_pre * (1.0 - gate_sig))
    grad_gate = grad_gate.reshape(row_count, -1).astype(jnp.bfloat16)
    unfloored = (stored["scale_out"] < 1.0).astype(jnp.float32)
    grad_out, head_terms = norm_back(
        grad_input * stored["gate_act"],
        stored["mixer_out"],
        stored["scale_out"],
        head_gain.astype(jnp.float32),
        unfloored,
    )
    grad_head_gain = jnp.sum(head_terms.reshape(-1, HV), axis=0)
    grad_out = grad_out.astype(jnp.bfloat16)
    grad_seen = grad_out * inter_mask[..., None, None].astype(jnp.bfloat16)
    values = stored["values"]
    query_gated = stored["query_gated"]
    key_carry = stored["key_carry"]
    grad_scores = (
        jnp.einsum("pnthb,pnshb->pnhts", grad_out, values, preferred_element_type=jnp.float32)
        * intra_mask[:, :, None]
    ).astype(jnp.bfloat16)
    grad_values = jnp.einsum(
        "pnhts,pnthb->pnshb", stored["scores"], grad_out, preferred_element_type=jnp.float32
    )
    grad_qgated = jnp.einsum(
        "pnhts,pnsha->pntha", grad_scores, stored["key_gated"], preferred_element_type=jnp.float32
    )
    grad_qgated = grad_qgated + jnp.einsum(
        "pnthb,pnhab->pntha", grad_seen, stored["before_low"], preferred_element_type=jnp.float32
    )
    grad_kgated = jnp.einsum(
        "pnhts,pntha->pnsha", grad_scores, query_gated, preferred_element_type=jnp.float32
    )
    grad_local = jnp.einsum(
        "pntha,pnthb->pnhab", query_gated, grad_seen, preferred_element_type=jnp.float32
    )

    def retreat(carry_grad, pieces):
        local_term, factor = pieces
        return (rounded(local_term + factor[..., None] * carry_grad), carry_grad)

    _, grad_after = lax.scan(
        retreat,
        jnp.zeros((seq_count, H, HK, HV), jnp.float32),
        (jnp.moveaxis(grad_local, 1, 0), jnp.moveaxis(stored["keep_factor"], 1, 0)),
        reverse=True,
    )
    grad_after = jnp.moveaxis(grad_after, 0, 1)
    after_low = grad_after.astype(jnp.bfloat16)
    grad_kcarry = jnp.einsum(
        "pnshb,pnhab->pnsha", stored["value_kept"], after_low, preferred_element_type=jnp.float32
    )
    grad_values = (
        grad_values
        + jnp.einsum("pnsha,pnhab->pnshb", key_carry, after_low, preferred_element_type=jnp.float32)
        * reach_last[..., None, None]
    )
    grad_end_state = jnp.sum(grad_after * stored["before"], axis=-1) * stored["keep_factor"]
    grad_cum = (
        grad_qgated * stored["query_scaled"]
        - grad_kgated * stored["key_scaled"]
        - grad_kcarry * stored["key_decayed"]
    )
    grad_end = (
        jnp.sum(grad_kcarry * stored["key_decayed"], axis=2, keepdims=True)
        + grad_end_state[:, :, None]
    )
    grad_decay = jnp.flip(jnp.cumsum(jnp.flip(grad_cum, 2), axis=2), 2) + grad_end
    grad_queries = (
        (grad_qgated * stored["grow_exp"] * HK ** (-0.5))
        .reshape(row_count, -1)
        .astype(jnp.bfloat16)
    )
    grad_keys = grad_kgated * stored["shrink_exp"] + grad_kcarry * stored["carry_exp"]
    grad_keys = grad_keys.reshape(row_count, -1).astype(jnp.bfloat16)
    grad_vals = grad_values.reshape(row_count, -1).astype(jnp.bfloat16)
    grad_pre = (
        grad_decay.reshape(row_count, -1) / 16.0 * jax.nn.sigmoid(-stored["decay_pre"])
    ).astype(jnp.bfloat16)
    grad_decay_bias = jnp.sum(grad_pre.astype(jnp.float32), axis=0)
    grad_w_decay = product_left(stored["rank_proj"], grad_pre)
    grad_rank = product_right(grad_pre, w_decay).astype(jnp.bfloat16)
    normed_in = stored["normed_in"]
    grad_normed = (
        product_right(grad_queries, w_query)
        + product_right(grad_keys, w_key)
        + product_right(grad_vals, w_value)
        + product_right(grad_gate, w_outgate)
        + product_right(grad_rank, w_rank)
    )
    grad_inputs, gain_terms = norm_back(
        grad_normed, inputs, stored["scale_in"], gain_mix.astype(jnp.float32)
    )
    big_grads = (
        jnp.sum(gain_terms, axis=0),
        product_left(normed_in, grad_queries),
        product_left(normed_in, grad_keys),
        product_left(normed_in, grad_vals),
        product_left(normed_in, grad_gate),
        product_left(normed_in, grad_rank),
        grad_w_output,
    )
    return (grad_inputs, big_grads, (grad_w_decay, grad_decay_bias, grad_head_gain))


def mlp_pass(rows_in, grad_rows, w_gate, w_up, w_down):
    gate_proj = product_right(rows_in, w_gate)
    up_proj = product_right(rows_in, w_up)
    gate_sig = jax.nn.sigmoid(gate_proj)
    hidden = (gate_proj * gate_sig * up_proj).astype(jnp.bfloat16)
    branch = product(hidden, w_down)
    grad_hidden = product_right(grad_rows, w_down)
    grad_w_down = product_left(hidden, grad_rows)
    grad_up = (grad_hidden * gate_proj * gate_sig).astype(jnp.bfloat16)
    grad_gate = (grad_hidden * up_proj * gate_sig * (1.0 + gate_proj * (1.0 - gate_sig))).astype(
        jnp.bfloat16
    )
    grad_rows_in = product(grad_gate, w_gate) + product(grad_up, w_up)
    return (
        branch,
        grad_rows_in,
        (product_left(grad_gate, rows_in), product_left(grad_up, rows_in), grad_w_down),
    )


def bits_of(count):
    return count.bit_length() - 1


def halve(grads, dim, bit, count):
    place = (lax.axis_index("rows") >> bit) & 1
    send = lax.dynamic_index_in_dim(grads, 1 - place, dim, keepdims=False)
    keep = lax.dynamic_index_in_dim(grads, place, dim, keepdims=False)
    pairs = [(i, i ^ (1 << bit)) for i in range(count)]
    came = lax.ppermute(send.astype(jnp.bfloat16), "rows", pairs)
    return keep.astype(jnp.float32) + came.astype(jnp.float32)


def line_sum(grads, count):
    me = lax.axis_index("mlp")
    up = [(i, i + 1) for i in range(count - 1)]
    down = [(i + 1, i) for i in range(count - 1)]

    def pick(at):
        return lax.dynamic_index_in_dim(grads, jnp.clip(at, 0, count - 1), 0, keepdims=False).astype(
            jnp.float32
        )

    total = pick(me)
    rising = falling = None
    for step in range(1, count):
        send_up = pick(me + count - step)
        send_down = pick(me - count + step)
        if rising is not None:
            send_up = send_up + rising
            send_down = send_down + falling
        rising = lax.ppermute(send_up.astype(jnp.bfloat16), "mlp", up).astype(jnp.float32)
        falling = lax.ppermute(send_down.astype(jnp.bfloat16), "mlp", down).astype(jnp.float32)
    if rising is not None:
        total = total + rising + falling
    return total


def reduce_rows(grads, dims, order, count):
    dims = dict(dims)
    for bit in order:
        dim = dims.pop(bit)
        grads = halve(grads, dim, bit, count)
        dims = {b: (d - 1 if d > dim else d) for b, d in dims.items()}
    return grads


def body(
    tokens,
    doc_lengths,
    cotangent,
    norm_gain_mix,
    w_query,
    w_key,
    w_value,
    w_outgate,
    w_rank,
    w_decay,
    decay_bias,
    head_gain,
    w_output,
    norm_gain_mlp,
    w_gate,
    w_up,
    w_down,
):
    rows = lax.axis_size("rows")
    mlps = lax.axis_size("mlp")
    nbits = bits_of(rows)
    small_params = (w_decay, decay_bias, head_gain)
    shard = w_query.shape[0]
    pad = jnp.zeros((shard, 110), jnp.bfloat16)
    mixer_local = jnp.concatenate(
        [
            w_query, w_key, w_value, w_outgate, w_output.T,
            w_rank, norm_gain_mix[:, None], norm_gain_mlp[:, None], pad,
        ],
        axis=1,
    )
    mixer_all = lax.all_gather(mixer_local, ("rows", "mlp"), axis=0, tiled=True)
    gain_mix = mixer_all[:, 4112]
    gain_mlp = mixer_all[:, 4113].astype(jnp.float32)
    mixer_part = (
        gain_mix,
        mixer_all[:, :512],
        mixer_all[:, 512:1024],
        mixer_all[:, 1024:2048],
        mixer_all[:, 2048:3072],
        mixer_all[:, 4096:4112],
        mixer_all[:, 3072:4096].T,
    )
    mlp_local = jnp.stack([w_gate.T, w_up.T, w_down])
    mlp_all = lax.all_gather(mlp_local, ("rows", "mlp"), axis=0)
    hid, wide = mlp_local.shape[1:]
    mlp_all = mlp_all.reshape(rows, mlps, 3, hid, wide).transpose(2, 1, 3, 0, 4)
    mlp_all = mlp_all.reshape(3, mlps * hid, rows * wide)
    inputs = tokens.astype(jnp.float32)
    masking = doc_masks(doc_lengths, LEN, BLOCK)
    mixed_out, stored = mixer_forward(inputs, masking, mixer_part, small_params)
    residual = inputs + mixed_out
    scale_mid = rms_scale(residual)
    normed_mid = (residual * scale_mid * gain_mlp).astype(jnp.bfloat16)
    branch, grad_mid, mlp_grads = mlp_pass(normed_mid, cotangent, mlp_all[0], mlp_all[1], mlp_all[2])
    block_out = (residual + branch).astype(jnp.bfloat16)
    mlp_grads = jnp.stack(mlp_grads).reshape((3, mlps, hid) + (2,) * nbits + (wide,))
    dims = {nbits - 1 - i: 3 + i for i in range(nbits)}
    mlp_grads = reduce_rows(mlp_grads, dims, range(nbits), rows)
    mlp_grads = line_sum(mlp_grads.transpose(1, 0, 2, 3), mlps)
    grad_mid_in, mid_terms = norm_back(grad_mid, residual, scale_mid, gain_mlp)
    grad_res = cotangent.astype(jnp.float32) + grad_mid_in
    grad_inputs, big_grads, small_grads = mixer_backward(
        grad_res.astype(jnp.bfloat16), inputs, masking, mixer_part, small_params, stored
    )
    grad_tokens = grad_res + grad_inputs
    big_grads = jnp.concatenate(
        [
            big_grads[1], big_grads[2], big_grads[3], big_grads[4], big_grads[6],
            big_grads[5], big_grads[0][:, None], jnp.sum(mid_terms, axis=0)[:, None],
            jnp.zeros((rows * mlps * shard, 110), jnp.float32),
        ],
        axis=1,
    )
    big_grads = big_grads.reshape((2,) * nbits + (mlps, shard, 4224))
    dims = {nbits - 1 - i: i for i in range(nbits)}
    big_grads = line_sum(reduce_rows(big_grads, dims, range(nbits), rows), mlps)
    small_acc = lax.psum(small_grads, ("rows", "mlp"))
    return (
        block_out,
        grad_tokens,
        big_grads[:, 4112],
        big_grads[:, :512],
        big_grads[:, 512:1024],
        big_grads[:, 1024:2048],
        big_grads[:, 2048:3072],
        big_grads[:, 4096:4112],
        small_acc[0],
        small_acc[1],
        small_acc[2],
        big_grads[:, 3072:4096].T,
        big_grads[:, 4113],
        mlp_grads[0].T,
        mlp_grads[1].T,
        mlp_grads[2],
    )


def solution(mesh):
    in_specs = (
        P(("rows", "mlp"), None),
        P(("rows", "mlp"), None),
        P(("rows", "mlp"), None),
        P(("rows", "mlp")),
        P(("rows", "mlp"), None),
        P(("rows", "mlp"), None),
        P(("rows", "mlp"), None),
        P(("rows", "mlp"), None),
        P(("rows", "mlp"), None),
        P(),
        P(),
        P(),
        P(None, ("rows", "mlp")),
        P(("rows", "mlp")),
        P("rows", "mlp"),
        P("rows", "mlp"),
        P("mlp", "rows"),
    )
    out_specs = (
        P(("rows", "mlp"), None),
        P(("rows", "mlp"), None),
        P(("rows", "mlp")),
        P(("rows", "mlp"), None),
        P(("rows", "mlp"), None),
        P(("rows", "mlp"), None),
        P(("rows", "mlp"), None),
        P(("rows", "mlp"), None),
        P(),
        P(),
        P(),
        P(None, ("rows", "mlp")),
        P(("rows", "mlp")),
        P("rows", "mlp"),
        P("rows", "mlp"),
        P("mlp", "rows"),
    )
    return jax.shard_map(body, mesh=mesh, in_specs=in_specs, out_specs=out_specs, check_vma=False)
```

```python
import functools

import jax
import jax.numpy as jnp
from jax import lax
from jax.experimental import pallas as pl
from jax.experimental.pallas import tpu as pltpu
from jax.sharding import PartitionSpec as P

F32 = jnp.float32
BF = jnp.bfloat16
EPS = 1e-5
LEN = 1024
BL = 64
H = 4
HK = 128
HV = 256
DK = 512
DV = 1024
CQ, CK, CV, CG, CR, CO = 0, 512, 1024, 2048, 3072, 3200
GW = 3200
SCALE = HK**-0.5
VMEM = 60 * 1024 * 1024


def nn(a,b): return lax.dot_general(a,b,(((1,),(0,)),((),())),preferred_element_type=F32)


def nt(a,b): return lax.dot_general(a,b,(((1,),(1,)),((),())),preferred_element_type=F32)


def tn(a,b): return lax.dot_general(a,b,(((0,),(0,)),((),())),preferred_element_type=F32)


def sigmoid(v): return 1.0/(1.0+jnp.exp(-v))


def softminus(x): return jnp.minimum(x,0.0)-jnp.log1p(jnp.exp(-jnp.abs(x)))


def split(x):
    hi=x.astype(BF); return hi,(x-hi.astype(F32)).astype(BF)


def doc_of(p,starts):
    out=(p>=starts[0]).astype(jnp.int32)
    for s in starts[1:]: out=out+(p>=s).astype(jnp.int32)
    return out


def tile_masks(base,T,starts):
    tc=lax.broadcasted_iota(jnp.int32,(T,1),0); tr=lax.broadcasted_iota(jnp.int32,(1,T),1)
    dc=doc_of(tc+base,starts); dr=doc_of(tr+base,starts)
    first=(tc & ~(BL-1))+base
    prior=jnp.where(first>0,doc_of(first-1,starts),-1)
    last=doc_of(first+(BL-1),starts)
    inter=(dc==prior); reach=(dc==last)
    same=(tc>>6)==(tr>>6)
    low=same&(tc>=tr)
    return inter,reach,same,low,low&(dc==dr)


def keep_of(first,starts):
    return jnp.where(first>0,(doc_of(first-1,starts)==doc_of(first+BL-1,starts)).astype(F32),0.0)


def starts_of(len_ref, seq):
    first = len_ref[seq * 4]
    second = first + len_ref[seq * 4 + 1]
    return [first, second, second + len_ref[seq * 4 + 2]]


def params(flops=0, moved=0):
    return dict(
        compiler_params=pltpu.CompilerParams(vmem_limit_bytes=VMEM),
        cost_estimate=pl.CostEstimate(flops=flops, bytes_accessed=moved, transcendentals=0),
    )


def fwd_kernel(NT,st_ref,tok_ref,w_ref,gain_ref,wdec_ref,bias_ref,hg_ref,res_ref,n_ref,q_ref,k_ref,cum_ref,dp_ref,v_ref,gp_ref,o_ref,bef_ref,mix_ref,rank_ref,state):
    T=tok_ref.shape[0]; nb=T//BL
    i=pl.program_id(0); seq=i//NT; tile=i%NT; base=tile*T
    starts=starts_of(st_ref,seq)
    inter,reach,same,low,intra=tile_masks(base,T,starts)
    @pl.when(tile==0)
    def _(): state[...]=jnp.zeros_like(state)
    x=tok_ref[...].astype(F32)
    r=lax.rsqrt(jnp.mean(x*x,axis=-1,keepdims=True)+EPS)
    n_ref[...]=(x*r*gain_ref[...]).astype(BF)
    n=n_ref[...]
    rank=nn(n,w_ref[:,CR:CR+128]).astype(BF)
    rank_ref[...]=rank
    dp=nn(rank,wdec_ref[...])+bias_ref[...]
    dp_ref[...]=dp
    dhi,dlo=split(softminus(dp)*(1.0/16.0))
    lowb=low.astype(BF)
    cum=nn(lowb,dhi)+nn(lowb,dlo)
    cum_ref[...]=cum
    q=nn(n,w_ref[:,CQ:CQ+DK])*SCALE; q_ref[...]=q
    k=nn(n,w_ref[:,CK:CK+DK]); k_ref[...]=k
    v_ref[...]=nn(n,w_ref[:,CV:CV+DV]).astype(BF)
    gp_ref[...]=nn(n,w_ref[:,CG:CG+DV]).astype(BF)
    interf=inter.astype(F32)
    ends=[cum[BL*b+BL-1:BL*b+BL,:] for b in range(nb)]
    endb=jnp.concatenate([jnp.broadcast_to(e,(BL,DK)) for e in ends],axis=0)
    qg=q*jnp.exp(cum)
    qgi=(qg*interf).astype(BF); qg=qg.astype(BF)
    kg=(k*jnp.exp(-cum)).astype(BF)
    kc=(k*jnp.exp(endb-cum)).astype(BF)
    keeps=jnp.concatenate([jnp.exp(ends[b])*keep_of(base+BL*b,starts) for b in range(nb)]+[jnp.zeros((8-nb,DK),F32)],axis=0)
    for h in range(H):
        a=slice(HK*h,HK*h+HK); c=slice(HV*h,HV*h+HV)
        v=v_ref[:,c]
        s=jnp.where(intra,nt(qg[:,a],kg[:,a]),0.0).astype(BF)
        vk=jnp.where(reach,v,jnp.zeros_like(v))
        kt=keeps[:,a].T
        o=nn(s,v)
        parts=[]
        st=state[h]
        for b in range(nb):
            t=slice(BL*b,BL*b+BL)
            sb=st.astype(BF)
            bef_ref[b,h]=sb
            parts.append(nn(qgi[t,a],sb))
            st=st*kt[:,b:b+1]+tn(kc[t,a],vk[t])
        state[h]=st
        o=o+jnp.concatenate(parts,axis=0)
        o_ref[:,c]=o
        sc=lax.rsqrt(jnp.maximum(jnp.mean(o*o,axis=-1,keepdims=True),1.0))
        gp=gp_ref[:,c].astype(F32)
        mix_ref[:,c]=(o*sc*hg_ref[...]*(gp*sigmoid(gp))).astype(BF)
    res_ref[...]=x+nt(mix_ref[...],w_ref[:,CO:CO+DV])


def fwd_call(st,tok,w,gain,wdec,bias,hg,T=256):
    n,d=tok.shape; NT=LEN//T; sd=jax.ShapeDtypeStruct
    row=lambda x: pl.BlockSpec((T,x),lambda i,s:(i,0))
    const=lambda a: pl.BlockSpec(a.shape,lambda i,s:(0,0),pipeline_mode=pl.Buffered(1))
    nb=T//BL
    outs=[(d,F32),(d,BF),(DK,F32),(DK,F32),(DK,F32),(DK,F32),(DV,BF),(DV,BF),(DV,F32),None,(DV,BF),(128,BF)]
    specs=[row(o[0]) if o else pl.BlockSpec((nb,H,HK,HV),lambda i,s:(i,0,0,0)) for o in outs]
    shapes=[sd((n,o[0]),o[1]) if o else sd((n//BL,H,HK,HV),BF) for o in outs]
    return pl.pallas_call(functools.partial(fwd_kernel,NT),
        grid_spec=pltpu.PrefetchScalarGridSpec(num_scalar_prefetch=1,grid=(n//T,),
            in_specs=[row(d),const(w),const(gain),const(wdec),const(bias),const(hg)],out_specs=specs,
            scratch_shapes=[pltpu.VMEM((H,HK,HV),F32)]),
        out_shape=shapes,name="mixer_fwd",**params(n*d*4224*2,60<<20))(st,tok,w,gain,wdec,bias,hg)


def bwd_kernel(NT,st_ref,gmix_ref,w_ref,wdec_ref,hg_ref,q_ref,k_ref,cum_ref,dp_ref,v_ref,gp_ref,o_ref,bef_ref,rank_ref,g_ref,dwd_ref,db_ref,dhg_ref,state):
    T=q_ref.shape[0]; nb=T//BL
    step=pl.program_id(0); i=pl.num_programs(0)-1-step; seq=i//NT; tile=i%NT; base=tile*T
    starts=starts_of(st_ref,seq)
    inter,reach,same,low,intra=tile_masks(base,T,starts)
    @pl.when(tile==NT-1)
    def _(): state[...]=jnp.zeros_like(state)
    @pl.when(step==0)
    def _():
        dwd_ref[...]=jnp.zeros_like(dwd_ref); db_ref[...]=jnp.zeros_like(db_ref); dhg_ref[...]=jnp.zeros_like(dhg_ref)
    cum=cum_ref[...]
    ends=[cum[BL*b+BL-1:BL*b+BL,:] for b in range(nb)]
    endb=jnp.concatenate([jnp.broadcast_to(e,(BL,DK)) for e in ends],axis=0)
    eg=jnp.exp(cum); es=jnp.exp(-cum); ec=jnp.exp(endb-cum)
    kend=jnp.concatenate([jnp.exp(ends[b])*keep_of(base+BL*b,starts) for b in range(nb)]+[jnp.zeros((8-nb,DK),F32)],axis=0)
    interb=inter.astype(F32).astype(BF); reachf=reach.astype(F32)
    tc=lax.broadcasted_iota(jnp.int32,(T,1),0); tr=lax.broadcasted_iota(jnp.int32,(1,T),1)
    upb=(same&(tc<=tr)).astype(BF); lsb=(same&(tc>tr)).astype(BF)
    hg=hg_ref[...]
    ones=jnp.ones((8,HV),BF)
    for h in range(H):
        a=slice(HK*h,HK*h+HK); c=slice(HV*h,HV*h+HV)
        gi=nn(gmix_ref[...],w_ref[:,CO+HV*h:CO+HV*h+HV])
        o=o_ref[:,c]; gp=gp_ref[:,c].astype(F32)
        ms=jnp.mean(o*o,axis=-1,keepdims=True)
        sc=lax.rsqrt(jnp.maximum(ms,1.0))
        hn0=o*sc
        s=sigmoid(gp); si=gp*s
        g_ref[:,CG+HV*h:CG+HV*h+HV]=(gi*hn0*hg*(s+si*(1.0-s))).astype(BF)
        G=gi*si
        dhg_ref[...]+=jnp.sum((G*hn0).reshape(-1,8,HV),axis=0)
        G=G*hg
        innr=jnp.mean(G*o,axis=-1,keepdims=True)*jnp.where(ms>1.0,1.0,0.0)
        go=(sc*G-o*(sc*sc*sc*innr)).astype(BF)
        goi=go*interb
        v=v_ref[:,c]
        qs=q_ref[:,a]*eg[:,a]; ks=k_ref[:,a]*es[:,a]; kd=k_ref[:,a]*ec[:,a]
        qg=qs.astype(BF); kg=ks.astype(BF); kc=kd.astype(BF)
        sco=jnp.where(intra,nt(qg,kg),0.0).astype(BF)
        gs=jnp.where(intra,nt(go,v),0.0).astype(BF)
        gv=tn(sco,go); gq=nn(gs,kg); gk=tn(gs,qg)
        kt=kend[:,a].T
        st=state[h]
        p_gv=[None]*nb; p_gq=[None]*nb; p_gkc=[None]*nb; p_end=[None]*nb
        for b in reversed(range(nb)):
            t=slice(BL*b,BL*b+BL)
            bef=bef_ref[b,h]
            sb=st.astype(BF)
            p_gv[b]=nn(kc[t],sb)
            p_gq[b]=nt(goi[t],bef)
            p_gkc[b]=nt(v[t],sb)
            m1,m2=split(st*bef.astype(F32))
            p_end[b]=(nt(ones,m1)+nt(ones,m2))[0:1]*kend[b:b+1,a]
            st=(tn(qg[t],goi[t])+kt[:,b:b+1]*st).astype(BF).astype(F32)
        state[h]=st
        cat=lambda p: jnp.concatenate(p,axis=0)
        gv=gv+cat(p_gv)*reachf
        g_ref[:,CV+HV*h:CV+HV*h+HV]=gv.astype(BF)
        gq=gq+cat(p_gq)
        gkc=cat(p_gkc)*reachf
        av1,av2=split(gq*qs-gk*ks)
        c1,c2=split(gkc*kd)
        endr=cat([jnp.broadcast_to(p,(BL,HK)) for p in p_end])
        gd=nn(upb,av1)+nn(upb,av2)+nn(lsb,c1)+nn(lsb,c2)+endr
        g_ref[:,CQ+HK*h:CQ+HK*h+HK]=(gq*eg[:,a]*SCALE).astype(BF)
        g_ref[:,CK+HK*h:CK+HK*h+HK]=(gk*es[:,a]+gkc*ec[:,a]).astype(BF)
        dp=dp_ref[:,a]
        gpre=(gd*(1.0/16.0)*(1.0/(1.0+jnp.exp(dp)))).astype(BF)
        db_ref[:,a]+=jnp.sum(gpre.astype(F32).reshape(-1,8,HK),axis=0)
        dwd_ref[:,a]+=tn(rank_ref[...],gpre)
        gr=nt(gpre,wdec_ref[:,a])
        grank=gr if h==0 else grank+gr
    g_ref[:,CR:CR+128]=grank.astype(BF)


def bwd_call(st,gmix,w,wdec,hg,q,k,cum,dp,v,gp,o,bef,rank,T=256):
    n,d=gmix.shape; NT=LEN//T; sd=jax.ShapeDtypeStruct; N1=n//T-1
    row=lambda a: pl.BlockSpec((T,a.shape[1]),lambda i,s:(N1-i,0))
    const=lambda a: pl.BlockSpec(a.shape,lambda i,s:(0,0),pipeline_mode=pl.Buffered(1))
    nb=T//BL
    acc=lambda s: pl.BlockSpec(s,lambda i,_:(0,0))
    return pl.pallas_call(functools.partial(bwd_kernel,NT),
        grid_spec=pltpu.PrefetchScalarGridSpec(num_scalar_prefetch=1,grid=(n//T,),
            in_specs=[row(gmix),const(w),const(wdec),const(hg),row(q),row(k),row(cum),row(dp),row(v),row(gp),row(o),pl.BlockSpec((nb,H,HK,HV),lambda i,s:(N1-i,0,0,0)),row(rank)],
            out_specs=[pl.BlockSpec((T,3200),lambda i,s:(N1-i,0)),acc((128,DK)),acc((8,DK)),acc((8,HV))],
            scratch_shapes=[pltpu.VMEM((H,HK,HV),F32)]),
        out_shape=[sd((n,3200),BF),sd((128,DK),F32),sd((8,DK),F32),sd((8,HV),F32)],
        name="mixer_bwd",**params(n*d*4224*3,70<<20))(st,gmix,w,wdec,hg,q,k,cum,dp,v,gp,o,bef,rank)


def dx_kernel(g_ref,w_ref,tok_ref,gain_ref,gres_ref,gt_ref,gn_ref):
    gm=nt(g_ref[...],w_ref[:,:3200])
    x=tok_ref[...].astype(F32)
    r=lax.rsqrt(jnp.mean(x*x,axis=-1,keepdims=True)+EPS)
    sc=gm*gain_ref[...]
    inner=jnp.mean(sc*x,axis=-1,keepdims=True)
    gt_ref[...]=gres_ref[...]+r*sc-x*(r*r*r*inner)
    part=jnp.sum((gm*x*r).reshape(-1,8,gm.shape[1]),axis=0)
    @pl.when(pl.program_id(0)==0)
    def _(): gn_ref[...]=part
    @pl.when(pl.program_id(0)>0)
    def _(): gn_ref[...]+=part


def dx_call(g,w,tok,gain,gres,T=256):
    n,d=tok.shape; sd=jax.ShapeDtypeStruct
    row=lambda a: pl.BlockSpec((T,a.shape[1]),lambda i:(i,0))
    const=lambda a: pl.BlockSpec(a.shape,lambda i:(0,0),pipeline_mode=pl.Buffered(1))
    return pl.pallas_call(dx_kernel,grid=(n//T,),in_specs=[row(g),const(w),row(tok),const(gain),row(gres)],
        out_specs=[row(gres),pl.BlockSpec((8,d),lambda i:(0,0))],out_shape=[sd((n,d),F32),sd((8,d),F32)],
        name="mixer_dx",**params(n*d*3200*2,40<<20))(g,w,tok,gain,gres)


def mlp_kernel(chunk, res_ref, cot_ref, gain_ref, w_hbm, bo_ref, n_ref, hid_ref, gg_ref, gu_ref, gres_ref, gmix_ref, gn_ref, w_ref, sems):
    wg_ref,wu_ref,wd_ref=w_ref.at[0],w_ref.at[1],w_ref.at[2]
    blocks,mlps,_,hid,_=w_hbm.shape
    @pl.when(pl.program_id(0)==0)
    def _():
        copies=[pltpu.make_async_copy(w_hbm.at[r,m],w_ref.at[:,pl.ds(m*hid,hid),pl.ds(r*128,128)],sems.at[r,m]) for m in range(mlps) for r in range(blocks)]
        for c in copies: c.start()
        for c in copies: c.wait()
    res=res_ref[...]
    gain=gain_ref[...]
    r=lax.rsqrt(jnp.mean(res*res,axis=-1,keepdims=True)+EPS)
    n_ref[...]=(res*r*gain).astype(BF)
    ff=wg_ref.shape[0]
    for c in range(ff//chunk):
        sl=slice(c*chunk,(c+1)*chunk)
        n=n_ref[...]
        gp=nt(n,wg_ref[sl,:]); up=nt(n,wu_ref[sl,:]); gh=nt(cot_ref[...],wd_ref[sl,:])
        s=sigmoid(gp)
        si=gp*s
        hid_ref[:,sl]=(si*up).astype(BF)
        gu_ref[:,sl]=(gh*si).astype(BF)
        gg_ref[:,sl]=(gh*up*(s+si*(1.0-s))).astype(BF)
    gm=nn(gg_ref[...],wg_ref[...])+nn(gu_ref[...],wu_ref[...])
    res=res_ref[...]
    sc=gm*gain
    inner=jnp.mean(sc*res,axis=-1,keepdims=True)
    gi=r*sc-res*(r*r*r*inner)
    gres=cot_ref[...].astype(F32)+gi
    gres_ref[...]=gres
    gmix_ref[...]=gres.astype(BF)
    part=jnp.sum((gm*res*r).reshape(-1,8,gm.shape[1]),axis=0)
    @pl.when(pl.program_id(0)==0)
    def _(): gn_ref[...]=part
    @pl.when(pl.program_id(0)>0)
    def _(): gn_ref[...]+=part
    bo_ref[...]=(res+nn(hid_ref[...],wd_ref[...])).astype(BF)


def mlp_call(res,cot,gain,w,T=256,chunk=256):
    n,d=res.shape; ff=w.shape[1]*w.shape[3]
    row=lambda w: pl.BlockSpec((T,w),lambda i:(i,0))
    const=lambda a: pl.BlockSpec(a.shape,lambda i:(0,0),pipeline_mode=pl.Buffered(1))
    sd=jax.ShapeDtypeStruct
    return pl.pallas_call(functools.partial(mlp_kernel,chunk),grid=(n//T,),
        in_specs=[row(d),row(d),const(gain),pl.BlockSpec(memory_space=pl.ANY)],
        out_specs=[row(d),row(d),row(ff),row(ff),row(ff),row(d),row(d),pl.BlockSpec((8,d),lambda i:(0,0))],
        out_shape=[sd((n,d),BF),sd((n,d),BF),sd((n,ff),BF),sd((n,ff),BF),sd((n,ff),BF),sd((n,d),F32),sd((n,d),BF),sd((8,d),F32)],
        scratch_shapes=[pltpu.VMEM((3,ff,d),BF),pltpu.SemaphoreType.DMA((w.shape[0],w.shape[1]))],
        name="mlp",**params(n*d*ff*12,90<<20))(res,cot,gain,w)


def load_half(sel_ref,x_hbm,xh,sems):
    copies=[pltpu.make_async_copy(x_hbm.at[:,pl.ds(pl.multiple_of((2*j+sel_ref[0])*128,128),128)],xh.at[:,pl.ds(128*j,128)],sems.at[j]) for j in range(4)]
    for c in copies: c.start()
    for c in copies: c.wait()


def dw_kernel(wide,sel_ref,g_ref,x_hbm,*rest):
    *recv,o_ref,xh,sems=rest
    @pl.when(pl.program_id(0)==0)
    def _(): load_half(sel_ref,x_hbm,xh,sems)
    o=tn(g_ref[...],xh[...]) if wide else tn(xh[...],g_ref[...])
    for j in range(4):
        v=o[:,128*j:128*(j+1)] if wide else o[128*j:128*(j+1),:]
        if recv: v=v+recv[0][j].astype(F32)
        o_ref[j]=v.astype(BF)


def dw_call(g,x,sel,recv=None,chunk=1408,wide=True):
    n,ff=g.shape; d=x.shape[1]
    out=pl.BlockSpec((4,chunk,128),lambda i,s:(0,i,0)) if wide else pl.BlockSpec((4,128,chunk),lambda i,s:(0,0,i))
    more=[] if recv is None else [recv]
    return pl.pallas_call(functools.partial(dw_kernel,wide),
        grid_spec=pltpu.PrefetchScalarGridSpec(num_scalar_prefetch=1,grid=(ff//chunk,),
            in_specs=[pl.BlockSpec((n,chunk),lambda i,s:(0,i)),pl.BlockSpec(memory_space=pl.ANY)]+[out]*len(more),
            out_specs=out,scratch_shapes=[pltpu.VMEM((n,d//2),BF),pltpu.SemaphoreType.DMA((4,))]),
        out_shape=jax.ShapeDtypeStruct((4,ff,128) if wide else (4,128,ff),BF),
        name="grad_w",**params(n*d*ff,n*ff*2+n*d+ff*d*2))(sel,g,x,*more)


def swap(x, axis, bit, count):
    return lax.ppermute(x, axis, [(i, i ^ (1 << bit)) for i in range(count)])


def bit_of(axis, bit):
    return (lax.axis_index(axis) >> bit) & 1


def halve(grads, dim, bit, count):
    place = bit_of("rows", bit)
    send = lax.dynamic_index_in_dim(grads, 1 - place, dim, keepdims=False)
    keep = lax.dynamic_index_in_dim(grads, place, dim, keepdims=False)
    came = swap(send.astype(BF), "rows", bit, count)
    return keep.astype(F32) + came.astype(F32)


def halve_both(grads, first, low, count):
    grads = grads.reshape((2, 2) + grads.shape[1:])
    if first == 0:
        return halve(halve(grads, 0, low + 2, count), 0, low + 1, count)
    return halve(halve(grads, 1, low + 1, count), 0, low + 2, count)


def line_sum(grads, count):
    me = lax.axis_index("mlp")
    up = [(i, i + 1) for i in range(count - 1)]
    down = [(i + 1, i) for i in range(count - 1)]

    def pick(at):
        return lax.dynamic_index_in_dim(grads, jnp.clip(at, 0, count - 1), 0, keepdims=False)

    total = pick(me)
    rising = falling = None
    for step in range(1, count):
        send_up = pick(me + count - step)
        send_down = pick(me - count + step)
        if rising is not None:
            send_up = send_up + rising
            send_down = send_down + falling
        rising = lax.ppermute(send_up.astype(BF), "mlp", up).astype(F32)
        falling = lax.ppermute(send_down.astype(BF), "mlp", down).astype(F32)
    if rising is not None:
        total = total + rising + falling
    return total


def sum_all(x, rows, mlps):
    for axis, count in (("rows", rows), ("mlp", mlps)):
        for bit in range(count.bit_length() - 1):
            x = x + swap(x, axis, bit, count)
    return x


def body(
    tokens,
    doc_lengths,
    cotangent,
    norm_gain_mix,
    w_query,
    w_key,
    w_value,
    w_outgate,
    w_rank,
    w_decay,
    decay_bias,
    head_gain,
    w_output,
    norm_gain_mlp,
    w_gate,
    w_up,
    w_down,
):
    rows = lax.axis_size("rows")
    mlps = lax.axis_size("mlp")
    low = rows.bit_length() - 4
    shard = w_query.shape[0]
    hid, wide = w_down.shape
    lens = doc_lengths.reshape(-1)
    mixer_local = jnp.concatenate(
        [
            w_query, w_key, w_value, w_outgate, w_rank,
            norm_gain_mix[:, None], norm_gain_mlp[:, None], jnp.zeros((shard, 110), BF), w_output.T,
        ],
        axis=1,
    )
    mixer_all = lax.all_gather(mixer_local, ("rows", "mlp"), axis=0, tiled=True)
    gain_mix = mixer_all[:, CR + 16].astype(F32)[None]
    gain_mlp = mixer_all[:, CR + 17].astype(F32)[None]
    mlp_local = jnp.stack([w_gate.T, w_up.T, w_down])
    mlp_all = lax.all_gather(mlp_local, ("rows", "mlp"), axis=0)
    mlp_all = mlp_all.reshape(8, rows // 8, mlps, 3, hid, wide)
    if rows > 8:
        mlp_all = mlp_all.transpose(0, 2, 3, 4, 1, 5)
    mlp_all = mlp_all.reshape(8, mlps, 3, hid, 128)
    decay_wide = jnp.concatenate([w_decay, jnp.zeros((112, DK), BF)], axis=0)
    head_row = head_gain.astype(F32)[None]
    residual, normed_in, q, k, cum, dp, v, gp, o, before, mixed, rank = fwd_call(
        lens, tokens, mixer_all, gain_mix, decay_wide, decay_bias.astype(F32)[None], head_row
    )
    block_out, normed_mid, hidden, grad_gate, grad_up, grad_res, grad_mixed, gain_mlp_part = mlp_call(
        residual, cotangent, gain_mlp, mlp_all
    )
    mine = bit_of("rows", low).astype(jnp.int32)[None]

    def grad_half(g, x, **how):
        sent = swap(dw_call(g, x, 1 - mine, **how), "rows", low, rows)
        return lambda: dw_call(g, x, mine, sent, **how)

    stacks = [grad_half(g, x) for g, x in ((grad_gate, normed_mid), (grad_up, normed_mid), (hidden, cotangent))]
    stack_out = grad_half(mixed, grad_mixed, wide=False, chunk=512)
    stacks = [s() for s in stacks]
    stack_out = stack_out()
    half = mlps * hid // 2
    parts = [
        halve_both(stacks[0], 0, low, rows),
        halve_both(stacks[1], 1, low, rows),
        jnp.concatenate(
            [halve_both(stacks[2][:, :half], 0, low, rows), halve_both(stacks[2][:, half:], 1, low, rows)], axis=0
        ),
    ]
    mlp_grads = jnp.stack([p.reshape(mlps, hid, 128) for p in parts], axis=1)
    if low:
        mlp_grads = mlp_grads.reshape((mlps, 3, hid) + (2,) * low + (wide,))
        for bit in reversed(range(low)):
            mlp_grads = halve(mlp_grads, 3, bit, rows)
    mlp_grads = line_sum(mlp_grads, mlps)

    grads, decay_part, bias_part, head_part = bwd_call(
        lens, grad_mixed, mixer_all, decay_wide, head_row, q, k, cum, dp, v, gp, o, before, rank
    )
    small = jnp.concatenate(
        [decay_part[:16].reshape(-1), bias_part.sum(0), head_part.sum(0), gain_mlp_part.sum(0)]
    )
    small = sum_all(small.reshape(-1, 256), rows, mlps).reshape(-1)
    stack_in = grad_half(grads, normed_in, wide=False, chunk=640)()
    grad_tokens, _ = dx_call(grads, mixer_all, tokens, gain_mix, grad_res)

    def finish(stack, first):
        part = halve_both(stack, first, low, rows)
        part = part.reshape((2,) * low + (mlps, shard, part.shape[-1]))
        for bit in reversed(range(low)):
            part = halve(part, 0, bit, rows)
        return line_sum(part, mlps)

    out_grads = finish(stack_out, 0)
    in_grads = jnp.concatenate(
        [finish(stack_in[:, :, :CV + 640], 0), finish(stack_in[:, :, CV + 640 :], 1)], axis=1
    )
    gain_mix_grad = jnp.sum(in_grads * mixer_local[:, :GW].astype(F32), axis=1) / norm_gain_mix.astype(F32)
    at = 16 * DK + DK + HV + (lax.axis_index("rows") * mlps + lax.axis_index("mlp")) * shard
    return (
        block_out,
        grad_tokens,
        gain_mix_grad,
        in_grads[:, CQ : CQ + DK],
        in_grads[:, CK : CK + DK],
        in_grads[:, CV : CV + DV],
        in_grads[:, CG : CG + DV],
        in_grads[:, CR : CR + 16],
        small[: 16 * DK].reshape(16, DK),
        small[16 * DK : 17 * DK],
        small[17 * DK : 17 * DK + HV],
        out_grads.T,
        lax.dynamic_slice_in_dim(small, at, shard),
        mlp_grads[0].T,
        mlp_grads[1].T,
        mlp_grads[2],
    )


def solution(mesh):
    in_specs = (
        P(("rows", "mlp"), None),
        P(("rows", "mlp"), None),
        P(("rows", "mlp"), None),
        P(("rows", "mlp")),
        P(("rows", "mlp"), None),
        P(("rows", "mlp"), None),
        P(("rows", "mlp"), None),
        P(("rows", "mlp"), None),
        P(("rows", "mlp"), None),
        P(),
        P(),
        P(),
        P(None, ("rows", "mlp")),
        P(("rows", "mlp")),
        P("rows", "mlp"),
        P("rows", "mlp"),
        P("mlp", "rows"),
    )
    out_specs = (
        P(("rows", "mlp"), None),
        P(("rows", "mlp"), None),
        P(("rows", "mlp")),
        P(("rows", "mlp"), None),
        P(("rows", "mlp"), None),
        P(("rows", "mlp"), None),
        P(("rows", "mlp"), None),
        P(("rows", "mlp"), None),
        P(),
        P(),
        P(),
        P(None, ("rows", "mlp")),
        P(("rows", "mlp")),
        P("rows", "mlp"),
        P("rows", "mlp"),
        P("mlp", "rows"),
    )
    return jax.shard_map(body, mesh=mesh, in_specs=in_specs, out_specs=out_specs, check_vma=False)
```

```python
import functools

import jax
import jax.numpy as jnp
from jax import lax
from jax.experimental import pallas as pl
from jax.experimental.pallas import tpu as pltpu
from jax.sharding import PartitionSpec as P

F32 = jnp.float32
BF = jnp.bfloat16
EPS = 1e-5
LEN = 1024
BL = 64
H = 4
HK = 128
HV = 256
DK = 512
DV = 1024
CQ, CK, CV, CG, CR, CO = 0, 512, 1024, 2048, 3072, 3200
GW = 3200
SCALE = HK**-0.5
VMEM = 60 * 1024 * 1024


def nn(a,b): return lax.dot_general(a,b,(((1,),(0,)),((),())),preferred_element_type=F32)


def nt(a,b): return lax.dot_general(a,b,(((1,),(1,)),((),())),preferred_element_type=F32)


def tn(a,b): return lax.dot_general(a,b,(((0,),(0,)),((),())),preferred_element_type=F32)


def sigmoid(v): return 1.0/(1.0+jnp.exp(-v))


def softminus(x): return jnp.minimum(x,0.0)-jnp.log1p(jnp.exp(-jnp.abs(x)))


def split(x):
    hi=x.astype(BF); return hi,(x-hi.astype(F32)).astype(BF)


def doc_of(p,starts):
    out=(p>=starts[0]).astype(jnp.int32)
    for s in starts[1:]: out=out+(p>=s).astype(jnp.int32)
    return out


def tile_masks(base,T,starts):
    tc=lax.broadcasted_iota(jnp.int32,(T,1),0); tr=lax.broadcasted_iota(jnp.int32,(1,T),1)
    dc=doc_of(tc+base,starts); dr=doc_of(tr+base,starts)
    first=(tc & ~(BL-1))+base
    prior=jnp.where(first>0,doc_of(first-1,starts),-1)
    last=doc_of(first+(BL-1),starts)
    inter=(dc==prior); reach=(dc==last)
    same=(tc>>6)==(tr>>6)
    low=same&(tc>=tr)
    return inter,reach,same,low,low&(dc==dr)


def keep_of(first,starts):
    return jnp.where(first>0,(doc_of(first-1,starts)==doc_of(first+BL-1,starts)).astype(F32),0.0)


def starts_of(len_ref, seq):
    first = len_ref[seq * 4]
    second = first + len_ref[seq * 4 + 1]
    return [first, second, second + len_ref[seq * 4 + 2]]


def params(flops=1):
    return dict(
        compiler_params=pltpu.CompilerParams(vmem_limit_bytes=VMEM),
        cost_estimate=pl.CostEstimate(flops=flops, bytes_accessed=1, transcendentals=0),
    )


def fwd_kernel(NT,cuts,st_ref,at_ref,tok_ref,wdec_ref,bias_ref,hg_ref,*rest):
    pieces=rest[:len(cuts)]
    n_ref,q_ref,k_ref,cum_ref,dp_ref,v_ref,gp_ref,o_ref,bef_ref,mix_ref,rank_ref,gains_ref,wout_ref,state,w_ref,sems,out_sem=rest[len(cuts):]
    T=tok_ref.shape[0]; nb=T//BL
    i=pl.program_id(0); seq=i//NT; tile=i%NT; base=tile*T
    starts=starts_of(st_ref,seq)
    inter,reach,same,low,intra=tile_masks(base,T,starts)
    @pl.when(tile==0)
    def _(): state[...]=jnp.zeros_like(state)
    save=pltpu.make_async_copy(w_ref,wout_ref,out_sem)
    @pl.when(i==0)
    def _():
        copies=[]
        for j,(block,first,width) in enumerate(cuts):
            for z in range(4):
                rows=pl.ds(pl.multiple_of(at_ref[block]*128+at_ref[8+z]*32,32),32)
                copies.append(pltpu.make_async_copy(pieces[j].at[pl.ds(32*z,32)],w_ref.at[rows,pl.ds(first,width)],sems.at[j,z]))
        for c in copies: c.start()
        for c in copies: c.wait()
        save.start()
        gains_ref[...]=w_ref[:,CR:CR+128].astype(F32).T[16:24]
    @pl.when(i==pl.num_programs(0)-1)
    def _(): save.wait()
    x=tok_ref[...].astype(F32)
    r=lax.rsqrt(jnp.mean(x*x,axis=-1,keepdims=True)+EPS)
    n_ref[...]=(x*r*gains_ref[0:1]).astype(BF)
    n=n_ref[...]
    rank=nn(n,w_ref[:,CR:CR+128]).astype(BF)
    rank_ref[...]=rank
    dp=nn(rank,wdec_ref[...])+bias_ref[...]
    dp_ref[...]=dp
    dhi,dlo=split(softminus(dp)*(1.0/16.0))
    lowb=low.astype(BF)
    cum=nn(lowb,dhi)+nn(lowb,dlo)
    cum_ref[...]=cum
    q=nn(n,w_ref[:,CQ:CQ+DK])*SCALE; q_ref[...]=q
    k=nn(n,w_ref[:,CK:CK+DK]); k_ref[...]=k
    v_ref[...]=nn(n,w_ref[:,CV:CV+DV]).astype(BF)
    gp_ref[...]=nn(n,w_ref[:,CG:CG+DV]).astype(BF)
    interf=inter.astype(F32)
    ends=[cum[BL*b+BL-1:BL*b+BL,:] for b in range(nb)]
    endb=jnp.concatenate([jnp.broadcast_to(e,(BL,DK)) for e in ends],axis=0)
    qg=q*jnp.exp(cum)
    qgi=(qg*interf).astype(BF); qg=qg.astype(BF)
    kg=(k*jnp.exp(-cum)).astype(BF)
    kc=(k*jnp.exp(endb-cum)).astype(BF)
    keeps=jnp.concatenate([jnp.exp(ends[b])*keep_of(base+BL*b,starts) for b in range(nb)]+[jnp.zeros((8-nb,DK),F32)],axis=0)
    for h in range(H):
        a=slice(HK*h,HK*h+HK); c=slice(HV*h,HV*h+HV)
        v=v_ref[:,c]
        s=jnp.where(intra,nt(qg[:,a],kg[:,a]),0.0).astype(BF)
        vk=jnp.where(reach,v,jnp.zeros_like(v))
        kt=keeps[:,a].T
        o=nn(s,v)
        parts=[]
        st=state[h]
        for b in range(nb):
            t=slice(BL*b,BL*b+BL)
            sb=st.astype(BF)
            bef_ref[b,h]=sb
            parts.append(nn(qgi[t,a],sb))
            st=st*kt[:,b:b+1]+tn(kc[t,a],vk[t])
        state[h]=st
        o=o+jnp.concatenate(parts,axis=0)
        o_ref[:,c]=o
        sc=lax.rsqrt(jnp.maximum(jnp.mean(o*o,axis=-1,keepdims=True),1.0))
        gp=gp_ref[:,c].astype(F32)
        mix_ref[:,c]=(o*sc*hg_ref[...]*(gp*sigmoid(gp))).astype(BF)


def fwd_call(st,at,tok,pieces,wdec,bias,hg,T=256):
    n,d=tok.shape; NT=LEN//T; sd=jax.ShapeDtypeStruct
    row=lambda x: pl.BlockSpec((T,x),lambda i,*s:(i,0))
    const=lambda a: pl.BlockSpec(a.shape,lambda i,*s:(0,0),pipeline_mode=pl.Buffered(1))
    hbm=pl.BlockSpec(memory_space=pl.ANY)
    nb=T//BL
    outs=[(d,BF),(DK,F32),(DK,F32),(DK,F32),(DK,F32),(DV,BF),(DV,BF),(DV,F32),None,(DV,BF),(128,BF)]
    specs=[row(o[0]) if o else pl.BlockSpec((nb,H,HK,HV),lambda i,*s:(i,0,0,0)) for o in outs]
    shapes=[sd((n,o[0]),o[1]) if o else sd((n//BL,H,HK,HV),BF) for o in outs]
    cuts=[(p[1],p[2],p[0].shape[1]) for p in pieces]
    return pl.pallas_call(functools.partial(fwd_kernel,NT,cuts),
        grid_spec=pltpu.PrefetchScalarGridSpec(num_scalar_prefetch=2,grid=(n//T,),
            in_specs=[row(d),const(wdec),const(bias),const(hg)]+[hbm]*len(pieces),out_specs=specs+[pl.BlockSpec((8,d),lambda i,*s:(0,0)),hbm],
            scratch_shapes=[pltpu.VMEM((H,HK,HV),F32),pltpu.VMEM((d,GW),BF),pltpu.SemaphoreType.DMA((len(pieces),4)),pltpu.SemaphoreType.DMA]),
        out_shape=shapes+[sd((8,d),F32),sd((d,GW),BF)],name="mixer_fwd",**params())(st,at,tok,wdec,bias,hg,*[p[0] for p in pieces])


def bwd_kernel(NT,seq,st_ref,gmix_ref,w_ref,wdec_ref,hg_ref,q_ref,k_ref,cum_ref,dp_ref,v_ref,gp_ref,o_ref,bef_ref,rank_ref,*rest):
    g_ref,dwd_ref,db_ref,dhg_ref,state=rest[-5:]
    T=q_ref.shape[0]; nb=T//BL
    step=pl.program_id(0); tile=NT-1-step; base=tile*T
    starts=starts_of(st_ref,seq)
    inter,reach,same,low,intra=tile_masks(base,T,starts)
    @pl.when(tile==NT-1)
    def _(): state[...]=jnp.zeros_like(state)
    @pl.when(step==0)
    def _():
        dwd_ref[...]=jnp.zeros_like(dwd_ref); db_ref[...]=jnp.zeros_like(db_ref); dhg_ref[...]=jnp.zeros_like(dhg_ref)
    cum=cum_ref[...]
    ends=[cum[BL*b+BL-1:BL*b+BL,:] for b in range(nb)]
    endb=jnp.concatenate([jnp.broadcast_to(e,(BL,DK)) for e in ends],axis=0)
    eg=jnp.exp(cum); es=jnp.exp(-cum); ec=jnp.exp(endb-cum)
    kend=jnp.concatenate([jnp.exp(ends[b])*keep_of(base+BL*b,starts) for b in range(nb)]+[jnp.zeros((8-nb,DK),F32)],axis=0)
    interb=inter.astype(F32).astype(BF); reachf=reach.astype(F32)
    tc=lax.broadcasted_iota(jnp.int32,(T,1),0); tr=lax.broadcasted_iota(jnp.int32,(1,T),1)
    upb=(same&(tc<=tr)).astype(BF); lsb=(same&(tc>tr)).astype(BF)
    hg=hg_ref[...]
    ones=jnp.ones((8,HV),BF)
    for h in range(H):
        a=slice(HK*h,HK*h+HK); c=slice(HV*h,HV*h+HV)
        gi=nn(gmix_ref[...],w_ref[:,HV*h:HV*h+HV])
        o=o_ref[:,c]; gp=gp_ref[:,c].astype(F32)
        ms=jnp.mean(o*o,axis=-1,keepdims=True)
        sc=lax.rsqrt(jnp.maximum(ms,1.0))
        hn0=o*sc
        s=sigmoid(gp); si=gp*s
        g_ref[:,CG+HV*h:CG+HV*h+HV]=(gi*hn0*hg*(s+si*(1.0-s))).astype(BF)
        G=gi*si
        dhg_ref[...]+=jnp.sum((G*hn0).reshape(-1,8,HV),axis=0)
        G=G*hg
        innr=jnp.mean(G*o,axis=-1,keepdims=True)*jnp.where(ms>1.0,1.0,0.0)
        go=(sc*G-o*(sc*sc*sc*innr)).astype(BF)
        goi=go*interb
        v=v_ref[:,c]
        qs=q_ref[:,a]*eg[:,a]; ks=k_ref[:,a]*es[:,a]; kd=k_ref[:,a]*ec[:,a]
        qg=qs.astype(BF); kg=ks.astype(BF); kc=kd.astype(BF)
        sco=jnp.where(intra,nt(qg,kg),0.0).astype(BF)
        gs=jnp.where(intra,nt(go,v),0.0).astype(BF)
        gv=tn(sco,go); gq=nn(gs,kg); gk=tn(gs,qg)
        kt=kend[:,a].T
        st=state[h]
        p_gv=[None]*nb; p_gq=[None]*nb; p_gkc=[None]*nb; p_end=[None]*nb
        for b in reversed(range(nb)):
            t=slice(BL*b,BL*b+BL)
            bef=bef_ref[b,h]
            sb=st.astype(BF)
            p_gv[b]=nn(kc[t],sb)
            p_gq[b]=nt(goi[t],bef)
            p_gkc[b]=nt(v[t],sb)
            m1,m2=split(st*bef.astype(F32))
            p_end[b]=(nt(ones,m1)+nt(ones,m2))[0:1]*kend[b:b+1,a]
            st=(tn(qg[t],goi[t])+kt[:,b:b+1]*st).astype(BF).astype(F32)
        state[h]=st
        cat=lambda p: jnp.concatenate(p,axis=0)
        gv=gv+cat(p_gv)*reachf
        g_ref[:,CV+HV*h:CV+HV*h+HV]=gv.astype(BF)
        gq=gq+cat(p_gq)
        gkc=cat(p_gkc)*reachf
        av1,av2=split(gq*qs-gk*ks)
        c1,c2=split(gkc*kd)
        endr=cat([jnp.broadcast_to(p,(BL,HK)) for p in p_end])
        gd=nn(upb,av1)+nn(upb,av2)+nn(lsb,c1)+nn(lsb,c2)+endr
        g_ref[:,CQ+HK*h:CQ+HK*h+HK]=(gq*eg[:,a]*SCALE).astype(BF)
        g_ref[:,CK+HK*h:CK+HK*h+HK]=(gk*es[:,a]+gkc*ec[:,a]).astype(BF)
        dp=dp_ref[:,a]
        gpre=(gd*(1.0/16.0)*(1.0/(1.0+jnp.exp(dp)))).astype(BF)
        db_ref[:,a]+=jnp.sum(gpre.astype(F32).reshape(-1,8,HK),axis=0)
        dwd_ref[:,a]+=tn(rank_ref[...],gpre)
        gr=nt(gpre,wdec_ref[:,a])
        grank=gr if h==0 else grank+gr
    g_ref[:,CR:CR+128]=grank.astype(BF)


def bwd_call(seq,before_g,deps,st,gmix,w,wdec,hg,q,k,cum,dp,v,gp,o,bef,rank,T=256):
    n,d=gmix.shape; NT=LEN//T; sd=jax.ShapeDtypeStruct; top=seq*NT+NT-1
    row=lambda a: pl.BlockSpec((T,a.shape[1]),lambda i,s:(top-i,0))
    const=lambda a: pl.BlockSpec(a.shape,lambda i,s:(0,0),pipeline_mode=pl.Buffered(1))
    hbm=pl.BlockSpec(memory_space=pl.ANY)
    nb=T//BL
    acc=lambda s: pl.BlockSpec(s,lambda i,_:(0,0))
    more=list(deps)+([before_g] if before_g is not None else [])
    return pl.pallas_call(functools.partial(bwd_kernel,NT,seq),
        grid_spec=pltpu.PrefetchScalarGridSpec(num_scalar_prefetch=1,grid=(NT,),
            in_specs=[row(gmix),const(w),const(wdec),const(hg),row(q),row(k),row(cum),row(dp),row(v),row(gp),row(o),pl.BlockSpec((nb,H,HK,HV),lambda i,s:(top-i,0,0,0)),row(rank)]+[hbm]*len(more),
            out_specs=[pl.BlockSpec((T,GW),lambda i,s:(top-i,0)),acc((128,DK)),acc((8,DK)),acc((8,HV))],
            scratch_shapes=[pltpu.VMEM((H,HK,HV),F32)]),
        input_output_aliases={} if before_g is None else {13+len(more):0},
        out_shape=[sd((n,GW),BF),sd((128,DK),F32),sd((8,DK),F32),sd((8,HV),F32)],
        name="mixer_bwd",**params())(st,gmix,w,wdec,hg,q,k,cum,dp,v,gp,o,bef,rank,*more)


def dx_kernel(g_ref,w_ref,tok_ref,gain_ref,gres_ref,*rest):
    gt_ref=rest[-1]
    gm=nt(g_ref[...],w_ref[...])
    x=tok_ref[...].astype(F32)
    r=lax.rsqrt(jnp.mean(x*x,axis=-1,keepdims=True)+EPS)
    sc=gm*gain_ref[...]
    inner=jnp.mean(sc*x,axis=-1,keepdims=True)
    gt_ref[...]=gres_ref[...]+r*sc-x*(r*r*r*inner)


def dx_call(part,parts,begun,g,w,tok,gain,gres,deps,T=256):
    n,d=tok.shape; sd=jax.ShapeDtypeStruct; steps=n//T//parts; first=part*steps
    row=lambda a: pl.BlockSpec((T,a.shape[1]),lambda i:(first+i,0))
    const=lambda a: pl.BlockSpec(a.shape,lambda i:(0,0),pipeline_mode=pl.Buffered(1))
    hbm=pl.BlockSpec(memory_space=pl.ANY)
    more=list(deps)+([] if begun is None else [begun])
    return pl.pallas_call(dx_kernel,grid=(steps,),in_specs=[row(g),const(w),row(tok),const(gain),row(gres)]+[hbm]*len(more),
        out_specs=row(gres),out_shape=sd((n,d),F32),input_output_aliases={} if begun is None else {4+len(more):0},
        name="mixer_dx",**params(5*10**10))(g,w,tok,gain,gres,*more)


def load_w(w_hbm,w_ref,sems,stacks):
    blocks,mlps,_,_=w_hbm.shape
    hid=w_ref.shape[1]//mlps
    copies=[pltpu.make_async_copy(w_hbm.at[r,m,pl.ds(s*hid,hid)],w_ref.at[i,pl.ds(m*hid,hid),pl.ds(r*128,128)],sems.at[i,r,m]) for i,s in enumerate(stacks) for m in range(mlps) for r in range(blocks)]
    for c in copies: c.start()
    for c in copies: c.wait()


def mlp_kernel(chunk,tok_ref,mix_ref,cot_ref,gain_ref,wo_ref,w_hbm,res_ref,n_ref,hid_ref,gg_ref,gu_ref,gres_ref,gmix_ref,gn_ref,w_ref,sems):
    @pl.when(pl.program_id(0)==0)
    def _(): load_w(w_hbm,w_ref,sems,(0,1,2))
    wg_ref,wu_ref,wd_ref=w_ref.at[0],w_ref.at[1],w_ref.at[2]
    res=tok_ref[...].astype(F32)+nt(mix_ref[...],wo_ref[...])
    res_ref[...]=res
    gain=gain_ref[...]
    r=lax.rsqrt(jnp.mean(res*res,axis=-1,keepdims=True)+EPS)
    n_ref[...]=(res*r*gain).astype(BF)
    ff=wg_ref.shape[0]
    for c in range(ff//chunk):
        sl=slice(c*chunk,(c+1)*chunk)
        n=n_ref[...]
        gp=nt(n,wg_ref[sl,:]); up=nt(n,wu_ref[sl,:]); gh=nt(cot_ref[...],wd_ref[sl,:])
        s=sigmoid(gp)
        si=gp*s
        hid_ref[:,sl]=(si*up).astype(BF)
        gu_ref[:,sl]=(gh*si).astype(BF)
        gg_ref[:,sl]=(gh*up*(s+si*(1.0-s))).astype(BF)
    gm=nn(gg_ref[...],wg_ref[...])+nn(gu_ref[...],wu_ref[...])
    res=res_ref[...]
    sc=gm*gain
    inner=jnp.mean(sc*res,axis=-1,keepdims=True)
    gi=r*sc-res*(r*r*r*inner)
    gres=cot_ref[...].astype(F32)+gi
    gres_ref[...]=gres
    gmix_ref[...]=gres.astype(BF)
    part=jnp.sum((gm*res*r).reshape(-1,8,gm.shape[1]),axis=0)
    @pl.when(pl.program_id(0)==0)
    def _(): gn_ref[...]=part
    @pl.when(pl.program_id(0)>0)
    def _(): gn_ref[...]+=part


def mlp_call(tok,mix,cot,gain,wo,w,ff,T=256,chunk=256):
    n,d=tok.shape
    row=lambda w: pl.BlockSpec((T,w),lambda i:(i,0))
    const=lambda a: pl.BlockSpec(a.shape,lambda i:(0,0),pipeline_mode=pl.Buffered(1))
    sd=jax.ShapeDtypeStruct
    return pl.pallas_call(functools.partial(mlp_kernel,chunk),grid=(n//T,),
        in_specs=[row(d),row(d),row(d),const(gain),const(wo),pl.BlockSpec(memory_space=pl.ANY)],
        out_specs=[row(d),row(d),row(ff),row(ff),row(ff),row(d),row(d),pl.BlockSpec((8,d),lambda i:(0,0))],
        out_shape=[sd((n,d),F32),sd((n,d),BF),sd((n,ff),BF),sd((n,ff),BF),sd((n,ff),BF),sd((n,d),F32),sd((n,d),BF),sd((8,d),F32)],
        scratch_shapes=[pltpu.VMEM((3,ff,d),BF),pltpu.SemaphoreType.DMA((3,)+w.shape[:2])],
        name="mlp",**params())(tok,mix,cot,gain,wo,w)


def down_kernel(res_ref,hid_ref,w_hbm,*rest):
    o_ref,w_ref,sems=rest[-3:]
    @pl.when(pl.program_id(0)==0)
    def _(): load_w(w_hbm,w_ref,sems,(2,))
    o_ref[...]=(res_ref[...]+nn(hid_ref[...],w_ref[0])).astype(BF)


def down_call(part,parts,begun,res,hid,w,deps,T=256):
    n,d=res.shape; ff=hid.shape[1]; steps=n//T//parts; first=part*steps
    row=lambda w: pl.BlockSpec((T,w),lambda i:(first+i,0))
    hbm=pl.BlockSpec(memory_space=pl.ANY)
    more=list(deps)+([] if begun is None else [begun])
    return pl.pallas_call(down_kernel,grid=(steps,),in_specs=[row(d),row(ff),hbm]+[hbm]*len(more),out_specs=row(d),
        out_shape=jax.ShapeDtypeStruct((n,d),BF),input_output_aliases={} if begun is None else {2+len(more):0},
        scratch_shapes=[pltpu.VMEM((1,ff,d),BF),pltpu.SemaphoreType.DMA((1,)+w.shape[:2])],
        name="mlp_down",**params())(res,hid,w,*more)


def dw_kernel(count,wide,sel_ref,*rest):
    g_refs=rest[:count]; x_hbm=rest[count]
    outs=rest[-2*count-2:-2]; xp,sems=rest[-2:]
    i=pl.program_id(0); steps=pl.num_programs(0)//count
    @pl.when(i==0)
    def _():
        copies=[]
        for p in range(2):
            for j in range(4):
                at=pl.multiple_of((2*j+(1-sel_ref[0] if p==0 else sel_ref[0]))*128,128)
                copies.append(pltpu.make_async_copy(x_hbm.at[:,pl.ds(at,128)],xp.at[:,pl.ds(512*p+128*j,128)],sems.at[p,j]))
        for c in copies: c.start()
        for c in copies: c.wait()
    for s in range(count):
        @pl.when(i//steps==s)
        def _():
            o=tn(g_refs[s][...],xp[...]) if wide else tn(xp[...],g_refs[s][...])
            for p in range(2):
                for j in range(4):
                    b=slice(512*p+128*j,512*p+128*j+128)
                    outs[2*s+p][j]=(o[:,b] if wide else o[b,:]).astype(BF)


def dw_call(gs,x,sel,deps,chunk,wide=True):
    n,ff=gs[0].shape; d=x.shape[1]; steps=ff//chunk; count=len(gs)
    hbm=pl.BlockSpec(memory_space=pl.ANY)
    spot=lambda i,s: jnp.clip(i-s*steps,0,steps-1)
    def out(s):
        return pl.BlockSpec((4,chunk,128),lambda i,_:(0,spot(i,s),0)) if wide else pl.BlockSpec((4,128,chunk),lambda i,_:(0,0,spot(i,s)))
    def inp(s):
        return pl.BlockSpec((n,chunk),lambda i,_:(0,spot(i,s)))
    return pl.pallas_call(functools.partial(dw_kernel,count,wide),
        grid_spec=pltpu.PrefetchScalarGridSpec(num_scalar_prefetch=1,grid=(steps*count,),
            in_specs=[inp(s) for s in range(count)]+[hbm]*(1+len(deps)),
            out_specs=[out(s) for s in range(count) for _ in range(2)],
            scratch_shapes=[pltpu.VMEM((n,d),BF),pltpu.SemaphoreType.DMA((2,4))]),
        out_shape=[jax.ShapeDtypeStruct((4,ff,128) if wide else (4,128,ff),BF)]*(2*count),
        name="grad_w",**params(10**11 if wide else 1))(sel,*gs,x,*deps)


def plane_kernel(count,at_ref,*rest):
    ins,outs=rest[:2*count],rest[-4:]
    for j in range(4):
        row=0
        for t in range(count):
            keep,came=ins[2*t],ins[2*t+1]
            rows=keep.shape[1]
            outs[j][0,row:row+rows]=(keep[at_ref[j]].astype(F32)+came[at_ref[j]].astype(F32)).astype(BF)
            row+=rows


def plane_call(pairs,at,deps,steps=8):
    each=[p[0].shape[1]//steps for p in pairs]
    return pl.pallas_call(functools.partial(plane_kernel,len(pairs)),
        grid_spec=pltpu.PrefetchScalarGridSpec(num_scalar_prefetch=1,grid=(steps,),
            in_specs=[pl.BlockSpec((4,r,128),lambda i,_:(0,i,0)) for r in each for _ in range(2)]+[pl.BlockSpec(memory_space=pl.ANY)]*len(deps),
            out_specs=[pl.BlockSpec((1,sum(each),128),lambda i,_:(i,0,0))]*4),
        out_shape=[jax.ShapeDtypeStruct((steps,sum(each),128),BF)]*4,name="plane",**params())(at,*[x for p in pairs for x in p],*deps)


def line_kernel(at_ref,*rest):
    ins=rest[:4]
    scr,turned=rest[-2:]; outs=rest[-6:-2]
    steps,rows,_=ins[0].shape
    main=rows-128
    for i in range(steps):
        v=functools.reduce(jnp.add,[x[i].astype(F32) for x in ins])
        scr[i]=v[:main].astype(BF)
        turned[i]=v[main:].T.astype(BF)
    each=steps//4
    for k in range(4):
        for e in range(each):
            outs[k][e*main:(e+1)*main]=scr[at_ref[k]*each+e]
        at=pl.multiple_of(at_ref[k]*32,32)
        for i in range(steps):
            outs[k][each*main+32*i:each*main+32*(i+1)]=turned[i,pl.ds(at,32)]


def line_call(parts,at,deps):
    steps,rows,_=parts[0].shape
    out=steps//4*(rows-128)+steps*32
    full=pl.BlockSpec(parts[0].shape,lambda i,_:(0,0,0))
    return pl.pallas_call(line_kernel,
        grid_spec=pltpu.PrefetchScalarGridSpec(num_scalar_prefetch=1,grid=(1,),
            in_specs=[full]*4+[pl.BlockSpec(memory_space=pl.ANY)]*len(deps),
            out_specs=[pl.BlockSpec((out,128),lambda i,_:(0,0))]*4,
            scratch_shapes=[pltpu.VMEM((steps,rows-128,128),BF),pltpu.VMEM((steps,128,128),BF)]),
        out_shape=[jax.ShapeDtypeStruct((out,128),BF)]*4,name="line",**params())(at,*parts,*deps)


def spread_kernel(sizes,count,at_ref,*rest):
    outs=rest[-count:]
    for j in range(count):
        first=k=0
        for stacks,parts in sizes:
            for t in range(stacks):
                v=rest[k][t,at_ref[j]].astype(F32)
                for p in range(1,parts): v=v+rest[k+p][t,at_ref[j]].astype(F32)
                outs[j][first+t]=v.astype(BF)
            first+=stacks; k+=parts


def spread(groups,at,axis,chunk,deps):
    _,count,rows,cols=groups[0][0].shape
    size=[rows,cols]; size[axis]=chunk
    place=(lambda i: (i,0)) if axis==0 else (lambda i: (0,i))
    stacks=sum(g[0].shape[0] for g in groups)
    return pl.pallas_call(functools.partial(spread_kernel,[(g[0].shape[0],len(g)) for g in groups],count),
        grid_spec=pltpu.PrefetchScalarGridSpec(num_scalar_prefetch=1,grid=((rows,cols)[axis]//chunk,),
            in_specs=[pl.BlockSpec((g[0].shape[0],count,*size),lambda i,_:(0,0,*place(i))) for g in groups for p in g]+[pl.BlockSpec(memory_space=pl.ANY)]*len(deps),
            out_specs=[pl.BlockSpec((stacks,*size),lambda i,_:(0,*place(i)))]*count),
        out_shape=[jax.ShapeDtypeStruct((stacks,rows,cols),BF)]*count,name="spread",**params())(at,*[p for g in groups for p in g],*deps)


def sum_kernel(count,*refs):
    refs[-1][...]=functools.reduce(jnp.add,[r[...].astype(F32) for r in refs[:count]])


def sum_call(parts,deps):
    full=pl.BlockSpec(parts[0].shape,lambda i:(0,)*parts[0].ndim)
    return pl.pallas_call(functools.partial(sum_kernel,len(parts)),grid=(1,),
        in_specs=[full]*len(parts)+[pl.BlockSpec(memory_space=pl.ANY)]*len(deps),out_specs=full,
        out_shape=jax.ShapeDtypeStruct(parts[0].shape,F32),name="sum_parts",**params())(*parts,*deps)


def rows_kernel(x_ref,*rest):
    rest[-1][...]=jnp.sum(x_ref[...],axis=0)


def rows_call(x,deps):
    return pl.pallas_call(rows_kernel,grid=(1,),
        in_specs=[pl.BlockSpec(x.shape,lambda i:(0,0,0))]+[pl.BlockSpec(memory_space=pl.ANY)]*len(deps),
        out_specs=pl.BlockSpec(x.shape[1:],lambda i:(0,0)),
        out_shape=jax.ShapeDtypeStruct(x.shape[1:],F32),name="sum_rows",**params())(x,*deps)


def swap(x, axis, bit, count):
    return lax.ppermute(x, axis, [(i, i ^ (1 << bit)) for i in range(count)])


def bit_of(axis, bit):
    return (lax.axis_index(axis) >> bit) & 1


def halve(x, dim, bit, count):
    place = bit_of("rows", bit)
    send = lax.dynamic_index_in_dim(x, 1 - place, dim, keepdims=False)
    keep = lax.dynamic_index_in_dim(x, place, dim, keepdims=False)
    return keep.astype(F32) + swap(send.astype(BF), "rows", bit, count).astype(F32)


def total(parts):
    return functools.reduce(jnp.add, [p.astype(F32) for p in parts])


def send_blocks(blocks, low, count):
    return [blocks[0]] + [
        lax.ppermute(blocks[j], "rows", [(i, i ^ (j << (low + 1))) for i in range(count)]) for j in range(1, 4)
    ]


def send_line(blocks, count):
    return [blocks[0]] + [
        lax.ppermute(blocks[j], "mlp", [(i, (i + j) % count) for i in range(count)]) for j in range(1, count)
    ]


def gather_pieces(x, low, mlps):
    half = x.shape[1] // 256 * 128
    line = [x] + [lax.ppermute(x, "mlp", [(i, (i + step) % mlps) for i in range(mlps)]) for step in range(1, mlps)]
    pieces = []
    for first, cols, bits in ((0, slice(0, half), (1, 2)), (half, slice(half, None), (2, 1))):
        held = [(jnp.concatenate([p[:, cols] for p in line], axis=0), 0)]
        for bit in bits + (0,):
            held = held + [(swap(p, "rows", bit, 8), at ^ (1 << bit)) for p, at in held]
        pieces += [(p, at, first) for p, at in held]
    return pieces


def body(
    tokens,
    doc_lengths,
    cotangent,
    norm_gain_mix,
    w_query,
    w_key,
    w_value,
    w_outgate,
    w_rank,
    w_decay,
    decay_bias,
    head_gain,
    w_output,
    norm_gain_mlp,
    w_gate,
    w_up,
    w_down,
):
    rows = lax.axis_size("rows")
    mlps = lax.axis_size("mlp")
    low = rows.bit_length() - 4
    shard = w_query.shape[0]
    hid, wide = w_down.shape
    lens = doc_lengths.reshape(-1)
    mixer_local = jnp.concatenate(
        [
            w_query, w_key, w_value, w_outgate, w_rank,
            norm_gain_mix[:, None], norm_gain_mlp[:, None], jnp.zeros((shard, 110), BF),
        ],
        axis=1,
    )
    mlp_local = jnp.concatenate([w_gate.T, w_up.T, w_down], axis=0)
    here = lax.axis_index("rows")
    if low == 0:
        local = [mlp_local, w_output.T.reshape(shard, 8, 128).transpose(1, 0, 2).reshape(8 * shard, 128)]
        mlp_all = lax.all_gather(jnp.concatenate(local, axis=0), ("rows", "mlp"), axis=0)
        w_out = mlp_all[:, 3 * hid :].reshape(rows * mlps, 8, shard, 128).transpose(0, 2, 1, 3).reshape(-1, DV)
        mlp_all = mlp_all.reshape(rows, mlps, 3 * hid + 8 * shard, 128)
        pieces = gather_pieces(mixer_local, low, mlps)
        at = jnp.concatenate([jnp.arange(8) ^ here, (lax.axis_index("mlp") - jnp.arange(mlps)) % mlps])
    else:
        mlp_all = lax.all_gather(mlp_local, ("rows", "mlp"), axis=0)
        mlp_all = mlp_all.reshape(8, rows // 8, mlps, 3 * hid, wide).transpose(0, 2, 3, 1, 4)
        mlp_all = mlp_all.reshape(8, mlps, 3 * hid, 128)
        w_out = lax.all_gather(w_output.T, ("rows", "mlp"), axis=0, tiled=True)
        whole = lax.all_gather(mixer_local, ("rows", "mlp"), axis=0, tiled=True)
        pieces = [(whole[128 * b : 128 * b + 128], b, 0) for b in range(8)]
        at = jnp.concatenate([jnp.arange(8), jnp.arange(4)])
    decay_wide = jnp.concatenate([w_decay, jnp.zeros((112, DK), BF)], axis=0)
    head_row = head_gain.astype(F32)[None]
    normed_in, q, k, cum, dp, v, gp, o, before, mixed, rank, gains, w_in = fwd_call(
        lens, at.astype(jnp.int32), tokens, pieces, decay_wide, decay_bias.astype(F32)[None], head_row
    )
    gain_mix, gain_mlp = gains[:1], gains[1:2]
    residual, normed_mid, hidden, grad_gate, grad_up, grad_res, grad_mixed, gain_mlp_part = mlp_call(
        tokens, mixed, cotangent, gain_mlp, w_out, mlp_all, mlps * hid
    )
    mine = bit_of("rows", low).astype(jnp.int32)[None]

    def with_other_core(send, keep):
        return [keep, swap(send, "rows", low, rows)]

    def within(parts, dim):
        if not low:
            return parts
        x = total(parts)
        x = x.reshape(x.shape[:dim] + (2,) * low + (x.shape[dim] >> low,) + x.shape[dim + 1 :])
        for bit in reversed(range(low)):
            x = halve(x, dim, bit, rows)
        return [x.astype(BF)]

    in_plane = ((here >> (low + 1)) ^ jnp.arange(4)).astype(jnp.int32)
    in_line = ((lax.axis_index("mlp") + jnp.arange(mlps)) % mlps).astype(jnp.int32)
    down_send, down_keep = dw_call([hidden], cotangent, mine, [normed_mid], 1408)
    down = with_other_core(down_send, down_keep)
    gate_send, gate_keep, up_send, up_keep = dw_call([grad_gate, grad_up], normed_mid, mine, [down_keep], 1408)
    gate = with_other_core(gate_send, gate_keep)
    up = with_other_core(up_send, up_keep)
    out_send, out_keep = dw_call([mixed], grad_mixed, mine, [gate_keep, down[1]], 512)
    out = with_other_core(out_send, out_keep)
    blocks = plane_call([gate, up, down, out], in_plane, [])
    common = (lens, grad_mixed, w_out, decay_wide, head_row, q, k, cum, dp, v, gp, o, before, rank)
    grads, small, deps = None, None, list(blocks)
    for seq in reversed(range(doc_lengths.shape[0])):
        grads, *sums = bwd_call(seq, grads, deps, *common)
        small = sums if small is None else [a + b for a, b in zip(small, sums)]
        deps = []
    in_send, in_keep = dw_call([grads], normed_in, mine, [], 640, wide=False)
    inner = with_other_core(in_send, in_keep)
    small = jnp.concatenate(
        [small[0][:16].reshape(-1), small[1].sum(0), small[2].sum(0), gain_mlp_part.sum(0)]
    )
    small = lax.all_gather(small.reshape(-1, 256), ("rows", "mlp"), axis=0)
    blocks = send_blocks(blocks, low, rows)
    if low:
        blocks = total(blocks)
        main = blocks[:, :-128].reshape(8, 3, -1, 128).transpose(1, 0, 2, 3).reshape(3, mlps, hid, 128)
        main = within([main], 3)[0]
        out = within([blocks[:, -128:].reshape(-1, 128)], 1)[0].reshape(DV, mlps, shard)
        main = send_line([jnp.take(main, in_line[j], axis=1) for j in range(mlps)], mlps)
        out = send_line([jnp.take(out, in_line[j], axis=1) for j in range(mlps)], mlps)
        deps = [in_keep]
    else:
        blocks = line_call(blocks, in_line, [in_keep])
        main = send_line(blocks, mlps)
        deps = list(blocks)
    grad_tokens = dx_call(0, 2, None, grads, w_in, tokens, gain_mix, grad_res, deps)
    blocks = spread([[p[None] for p in inner]], in_plane, 1, 640, [grad_tokens])
    grad_tokens = dx_call(1, 2, grad_tokens, grads, w_in, tokens, gain_mix, grad_res, list(blocks))
    block_out = down_call(0, 2, None, residual, hidden, mlp_all, [grad_tokens])
    block_out = down_call(1, 2, block_out, residual, hidden, mlp_all, [])
    blocks = within(send_blocks(blocks, low, rows), 1)
    blocks = [b.reshape(1, mlps, shard, GW) for b in blocks]
    if low:
        in_grads = send_line([jnp.take(blocks[0], in_line[j], axis=1).astype(BF) for j in range(mlps)], mlps)
    else:
        in_grads = send_line(spread([blocks], in_line, 1, 640, [block_out]), mlps)
    small = rows_call(small, [in_grads[0], block_out]).reshape(-1)
    if low:
        mlp_grads, out_grads = total(main), total(out)
    else:
        main = sum_call(main, [small])
        mlp_grads = main[: 3 * hid].reshape(2, 3, hid // 2, 128).transpose(1, 0, 2, 3).reshape(3, hid, 128)
        out_grads = main[3 * hid :].reshape(8, shard, 128).transpose(0, 2, 1).reshape(DV, shard)
    in_grads = total(in_grads)[0]
    gain_mix_grad = jnp.sum(in_grads * mixer_local.astype(F32), axis=1) / norm_gain_mix.astype(F32)
    at = 16 * DK + DK + HV + (here * mlps + lax.axis_index("mlp")) * shard
    return (
        block_out,
        grad_tokens,
        gain_mix_grad,
        in_grads[:, CQ : CQ + DK],
        in_grads[:, CK : CK + DK],
        in_grads[:, CV : CV + DV],
        in_grads[:, CG : CG + DV],
        in_grads[:, CR : CR + 16],
        small[: 16 * DK].reshape(16, DK),
        small[16 * DK : 17 * DK],
        small[17 * DK : 17 * DK + HV],
        out_grads,
        lax.dynamic_slice_in_dim(small, at, shard),
        mlp_grads[0].T,
        mlp_grads[1].T,
        mlp_grads[2],
    )


def solution(mesh):
    in_specs = (
        P(("rows", "mlp"), None),
        P(("rows", "mlp"), None),
        P(("rows", "mlp"), None),
        P(("rows", "mlp")),
        P(("rows", "mlp"), None),
        P(("rows", "mlp"), None),
        P(("rows", "mlp"), None),
        P(("rows", "mlp"), None),
        P(("rows", "mlp"), None),
        P(),
        P(),
        P(),
        P(None, ("rows", "mlp")),
        P(("rows", "mlp")),
        P("rows", "mlp"),
        P("rows", "mlp"),
        P("mlp", "rows"),
    )
    out_specs = (
        P(("rows", "mlp"), None),
        P(("rows", "mlp"), None),
        P(("rows", "mlp")),
        P(("rows", "mlp"), None),
        P(("rows", "mlp"), None),
        P(("rows", "mlp"), None),
        P(("rows", "mlp"), None),
        P(("rows", "mlp"), None),
        P(),
        P(),
        P(),
        P(None, ("rows", "mlp")),
        P(("rows", "mlp")),
        P("rows", "mlp"),
        P("rows", "mlp"),
        P("mlp", "rows"),
    )
    return jax.shard_map(body, mesh=mesh, in_specs=in_specs, out_specs=out_specs, check_vma=False)
```

```python
import functools

import jax
import jax.numpy as jnp
from jax import lax
from jax.experimental import pallas as pl
from jax.experimental.pallas import tpu as pltpu
from jax.sharding import PartitionSpec as P

F32 = jnp.float32
BF = jnp.bfloat16
EPS = 1e-5
LEN = 1024
BL = 64
H = 4
HK = 128
HV = 256
DK = 512
DV = 1024
CQ, CK, CV, CG, CR, CO = 0, 512, 1024, 2048, 3072, 3200
GW = 3200
SCALE = HK**-0.5
VMEM = 60 * 1024 * 1024


def nn(a,b): return lax.dot_general(a,b,(((1,),(0,)),((),())),preferred_element_type=F32)


def nt(a,b): return lax.dot_general(a,b,(((1,),(1,)),((),())),preferred_element_type=F32)


def tn(a,b): return lax.dot_general(a,b,(((0,),(0,)),((),())),preferred_element_type=F32)


def sigmoid(v): return 1.0/(1.0+jnp.exp(-v))


def softminus(x): return jnp.minimum(x,0.0)-jnp.log1p(jnp.exp(-jnp.abs(x)))


def split(x):
    hi=x.astype(BF); return hi,(x-hi.astype(F32)).astype(BF)


def doc_of(p,starts):
    out=(p>=starts[0]).astype(jnp.int32)
    for s in starts[1:]: out=out+(p>=s).astype(jnp.int32)
    return out


def tile_masks(base,T,starts):
    tc=lax.broadcasted_iota(jnp.int32,(T,1),0); tr=lax.broadcasted_iota(jnp.int32,(1,T),1)
    dc=doc_of(tc+base,starts); dr=doc_of(tr+base,starts)
    first=(tc & ~(BL-1))+base
    prior=jnp.where(first>0,doc_of(first-1,starts),-1)
    last=doc_of(first+(BL-1),starts)
    inter=(dc==prior); reach=(dc==last)
    same=(tc>>6)==(tr>>6)
    low=same&(tc>=tr)
    return inter,reach,same,low,low&(dc==dr)


def keep_of(first,starts):
    return jnp.where(first>0,(doc_of(first-1,starts)==doc_of(first+BL-1,starts)).astype(F32),0.0)


def starts_of(len_ref, seq):
    first = len_ref[seq * 4]
    second = first + len_ref[seq * 4 + 1]
    return [first, second, second + len_ref[seq * 4 + 2]]


def params(flops=1):
    return dict(
        compiler_params=pltpu.CompilerParams(vmem_limit_bytes=VMEM),
        cost_estimate=pl.CostEstimate(flops=flops, bytes_accessed=1, transcendentals=0),
    )


def fwd_kernel(NT,cuts,st_ref,at_ref,tok_ref,wdec_ref,bias_ref,hg_ref,*rest):
    pieces=rest[:len(cuts)]
    n_ref,q_ref,k_ref,cum_ref,dp_ref,v_ref,gp_ref,o_ref,bef_ref,mix_ref,rank_ref,gains_ref,wout_ref,state,w_ref,sems,out_sem=rest[len(cuts):]
    T=tok_ref.shape[0]; nb=T//BL
    i=pl.program_id(0); seq=i//NT; tile=i%NT; base=tile*T
    starts=starts_of(st_ref,seq)
    inter,reach,same,low,intra=tile_masks(base,T,starts)
    @pl.when(tile==0)
    def _(): state[...]=jnp.zeros_like(state)
    save=pltpu.make_async_copy(w_ref,wout_ref,out_sem)
    @pl.when(i==0)
    def _():
        copies=[]
        for j,(block,first,width) in enumerate(cuts):
            for z in range(4):
                rows=pl.ds(pl.multiple_of(at_ref[block]*128+at_ref[8+z]*32,32),32)
                copies.append(pltpu.make_async_copy(pieces[j].at[pl.ds(32*z,32)],w_ref.at[rows,pl.ds(first,width)],sems.at[j,z]))
        for c in copies: c.start()
        for c in copies: c.wait()
        save.start()
        gains_ref[...]=w_ref[:,CR:CR+128].astype(F32).T[16:24]
    @pl.when(i==pl.num_programs(0)-1)
    def _(): save.wait()
    x=tok_ref[...].astype(F32)
    r=lax.rsqrt(jnp.mean(x*x,axis=-1,keepdims=True)+EPS)
    n_ref[...]=(x*r*gains_ref[0:1]).astype(BF)
    n=n_ref[...]
    rank=nn(n,w_ref[:,CR:CR+128]).astype(BF)
    rank_ref[...]=rank
    dp=nn(rank,wdec_ref[...])+bias_ref[...]
    dp_ref[...]=dp
    dhi,dlo=split(softminus(dp)*(1.0/16.0))
    lowb=low.astype(BF)
    cum=nn(lowb,dhi)+nn(lowb,dlo)
    cum_ref[...]=cum
    q=nn(n,w_ref[:,CQ:CQ+DK])*SCALE; q_ref[...]=q
    k=nn(n,w_ref[:,CK:CK+DK]); k_ref[...]=k
    v_ref[...]=nn(n,w_ref[:,CV:CV+DV]).astype(BF)
    gp_ref[...]=nn(n,w_ref[:,CG:CG+DV]).astype(BF)
    interf=inter.astype(F32)
    ends=[cum[BL*b+BL-1:BL*b+BL,:] for b in range(nb)]
    endb=jnp.concatenate([jnp.broadcast_to(e,(BL,DK)) for e in ends],axis=0)
    qg=q*jnp.exp(cum)
    qgi=(qg*interf).astype(BF); qg=qg.astype(BF)
    kg=(k*jnp.exp(-cum)).astype(BF)
    kc=(k*jnp.exp(endb-cum)).astype(BF)
    keeps=jnp.concatenate([jnp.exp(ends[b])*keep_of(base+BL*b,starts) for b in range(nb)]+[jnp.zeros((8-nb,DK),F32)],axis=0)
    for h in range(H):
        a=slice(HK*h,HK*h+HK); c=slice(HV*h,HV*h+HV)
        v=v_ref[:,c]
        s=jnp.where(intra,nt(qg[:,a],kg[:,a]),0.0).astype(BF)
        vk=jnp.where(reach,v,jnp.zeros_like(v))
        kt=keeps[:,a].T
        o=nn(s,v)
        parts=[]
        st=state[h]
        for b in range(nb):
            t=slice(BL*b,BL*b+BL)
            sb=st.astype(BF)
            bef_ref[b,h]=sb
            parts.append(nn(qgi[t,a],sb))
            st=st*kt[:,b:b+1]+tn(kc[t,a],vk[t])
        state[h]=st
        o=o+jnp.concatenate(parts,axis=0)
        o_ref[:,c]=o
        sc=lax.rsqrt(jnp.maximum(jnp.mean(o*o,axis=-1,keepdims=True),1.0))
        gp=gp_ref[:,c].astype(F32)
        mix_ref[:,c]=(o*sc*hg_ref[...]*(gp*sigmoid(gp))).astype(BF)


def fwd_call(st,at,tok,pieces,wdec,bias,hg,T=256):
    n,d=tok.shape; NT=LEN//T; sd=jax.ShapeDtypeStruct
    row=lambda x: pl.BlockSpec((T,x),lambda i,*s:(i,0))
    const=lambda a: pl.BlockSpec(a.shape,lambda i,*s:(0,0),pipeline_mode=pl.Buffered(1))
    hbm=pl.BlockSpec(memory_space=pl.ANY)
    nb=T//BL
    outs=[(d,BF),(DK,F32),(DK,F32),(DK,F32),(DK,F32),(DV,BF),(DV,BF),(DV,F32),None,(DV,BF),(128,BF)]
    specs=[row(o[0]) if o else pl.BlockSpec((nb,H,HK,HV),lambda i,*s:(i,0,0,0)) for o in outs]
    shapes=[sd((n,o[0]),o[1]) if o else sd((n//BL,H,HK,HV),BF) for o in outs]
    cuts=[(p[1],p[2],p[0].shape[1]) for p in pieces]
    return pl.pallas_call(functools.partial(fwd_kernel,NT,cuts),
        grid_spec=pltpu.PrefetchScalarGridSpec(num_scalar_prefetch=2,grid=(n//T,),
            in_specs=[row(d),const(wdec),const(bias),const(hg)]+[hbm]*len(pieces),out_specs=specs+[pl.BlockSpec((8,d),lambda i,*s:(0,0)),hbm],
            scratch_shapes=[pltpu.VMEM((H,HK,HV),F32),pltpu.VMEM((d,GW),BF),pltpu.SemaphoreType.DMA((len(pieces),4)),pltpu.SemaphoreType.DMA]),
        out_shape=shapes+[sd((8,d),F32),sd((d,GW),BF)],name="mixer_fwd",**params())(st,at,tok,wdec,bias,hg,*[p[0] for p in pieces])


def bwd_kernel(NT,seq,st_ref,gmix_ref,w_ref,wdec_ref,hg_ref,q_ref,k_ref,cum_ref,dp_ref,v_ref,gp_ref,o_ref,bef_ref,rank_ref,*rest):
    g_ref,dwd_ref,db_ref,dhg_ref,state=rest[-5:]
    T=q_ref.shape[0]; nb=T//BL
    step=pl.program_id(0); tile=NT-1-step; base=tile*T
    starts=starts_of(st_ref,seq)
    inter,reach,same,low,intra=tile_masks(base,T,starts)
    @pl.when(tile==NT-1)
    def _(): state[...]=jnp.zeros_like(state)
    @pl.when(step==0)
    def _():
        dwd_ref[...]=jnp.zeros_like(dwd_ref); db_ref[...]=jnp.zeros_like(db_ref); dhg_ref[...]=jnp.zeros_like(dhg_ref)
    cum=cum_ref[...]
    ends=[cum[BL*b+BL-1:BL*b+BL,:] for b in range(nb)]
    endb=jnp.concatenate([jnp.broadcast_to(e,(BL,DK)) for e in ends],axis=0)
    eg=jnp.exp(cum); es=jnp.exp(-cum); ec=jnp.exp(endb-cum)
    kend=jnp.concatenate([jnp.exp(ends[b])*keep_of(base+BL*b,starts) for b in range(nb)]+[jnp.zeros((8-nb,DK),F32)],axis=0)
    interb=inter.astype(F32).astype(BF); reachf=reach.astype(F32)
    tc=lax.broadcasted_iota(jnp.int32,(T,1),0); tr=lax.broadcasted_iota(jnp.int32,(1,T),1)
    upb=(same&(tc<=tr)).astype(BF); lsb=(same&(tc>tr)).astype(BF)
    hg=hg_ref[...]
    ones=jnp.ones((8,HV),BF)
    for h in range(H):
        a=slice(HK*h,HK*h+HK); c=slice(HV*h,HV*h+HV)
        gi=nn(gmix_ref[...],w_ref[:,HV*h:HV*h+HV])
        o=o_ref[:,c]; gp=gp_ref[:,c].astype(F32)
        ms=jnp.mean(o*o,axis=-1,keepdims=True)
        sc=lax.rsqrt(jnp.maximum(ms,1.0))
        hn0=o*sc
        s=sigmoid(gp); si=gp*s
        g_ref[:,CG+HV*h:CG+HV*h+HV]=(gi*hn0*hg*(s+si*(1.0-s))).astype(BF)
        G=gi*si
        dhg_ref[...]+=jnp.sum((G*hn0).reshape(-1,8,HV),axis=0)
        G=G*hg
        innr=jnp.mean(G*o,axis=-1,keepdims=True)*jnp.where(ms>1.0,1.0,0.0)
        go=(sc*G-o*(sc*sc*sc*innr)).astype(BF)
        goi=go*interb
        v=v_ref[:,c]
        qs=q_ref[:,a]*eg[:,a]; ks=k_ref[:,a]*es[:,a]; kd=k_ref[:,a]*ec[:,a]
        qg=qs.astype(BF); kg=ks.astype(BF); kc=kd.astype(BF)
        sco=jnp.where(intra,nt(qg,kg),0.0).astype(BF)
        gs=jnp.where(intra,nt(go,v),0.0).astype(BF)
        gv=tn(sco,go); gq=nn(gs,kg); gk=tn(gs,qg)
        kt=kend[:,a].T
        st=state[h]
        p_gv=[None]*nb; p_gq=[None]*nb; p_gkc=[None]*nb; p_end=[None]*nb
        for b in reversed(range(nb)):
            t=slice(BL*b,BL*b+BL)
            bef=bef_ref[b,h]
            sb=st.astype(BF)
            p_gv[b]=nn(kc[t],sb)
            p_gq[b]=nt(goi[t],bef)
            p_gkc[b]=nt(v[t],sb)
            m1,m2=split(st*bef.astype(F32))
            p_end[b]=(nt(ones,m1)+nt(ones,m2))[0:1]*kend[b:b+1,a]
            st=(tn(qg[t],goi[t])+kt[:,b:b+1]*st).astype(BF).astype(F32)
        state[h]=st
        cat=lambda p: jnp.concatenate(p,axis=0)
        gv=gv+cat(p_gv)*reachf
        g_ref[:,CV+HV*h:CV+HV*h+HV]=gv.astype(BF)
        gq=gq+cat(p_gq)
        gkc=cat(p_gkc)*reachf
        av1,av2=split(gq*qs-gk*ks)
        c1,c2=split(gkc*kd)
        endr=cat([jnp.broadcast_to(p,(BL,HK)) for p in p_end])
        gd=nn(upb,av1)+nn(upb,av2)+nn(lsb,c1)+nn(lsb,c2)+endr
        g_ref[:,CQ+HK*h:CQ+HK*h+HK]=(gq*eg[:,a]*SCALE).astype(BF)
        g_ref[:,CK+HK*h:CK+HK*h+HK]=(gk*es[:,a]+gkc*ec[:,a]).astype(BF)
        dp=dp_ref[:,a]
        gpre=(gd*(1.0/16.0)*(1.0/(1.0+jnp.exp(dp)))).astype(BF)
        db_ref[:,a]+=jnp.sum(gpre.astype(F32).reshape(-1,8,HK),axis=0)
        dwd_ref[:,a]+=tn(rank_ref[...],gpre)
        gr=nt(gpre,wdec_ref[:,a])
        grank=gr if h==0 else grank+gr
    g_ref[:,CR:CR+128]=grank.astype(BF)


def bwd_call(seq,before_g,deps,st,gmix,w,wdec,hg,q,k,cum,dp,v,gp,o,bef,rank,T=256):
    n,d=gmix.shape; NT=LEN//T; sd=jax.ShapeDtypeStruct; top=seq*NT+NT-1
    row=lambda a: pl.BlockSpec((T,a.shape[1]),lambda i,s:(top-i,0))
    const=lambda a: pl.BlockSpec(a.shape,lambda i,s:(0,0),pipeline_mode=pl.Buffered(1))
    hbm=pl.BlockSpec(memory_space=pl.ANY)
    nb=T//BL
    acc=lambda s: pl.BlockSpec(s,lambda i,_:(0,0))
    more=list(deps)+([before_g] if before_g is not None else [])
    return pl.pallas_call(functools.partial(bwd_kernel,NT,seq),
        grid_spec=pltpu.PrefetchScalarGridSpec(num_scalar_prefetch=1,grid=(NT,),
            in_specs=[row(gmix),const(w),const(wdec),const(hg),row(q),row(k),row(cum),row(dp),row(v),row(gp),row(o),pl.BlockSpec((nb,H,HK,HV),lambda i,s:(top-i,0,0,0)),row(rank)]+[hbm]*len(more),
            out_specs=[pl.BlockSpec((T,GW),lambda i,s:(top-i,0)),acc((128,DK)),acc((8,DK)),acc((8,HV))],
            scratch_shapes=[pltpu.VMEM((H,HK,HV),F32)]),
        input_output_aliases={} if before_g is None else {13+len(more):0},
        out_shape=[sd((n,GW),BF),sd((128,DK),F32),sd((8,DK),F32),sd((8,HV),F32)],
        name="mixer_bwd",**params())(st,gmix,w,wdec,hg,q,k,cum,dp,v,gp,o,bef,rank,*more)


def dx_kernel(g_ref,w_ref,tok_ref,gain_ref,gres_ref,*rest):
    gt_ref=rest[-1]
    gm=nt(g_ref[...],w_ref[...])
    x=tok_ref[...].astype(F32)
    r=lax.rsqrt(jnp.mean(x*x,axis=-1,keepdims=True)+EPS)
    sc=gm*gain_ref[...]
    inner=jnp.mean(sc*x,axis=-1,keepdims=True)
    gt_ref[...]=gres_ref[...]+r*sc-x*(r*r*r*inner)


def dx_call(part,parts,begun,g,w,tok,gain,gres,deps,T=256):
    n,d=tok.shape; sd=jax.ShapeDtypeStruct; steps=n//T//parts; first=part*steps
    row=lambda a: pl.BlockSpec((T,a.shape[1]),lambda i:(first+i,0))
    const=lambda a: pl.BlockSpec(a.shape,lambda i:(0,0),pipeline_mode=pl.Buffered(1))
    hbm=pl.BlockSpec(memory_space=pl.ANY)
    more=list(deps)+([] if begun is None else [begun])
    return pl.pallas_call(dx_kernel,grid=(steps,),in_specs=[row(g),const(w),row(tok),const(gain),row(gres)]+[hbm]*len(more),
        out_specs=row(gres),out_shape=sd((n,d),F32),input_output_aliases={} if begun is None else {4+len(more):0},
        name="mixer_dx",**params())(g,w,tok,gain,gres,*more)


def load_w(w_hbm,w_ref,sems,stacks):
    blocks,mlps,_,_=w_hbm.shape
    hid=w_ref.shape[1]//mlps
    copies=[pltpu.make_async_copy(w_hbm.at[r,m,pl.ds(s*hid,hid)],w_ref.at[i,pl.ds(m*hid,hid),pl.ds(r*128,128)],sems.at[i,r,m]) for i,s in enumerate(stacks) for m in range(mlps) for r in range(blocks)]
    for c in copies: c.start()
    for c in copies: c.wait()


def mlp_kernel(chunk,tok_ref,mix_ref,cot_ref,gain_ref,wo_ref,w_hbm,res_ref,n_ref,hid_ref,gg_ref,gu_ref,gres_ref,gmix_ref,gn_ref,w_ref,sems):
    @pl.when(pl.program_id(0)==0)
    def _(): load_w(w_hbm,w_ref,sems,(0,1,2))
    wg_ref,wu_ref,wd_ref=w_ref.at[0],w_ref.at[1],w_ref.at[2]
    res=tok_ref[...].astype(F32)+nt(mix_ref[...],wo_ref[...])
    res_ref[...]=res
    gain=gain_ref[...]
    r=lax.rsqrt(jnp.mean(res*res,axis=-1,keepdims=True)+EPS)
    n_ref[...]=(res*r*gain).astype(BF)
    ff=wg_ref.shape[0]
    for c in range(ff//chunk):
        sl=slice(c*chunk,(c+1)*chunk)
        n=n_ref[...]
        gp=nt(n,wg_ref[sl,:]); up=nt(n,wu_ref[sl,:]); gh=nt(cot_ref[...],wd_ref[sl,:])
        s=sigmoid(gp)
        si=gp*s
        hid_ref[:,sl]=(si*up).astype(BF)
        gu_ref[:,sl]=(gh*si).astype(BF)
        gg_ref[:,sl]=(gh*up*(s+si*(1.0-s))).astype(BF)
    gm=nn(gg_ref[...],wg_ref[...])+nn(gu_ref[...],wu_ref[...])
    res=res_ref[...]
    sc=gm*gain
    inner=jnp.mean(sc*res,axis=-1,keepdims=True)
    gi=r*sc-res*(r*r*r*inner)
    gres=cot_ref[...].astype(F32)+gi
    gres_ref[...]=gres
    gmix_ref[...]=gres.astype(BF)
    part=jnp.sum((gm*res*r).reshape(-1,8,gm.shape[1]),axis=0)
    @pl.when(pl.program_id(0)==0)
    def _(): gn_ref[...]=part
    @pl.when(pl.program_id(0)>0)
    def _(): gn_ref[...]+=part


def mlp_call(tok,mix,cot,gain,wo,w,ff,T=256,chunk=256):
    n,d=tok.shape
    row=lambda w: pl.BlockSpec((T,w),lambda i:(i,0))
    const=lambda a: pl.BlockSpec(a.shape,lambda i:(0,0),pipeline_mode=pl.Buffered(1))
    sd=jax.ShapeDtypeStruct
    return pl.pallas_call(functools.partial(mlp_kernel,chunk),grid=(n//T,),
        in_specs=[row(d),row(d),row(d),const(gain),const(wo),pl.BlockSpec(memory_space=pl.ANY)],
        out_specs=[row(d),row(d),row(ff),row(ff),row(ff),row(d),row(d),pl.BlockSpec((8,d),lambda i:(0,0))],
        out_shape=[sd((n,d),F32),sd((n,d),BF),sd((n,ff),BF),sd((n,ff),BF),sd((n,ff),BF),sd((n,d),F32),sd((n,d),BF),sd((8,d),F32)],
        scratch_shapes=[pltpu.VMEM((3,ff,d),BF),pltpu.SemaphoreType.DMA((3,)+w.shape[:2])],
        name="mlp",**params())(tok,mix,cot,gain,wo,w)


def down_kernel(res_ref,hid_ref,w_hbm,*rest):
    o_ref,w_ref,sems=rest[-3:]
    @pl.when(pl.program_id(0)==0)
    def _(): load_w(w_hbm,w_ref,sems,(2,))
    o_ref[...]=(res_ref[...]+nn(hid_ref[...],w_ref[0])).astype(BF)


def down_call(part,parts,begun,res,hid,w,deps,T=256):
    n,d=res.shape; ff=hid.shape[1]; steps=n//T//parts; first=part*steps
    row=lambda w: pl.BlockSpec((T,w),lambda i:(first+i,0))
    hbm=pl.BlockSpec(memory_space=pl.ANY)
    more=list(deps)+([] if begun is None else [begun])
    return pl.pallas_call(down_kernel,grid=(steps,),in_specs=[row(d),row(ff),hbm]+[hbm]*len(more),out_specs=row(d),
        out_shape=jax.ShapeDtypeStruct((n,d),BF),input_output_aliases={} if begun is None else {2+len(more):0},
        scratch_shapes=[pltpu.VMEM((1,ff,d),BF),pltpu.SemaphoreType.DMA((1,)+w.shape[:2])],
        name="mlp_down",**params())(res,hid,w,*more)


def dw_kernel(count,wide,sel_ref,*rest):
    g_refs=rest[:count]; x_hbm=rest[count]
    outs=rest[-2*count-2:-2]; xp,sems=rest[-2:]
    i=pl.program_id(0); steps=pl.num_programs(0)//count
    @pl.when(i==0)
    def _():
        copies=[]
        for p in range(2):
            for j in range(4):
                at=pl.multiple_of((2*j+(1-sel_ref[0] if p==0 else sel_ref[0]))*128,128)
                copies.append(pltpu.make_async_copy(x_hbm.at[:,pl.ds(at,128)],xp.at[:,pl.ds(512*p+128*j,128)],sems.at[p,j]))
        for c in copies: c.start()
        for c in copies: c.wait()
    for s in range(count):
        @pl.when(i//steps==s)
        def _():
            o=tn(g_refs[s][...],xp[...]) if wide else tn(xp[...],g_refs[s][...])
            for p in range(2):
                for j in range(4):
                    b=slice(512*p+128*j,512*p+128*j+128)
                    outs[2*s+p][j]=(o[:,b] if wide else o[b,:]).astype(BF)


def dw_call(gs,x,sel,deps,chunk,wide=True):
    n,ff=gs[0].shape; d=x.shape[1]; steps=ff//chunk; count=len(gs)
    hbm=pl.BlockSpec(memory_space=pl.ANY)
    spot=lambda i,s: jnp.clip(i-s*steps,0,steps-1)
    def out(s):
        return pl.BlockSpec((4,chunk,128),lambda i,_:(0,spot(i,s),0)) if wide else pl.BlockSpec((4,128,chunk),lambda i,_:(0,0,spot(i,s)))
    def inp(s):
        return pl.BlockSpec((n,chunk),lambda i,_:(0,spot(i,s)))
    return pl.pallas_call(functools.partial(dw_kernel,count,wide),
        grid_spec=pltpu.PrefetchScalarGridSpec(num_scalar_prefetch=1,grid=(steps*count,),
            in_specs=[inp(s) for s in range(count)]+[hbm]*(1+len(deps)),
            out_specs=[out(s) for s in range(count) for _ in range(2)],
            scratch_shapes=[pltpu.VMEM((n,d),BF),pltpu.SemaphoreType.DMA((2,4))]),
        out_shape=[jax.ShapeDtypeStruct((4,ff,128) if wide else (4,128,ff),BF)]*(2*count),
        name="grad_w",**params(10**11 if wide else 1))(sel,*gs,x,*deps)


def plane_kernel(count,at_ref,*rest):
    ins,outs=rest[:2*count],rest[-4:]
    for j in range(4):
        row=0
        for t in range(count):
            keep,came=ins[2*t],ins[2*t+1]
            rows=keep.shape[1]
            outs[j][0,row:row+rows]=keep[at_ref[j]]+came[at_ref[j]]
            row+=rows


def plane_call(pairs,at,deps,steps=8):
    each=[p[0].shape[1]//steps for p in pairs]
    return pl.pallas_call(functools.partial(plane_kernel,len(pairs)),
        grid_spec=pltpu.PrefetchScalarGridSpec(num_scalar_prefetch=1,grid=(steps,),
            in_specs=[pl.BlockSpec((4,r,128),lambda i,_:(0,i,0)) for r in each for _ in range(2)]+[pl.BlockSpec(memory_space=pl.ANY)]*len(deps),
            out_specs=[pl.BlockSpec((1,sum(each),128),lambda i,_:(i,0,0))]*4),
        out_shape=[jax.ShapeDtypeStruct((steps,sum(each),128),BF)]*4,name="plane",**params())(at,*[x for p in pairs for x in p],*deps)


def line_kernel(*refs):
    ins=refs[:4]
    out,scr,turned=refs[-3:]
    steps,rows,_=ins[0].shape
    main=rows-128
    for i in range(steps):
        v=functools.reduce(jnp.add,[x[i].astype(F32) for x in ins])
        scr[i]=v[:main].astype(BF)
        turned[i]=v[main:].T.astype(BF)
    each=steps//4; size=each*main+32*steps
    for k in range(4):
        for e in range(each):
            out[k*size+e*main:k*size+(e+1)*main]=scr[k*each+e]
        for i in range(steps):
            at=k*size+each*main+32*i
            out[at:at+32]=turned[i,32*k:32*k+32]


def line_call(parts,deps):
    steps,rows,_=parts[0].shape
    shape=(4*(steps//4*(rows-128)+steps*32),128)
    full=pl.BlockSpec(parts[0].shape,lambda i:(0,0,0))
    return pl.pallas_call(line_kernel,grid=(1,),
        in_specs=[full]*4+[pl.BlockSpec(memory_space=pl.ANY)]*len(deps),out_specs=pl.BlockSpec(shape,lambda i:(0,0)),
        scratch_shapes=[pltpu.VMEM((steps,rows-128,128),BF),pltpu.VMEM((steps,128,128),BF)],
        out_shape=jax.ShapeDtypeStruct(shape,BF),name="line",**params(5*10**10))(*parts,*deps)


def stack_kernel(count,*refs):
    refs[-1][...]=functools.reduce(jnp.add,[r[...].astype(F32) for r in refs[:count]]).astype(BF)


def stack_call(parts,chunk,deps):
    rows,cols=parts[0].shape
    spec=pl.BlockSpec((rows,chunk),lambda i:(0,i))
    return pl.pallas_call(functools.partial(stack_kernel,len(parts)),grid=(cols//chunk,),
        in_specs=[spec]*len(parts)+[pl.BlockSpec(memory_space=pl.ANY)]*len(deps),out_specs=spec,
        out_shape=jax.ShapeDtypeStruct((rows,cols),BF),name="stack",**params())(*parts,*deps)


def spread_kernel(sizes,count,at_ref,*rest):
    outs=rest[-count:]
    for j in range(count):
        first=k=0
        for stacks,parts in sizes:
            for t in range(stacks):
                v=rest[k][t,at_ref[j]].astype(F32)
                for p in range(1,parts): v=v+rest[k+p][t,at_ref[j]].astype(F32)
                outs[j][first+t]=v.astype(BF)
            first+=stacks; k+=parts


def spread(groups,at,axis,chunk,deps):
    _,count,rows,cols=groups[0][0].shape
    size=[rows,cols]; size[axis]=chunk
    place=(lambda i: (i,0)) if axis==0 else (lambda i: (0,i))
    stacks=sum(g[0].shape[0] for g in groups)
    return pl.pallas_call(functools.partial(spread_kernel,[(g[0].shape[0],len(g)) for g in groups],count),
        grid_spec=pltpu.PrefetchScalarGridSpec(num_scalar_prefetch=1,grid=((rows,cols)[axis]//chunk,),
            in_specs=[pl.BlockSpec((g[0].shape[0],count,*size),lambda i,_:(0,0,*place(i))) for g in groups for p in g]+[pl.BlockSpec(memory_space=pl.ANY)]*len(deps),
            out_specs=[pl.BlockSpec((stacks,*size),lambda i,_:(0,*place(i)))]*count),
        out_shape=[jax.ShapeDtypeStruct((stacks,rows,cols),BF)]*count,name="spread",**params())(at,*[p for g in groups for p in g],*deps)


def rows_kernel(x_ref,*rest):
    rest[-1][...]=jnp.sum(x_ref[...].astype(F32),axis=0)


def rows_call(x,deps):
    return pl.pallas_call(rows_kernel,grid=(1,),
        in_specs=[pl.BlockSpec(x.shape,lambda i:(0,0,0))]+[pl.BlockSpec(memory_space=pl.ANY)]*len(deps),
        out_specs=pl.BlockSpec(x.shape[1:],lambda i:(0,0)),
        out_shape=jax.ShapeDtypeStruct(x.shape[1:],F32),name="sum_rows",**params())(x,*deps)


def swap(x, axis, bit, count):
    return lax.ppermute(x, axis, [(i, i ^ (1 << bit)) for i in range(count)])


def bit_of(axis, bit):
    return (lax.axis_index(axis) >> bit) & 1


def halve(x, dim, bit, count):
    place = bit_of("rows", bit)
    send = lax.dynamic_index_in_dim(x, 1 - place, dim, keepdims=False)
    keep = lax.dynamic_index_in_dim(x, place, dim, keepdims=False)
    return keep.astype(F32) + swap(send.astype(BF), "rows", bit, count).astype(F32)


def total(parts):
    return functools.reduce(jnp.add, [p.astype(F32) for p in parts])


def send_blocks(blocks, low, count):
    return [blocks[0]] + [
        lax.ppermute(blocks[j], "rows", [(i, i ^ (j << (low + 1))) for i in range(count)]) for j in range(1, 4)
    ]


def send_line(blocks, count):
    return [blocks[0]] + [
        lax.ppermute(blocks[j], "mlp", [(i, (i + j) % count) for i in range(count)]) for j in range(1, count)
    ]


def gather_pieces(x, low, mlps):
    half = x.shape[1] // 256 * 128
    line = [x] + [lax.ppermute(x, "mlp", [(i, (i + step) % mlps) for i in range(mlps)]) for step in range(1, mlps)]
    pieces = []
    for first, cols, bits in ((0, slice(0, half), (1, 2)), (half, slice(half, None), (2, 1))):
        held = [(jnp.concatenate([p[:, cols] for p in line], axis=0), 0)]
        for bit in bits + (0,):
            held = held + [(swap(p, "rows", bit, 8), at ^ (1 << bit)) for p, at in held]
        pieces += [(p, at, first) for p, at in held]
    return pieces


def body(
    tokens,
    doc_lengths,
    cotangent,
    norm_gain_mix,
    w_query,
    w_key,
    w_value,
    w_outgate,
    w_rank,
    w_decay,
    decay_bias,
    head_gain,
    w_output,
    norm_gain_mlp,
    w_gate,
    w_up,
    w_down,
):
    rows = lax.axis_size("rows")
    mlps = lax.axis_size("mlp")
    low = rows.bit_length() - 4
    shard = w_query.shape[0]
    hid, wide = w_down.shape
    lens = doc_lengths.reshape(-1)
    mixer_local = jnp.concatenate(
        [
            w_query, w_key, w_value, w_outgate, w_rank,
            norm_gain_mix[:, None], norm_gain_mlp[:, None], jnp.zeros((shard, 110), BF),
        ],
        axis=1,
    )
    mlp_local = jnp.concatenate([w_gate.T, w_up.T, w_down], axis=0)
    here = lax.axis_index("rows")
    if low == 0:
        local = [mlp_local, w_output.T.reshape(shard, 8, 128).transpose(1, 0, 2).reshape(8 * shard, 128)]
        mlp_all = lax.all_gather(jnp.concatenate(local, axis=0), ("rows", "mlp"), axis=0)
        w_out = mlp_all[:, 3 * hid :].reshape(rows * mlps, 8, shard, 128).transpose(0, 2, 1, 3).reshape(-1, DV)
        mlp_all = mlp_all.reshape(rows, mlps, 3 * hid + 8 * shard, 128)
        pieces = gather_pieces(mixer_local, low, mlps)
        at = jnp.concatenate([jnp.arange(8) ^ here, (lax.axis_index("mlp") - jnp.arange(mlps)) % mlps])
    else:
        mlp_all = lax.all_gather(mlp_local, ("rows", "mlp"), axis=0)
        mlp_all = mlp_all.reshape(8, rows // 8, mlps, 3 * hid, wide).transpose(0, 2, 3, 1, 4)
        mlp_all = mlp_all.reshape(8, mlps, 3 * hid, 128)
        w_out = lax.all_gather(w_output.T, ("rows", "mlp"), axis=0, tiled=True)
        whole = lax.all_gather(mixer_local, ("rows", "mlp"), axis=0, tiled=True)
        pieces = [(whole[128 * b : 128 * b + 128], b, 0) for b in range(8)]
        at = jnp.concatenate([jnp.arange(8), jnp.arange(4)])
    decay_wide = jnp.concatenate([w_decay, jnp.zeros((112, DK), BF)], axis=0)
    head_row = head_gain.astype(F32)[None]
    normed_in, q, k, cum, dp, v, gp, o, before, mixed, rank, gains, w_in = fwd_call(
        lens, at.astype(jnp.int32), tokens, pieces, decay_wide, decay_bias.astype(F32)[None], head_row
    )
    gain_mix, gain_mlp = gains[:1], gains[1:2]
    residual, normed_mid, hidden, grad_gate, grad_up, grad_res, grad_mixed, gain_mlp_part = mlp_call(
        tokens, mixed, cotangent, gain_mlp, w_out, mlp_all, mlps * hid
    )
    mine = bit_of("rows", low).astype(jnp.int32)[None]

    def with_other_core(send, keep):
        return [keep, swap(send, "rows", low, rows)]

    def within(parts, dim):
        if not low:
            return parts
        x = total(parts)
        x = x.reshape(x.shape[:dim] + (2,) * low + (x.shape[dim] >> low,) + x.shape[dim + 1 :])
        for bit in reversed(range(low)):
            x = halve(x, dim, bit, rows)
        return [x.astype(BF)]

    in_plane = ((here >> (low + 1)) ^ jnp.arange(4)).astype(jnp.int32)
    in_line = ((lax.axis_index("mlp") + jnp.arange(mlps)) % mlps).astype(jnp.int32)
    down_send, down_keep = dw_call([hidden], cotangent, mine, [normed_mid], 1408)
    down = with_other_core(down_send, down_keep)
    gate_send, gate_keep, up_send, up_keep = dw_call([grad_gate, grad_up], normed_mid, mine, [down_keep], 1408)
    gate = with_other_core(gate_send, gate_keep)
    up = with_other_core(up_send, up_keep)
    out_send, out_keep = dw_call([mixed], grad_mixed, mine, [gate_keep, down[1]], 512)
    out = with_other_core(out_send, out_keep)
    blocks = plane_call([gate, up, down, out], in_plane, [])
    common = (lens, grad_mixed, w_out, decay_wide, head_row, q, k, cum, dp, v, gp, o, before, rank)
    grads, small, deps = None, None, list(blocks)
    for seq in reversed(range(doc_lengths.shape[0])):
        grads, *sums = bwd_call(seq, grads, deps, *common)
        small = sums if small is None else [a + b for a, b in zip(small, sums)]
        deps = []
    in_send, in_keep = dw_call([grads], normed_in, mine, [], 640, wide=False)
    inner = with_other_core(in_send, in_keep)
    small = jnp.concatenate(
        [small[0][:16].reshape(-1), small[1].sum(0), small[2].sum(0), gain_mlp_part.sum(0)]
    )
    small = lax.all_gather(small.reshape(-1, 256), ("rows", "mlp"), axis=0)
    blocks = send_blocks(blocks, low, rows)
    if low:
        blocks = total(blocks)
        main = blocks[:, :-128].reshape(8, 3, -1, 128).transpose(1, 0, 2, 3).reshape(3, mlps, hid, 128)
        main = within([main], 3)[0]
        out = within([blocks[:, -128:].reshape(-1, 128)], 1)[0].reshape(DV, mlps, shard)
        main = send_line([jnp.take(main, in_line[j], axis=1) for j in range(mlps)], mlps)
        out = send_line([jnp.take(out, in_line[j], axis=1) for j in range(mlps)], mlps)
        deps = [in_keep]
    else:
        blocks = line_call(blocks, [in_keep])
        main = lax.psum_scatter(blocks, "mlp", scatter_dimension=0, tiled=True)
        deps = [blocks]
    blocks = spread([[p[None] for p in inner]], in_plane, 1, 640, deps)
    grad_tokens = dx_call(0, 2, None, grads, w_in, tokens, gain_mix, grad_res, list(blocks))
    grad_tokens = dx_call(1, 2, grad_tokens, grads, w_in, tokens, gain_mix, grad_res, [])
    block_out = down_call(0, 2, None, residual, hidden, mlp_all, [grad_tokens])
    small = rows_call(small, [block_out])
    blocks = within(send_blocks(blocks, low, rows), 1)
    blocks = stack_call([b.reshape(-1, GW) for b in blocks], 640, [block_out]).reshape(mlps, shard, GW)
    in_grads = lax.all_to_all(blocks, "mlp", 0, 0, tiled=True)
    block_out = down_call(1, 2, block_out, residual, hidden, mlp_all, [small, blocks])
    small = small.reshape(-1)
    in_grads = total([in_grads[j] for j in range(mlps)])
    if low:
        mlp_grads, out_grads = total(main), total(out)
    else:
        main = main.astype(F32)
        mlp_grads = main[: 3 * hid].reshape(2, 3, hid // 2, 128).transpose(1, 0, 2, 3).reshape(3, hid, 128)
        out_grads = main[3 * hid :].reshape(8, shard, 128).transpose(0, 2, 1).reshape(DV, shard)
    gain_mix_grad = jnp.sum(in_grads * mixer_local.astype(F32), axis=1) / norm_gain_mix.astype(F32)
    at = 16 * DK + DK + HV + (here * mlps + lax.axis_index("mlp")) * shard
    return (
        block_out,
        grad_tokens,
        gain_mix_grad,
        in_grads[:, CQ : CQ + DK],
        in_grads[:, CK : CK + DK],
        in_grads[:, CV : CV + DV],
        in_grads[:, CG : CG + DV],
        in_grads[:, CR : CR + 16],
        small[: 16 * DK].reshape(16, DK),
        small[16 * DK : 17 * DK],
        small[17 * DK : 17 * DK + HV],
        out_grads,
        lax.dynamic_slice_in_dim(small, at, shard),
        mlp_grads[0].T,
        mlp_grads[1].T,
        mlp_grads[2],
    )


def solution(mesh):
    in_specs = (
        P(("rows", "mlp"), None),
        P(("rows", "mlp"), None),
        P(("rows", "mlp"), None),
        P(("rows", "mlp")),
        P(("rows", "mlp"), None),
        P(("rows", "mlp"), None),
        P(("rows", "mlp"), None),
        P(("rows", "mlp"), None),
        P(("rows", "mlp"), None),
        P(),
        P(),
        P(),
        P(None, ("rows", "mlp")),
        P(("rows", "mlp")),
        P("rows", "mlp"),
        P("rows", "mlp"),
        P("mlp", "rows"),
    )
    out_specs = (
        P(("rows", "mlp"), None),
        P(("rows", "mlp"), None),
        P(("rows", "mlp")),
        P(("rows", "mlp"), None),
        P(("rows", "mlp"), None),
        P(("rows", "mlp"), None),
        P(("rows", "mlp"), None),
        P(("rows", "mlp"), None),
        P(),
        P(),
        P(),
        P(None, ("rows", "mlp")),
        P(("rows", "mlp")),
        P("rows", "mlp"),
        P("rows", "mlp"),
        P("mlp", "rows"),
    )
    return jax.shard_map(body, mesh=mesh, in_specs=in_specs, out_specs=out_specs, check_vma=False)
```

```python
import functools

import jax
import jax.numpy as jnp
from jax import lax
from jax.experimental import pallas as pl
from jax.experimental.pallas import tpu as pltpu
from jax.sharding import PartitionSpec as P

F32 = jnp.float32
BF = jnp.bfloat16
EPS = 1e-5
LEN = 1024
BL = 64
H = 4
HK = 128
HV = 256
DK = 512
DV = 1024
CQ, CK, CV, CG, CR, CO = 0, 512, 1024, 2048, 3072, 3200
GW = 3200
SCALE = HK**-0.5
VMEM = 60 * 1024 * 1024


def nn(a,b): return lax.dot_general(a,b,(((1,),(0,)),((),())),preferred_element_type=F32)


def nt(a,b): return lax.dot_general(a,b,(((1,),(1,)),((),())),preferred_element_type=F32)


def tn(a,b): return lax.dot_general(a,b,(((0,),(0,)),((),())),preferred_element_type=F32)


def sigmoid(v): return 1.0/(1.0+jnp.exp(-v))


def softminus(x): return jnp.minimum(x,0.0)-jnp.log1p(jnp.exp(-jnp.abs(x)))


def split(x):
    hi=x.astype(BF); return hi,(x-hi.astype(F32)).astype(BF)


def doc_of(p,starts):
    out=(p>=starts[0]).astype(jnp.int32)
    for s in starts[1:]: out=out+(p>=s).astype(jnp.int32)
    return out


def tile_masks(base,T,starts):
    tc=lax.broadcasted_iota(jnp.int32,(T,1),0); tr=lax.broadcasted_iota(jnp.int32,(1,T),1)
    dc=doc_of(tc+base,starts); dr=doc_of(tr+base,starts)
    first=(tc & ~(BL-1))+base
    prior=jnp.where(first>0,doc_of(first-1,starts),-1)
    last=doc_of(first+(BL-1),starts)
    inter=(dc==prior); reach=(dc==last)
    same=(tc>>6)==(tr>>6)
    low=same&(tc>=tr)
    return inter,reach,same,low,low&(dc==dr)


def keep_of(first,starts):
    return jnp.where(first>0,(doc_of(first-1,starts)==doc_of(first+BL-1,starts)).astype(F32),0.0)


def starts_of(len_ref, seq):
    first = len_ref[seq * 4]
    second = first + len_ref[seq * 4 + 1]
    return [first, second, second + len_ref[seq * 4 + 2]]


def params(flops=1):
    return dict(
        compiler_params=pltpu.CompilerParams(vmem_limit_bytes=VMEM),
        cost_estimate=pl.CostEstimate(flops=flops, bytes_accessed=1, transcendentals=0),
    )


def fwd_kernel(NT,cuts,st_ref,at_ref,tok_ref,wdec_ref,bias_ref,hg_ref,*rest):
    pieces=rest[:len(cuts)]
    n_ref,q_ref,k_ref,cum_ref,dp_ref,v_ref,gp_ref,o_ref,bef_ref,mix_ref,rank_ref,gains_ref,win_ref,wout_ref,state,w_ref,sems,save_sems=rest[len(cuts):]
    T=tok_ref.shape[0]; nb=T//BL
    i=pl.program_id(0); seq=i//NT; tile=i%NT; base=tile*T
    starts=starts_of(st_ref,seq)
    inter,reach,same,low,intra=tile_masks(base,T,starts)
    @pl.when(tile==0)
    def _(): state[...]=jnp.zeros_like(state)
    saves=[pltpu.make_async_copy(w_ref.at[:,pl.ds(0,GW)],win_ref,save_sems.at[0]),pltpu.make_async_copy(w_ref.at[:,pl.ds(GW,DV)],wout_ref,save_sems.at[1])]
    @pl.when(i==0)
    def _():
        copies=[]
        for j,(block,first,width) in enumerate(cuts):
            for z in range(4):
                rows=pl.ds(pl.multiple_of(at_ref[block]*128+at_ref[8+z]*32,32),32)
                copies.append(pltpu.make_async_copy(pieces[j].at[pl.ds(32*z,32)],w_ref.at[rows,pl.ds(first,width)],sems.at[j,z]))
        for c in copies: c.start()
        for c in copies: c.wait()
        for c in saves: c.start()
        gains_ref[...]=w_ref[:,CR:CR+128].astype(F32).T[16:24]
    @pl.when(i==pl.num_programs(0)-1)
    def _():
        for c in saves: c.wait()
    x=tok_ref[...].astype(F32)
    r=lax.rsqrt(jnp.mean(x*x,axis=-1,keepdims=True)+EPS)
    n_ref[...]=(x*r*gains_ref[0:1]).astype(BF)
    n=n_ref[...]
    rank=nn(n,w_ref[:,CR:CR+128]).astype(BF)
    rank_ref[...]=rank
    dp=nn(rank,wdec_ref[...])+bias_ref[...]
    dp_ref[...]=dp
    q_ref[...]=nn(n_ref[...],w_ref[:,CQ:CQ+DK])*SCALE
    k_ref[...]=nn(n_ref[...],w_ref[:,CK:CK+DK])
    dhi,dlo=split(softminus(dp)*(1.0/16.0))
    lowb=low.astype(BF)
    cum=nn(lowb,dhi)+nn(lowb,dlo)
    cum_ref[...]=cum
    heads=range(H)
    sa=[slice(HK*h,HK*h+HK) for h in heads]; sv=[slice(HV*h,HV*h+HV) for h in heads]
    blocks=[slice(BL*b,BL*b+BL) for b in range(nb)]
    for h in heads: v_ref[:,sv[h]]=nn(n_ref[...],w_ref[:,CV+HV*h:CV+HV*h+HV]).astype(BF)
    interf=inter.astype(F32)
    ends=[cum[BL*b+BL-1:BL*b+BL,:] for b in range(nb)]
    endb=jnp.concatenate([jnp.broadcast_to(e,(BL,DK)) for e in ends],axis=0)
    keeps=jnp.concatenate([jnp.exp(ends[b])*keep_of(base+BL*b,starts) for b in range(nb)]+[jnp.zeros((8-nb,DK),F32)],axis=0)
    qgi=[None]*H; kc=[None]*H; s=[None]*H
    for h in heads:
        a=sa[h]; c=cum[:,a]
        qf=q_ref[:,a]*jnp.exp(c); kf=k_ref[:,a]
        qgi[h]=(qf*interf).astype(BF)
        kc[h]=(kf*jnp.exp(endb[:,a]-c)).astype(BF)
        s[h]=jnp.where(intra,nt(qf.astype(BF),(kf*jnp.exp(-c)).astype(BF)),0.0).astype(BF)
    for h in heads: gp_ref[:,sv[h]]=nn(n_ref[...],w_ref[:,CG+HV*h:CG+HV*h+HV]).astype(BF)
    vk=[jnp.where(reach,v_ref[:,sv[h]],jnp.zeros((T,HV),BF)) for h in heads]
    upd=[[tn(kc[h][t],vk[h][t]) for t in blocks] for h in heads]
    kt=[keeps[:,sa[h]].T for h in heads]
    cur=[state[h] for h in heads]
    parts=[[None]*nb for h in heads]
    for b in range(nb):
        for h in heads:
            sb=cur[h].astype(BF)
            bef_ref[b,h]=sb
            parts[h][b]=nn(qgi[h][blocks[b]],sb)
            cur[h]=cur[h]*kt[h][:,b:b+1]+upd[h][b]
    for h in heads: state[h]=cur[h]
    for h in heads:
        c=sv[h]
        o=nn(s[h],v_ref[:,c])+jnp.concatenate(parts[h],axis=0)
        o_ref[:,c]=o
        sc=lax.rsqrt(jnp.maximum(jnp.mean(o*o,axis=-1,keepdims=True),1.0))
        gp=gp_ref[:,c].astype(F32)
        mix_ref[:,c]=(o*sc*hg_ref[...]*(gp*sigmoid(gp))).astype(BF)


def fwd_call(st,at,tok,pieces,wdec,bias,hg,T=256):
    n,d=tok.shape; NT=LEN//T; sd=jax.ShapeDtypeStruct
    row=lambda x: pl.BlockSpec((T,x),lambda i,*s:(i,0))
    const=lambda a: pl.BlockSpec(a.shape,lambda i,*s:(0,0),pipeline_mode=pl.Buffered(1))
    hbm=pl.BlockSpec(memory_space=pl.ANY)
    nb=T//BL
    outs=[(d,BF),(DK,F32),(DK,F32),(DK,F32),(DK,F32),(DV,BF),(DV,BF),(DV,F32),None,(DV,BF),(128,BF)]
    specs=[row(o[0]) if o else pl.BlockSpec((nb,H,HK,HV),lambda i,*s:(i,0,0,0)) for o in outs]
    shapes=[sd((n,o[0]),o[1]) if o else sd((n//BL,H,HK,HV),BF) for o in outs]
    cuts=[(p[1],p[2],p[0].shape[1]) for p in pieces]
    return pl.pallas_call(functools.partial(fwd_kernel,NT,cuts),
        grid_spec=pltpu.PrefetchScalarGridSpec(num_scalar_prefetch=2,grid=(n//T,),
            in_specs=[row(d),const(wdec),const(bias),const(hg)]+[hbm]*len(pieces),out_specs=specs+[pl.BlockSpec((8,d),lambda i,*s:(0,0)),hbm,hbm],
            scratch_shapes=[pltpu.VMEM((H,HK,HV),F32),pltpu.VMEM((d,GW+DV),BF),pltpu.SemaphoreType.DMA((len(pieces),4)),pltpu.SemaphoreType.DMA((2,))]),
        out_shape=shapes+[sd((8,d),F32),sd((d,GW),BF),sd((d,DV),BF)],name="mixer_fwd",**params())(st,at,tok,wdec,bias,hg,*[p[0] for p in pieces])


def bwd_kernel(NT,seq,st_ref,gmix_ref,w_ref,wdec_ref,hg_ref,q_ref,k_ref,cum_ref,dp_ref,v_ref,gp_ref,o_ref,bef_ref,rank_ref,*rest):
    g_ref,dwd_ref,db_ref,dhg_ref,state=rest[-5:]
    T=q_ref.shape[0]; nb=T//BL
    step=pl.program_id(0); tile=NT-1-step; base=tile*T
    starts=starts_of(st_ref,seq)
    inter,reach,same,low,intra=tile_masks(base,T,starts)
    @pl.when(tile==NT-1)
    def _(): state[...]=jnp.zeros_like(state)
    @pl.when(step==0)
    def _():
        dwd_ref[...]=jnp.zeros_like(dwd_ref); db_ref[...]=jnp.zeros_like(db_ref); dhg_ref[...]=jnp.zeros_like(dhg_ref)
    cum=cum_ref[...]
    ends=[cum[BL*b+BL-1:BL*b+BL,:] for b in range(nb)]
    endb=jnp.concatenate([jnp.broadcast_to(e,(BL,DK)) for e in ends],axis=0)
    eg=jnp.exp(cum); es=jnp.exp(-cum); ec=jnp.exp(endb-cum)
    kend=jnp.concatenate([jnp.exp(ends[b])*keep_of(base+BL*b,starts) for b in range(nb)]+[jnp.zeros((8-nb,DK),F32)],axis=0)
    interb=inter.astype(F32).astype(BF); reachf=reach.astype(F32)
    tc=lax.broadcasted_iota(jnp.int32,(T,1),0); tr=lax.broadcasted_iota(jnp.int32,(1,T),1)
    upb=(same&(tc<=tr)).astype(BF); lsb=(same&(tc>tr)).astype(BF)
    hg=hg_ref[...]
    ones=jnp.ones((8,HV),BF)
    heads=range(H)
    sa=[slice(HK*h,HK*h+HK) for h in heads]; sc_=[slice(HV*h,HV*h+HV) for h in heads]
    go=[None]*H; goi=[None]*H
    qs=[q_ref[:,sa[h]]*eg[:,sa[h]] for h in heads]; ks=[k_ref[:,sa[h]]*es[:,sa[h]] for h in heads]; kd=[k_ref[:,sa[h]]*ec[:,sa[h]] for h in heads]
    qg=[x.astype(BF) for x in qs]; kg=[x.astype(BF) for x in ks]; kc=[x.astype(BF) for x in kd]
    sco=[jnp.where(intra,nt(qg[h],kg[h]),0.0).astype(BF) for h in heads]
    for h in heads:
        c=sc_[h]
        gi=nn(gmix_ref[...],w_ref[:,c])
        o=o_ref[:,c]; gp=gp_ref[:,c].astype(F32)
        ms=jnp.mean(o*o,axis=-1,keepdims=True)
        sc=lax.rsqrt(jnp.maximum(ms,1.0))
        hn0=o*sc
        s=sigmoid(gp); si=gp*s
        g_ref[:,CG+HV*h:CG+HV*h+HV]=(gi*hn0*hg*(s+si*(1.0-s))).astype(BF)
        G=gi*si
        dhg_ref[...]+=jnp.sum((G*hn0).reshape(-1,8,HV),axis=0)
        G=G*hg
        innr=jnp.mean(G*o,axis=-1,keepdims=True)*jnp.where(ms>1.0,1.0,0.0)
        go[h]=(sc*G-o*(sc*sc*sc*innr)).astype(BF)
        goi[h]=go[h]*interb
    gs=[jnp.where(intra,nt(go[h],v_ref[:,sc_[h]]),0.0).astype(BF) for h in heads]
    loc=[[tn(qg[h][BL*b:BL*b+BL],goi[h][BL*b:BL*b+BL]) for b in range(nb)] for h in heads]
    kt=[kend[:,sa[h]].T for h in heads]
    sbs=[[None]*nb for h in heads]
    p_end=[[None]*nb for h in heads]
    for b in reversed(range(nb)):
        for h in heads:
            st=state[h] if b==nb-1 else cur[h]
            sbs[h][b]=st.astype(BF)
            m1,m2=split(st*bef_ref[b,h].astype(F32))
            p_end[h][b]=(nt(ones,m1)+nt(ones,m2))[0:1]*kend[b:b+1,sa[h]]
            st=(loc[h][b]+kt[h][:,b:b+1]*st).astype(BF).astype(F32)
            if b==nb-1:
                if h==0: cur=[None]*H
            cur[h]=st
    for h in heads: state[h]=cur[h]
    cat=lambda p: jnp.concatenate(p,axis=0)
    for h in heads:
        a=sa[h]; c=sc_[h]; v=v_ref[:,c]
        tt=[slice(BL*b,BL*b+BL) for b in range(nb)]
        gv=tn(sco[h],go[h])+cat([nn(kc[h][tt[b]],sbs[h][b]) for b in range(nb)])*reachf
        g_ref[:,CV+HV*h:CV+HV*h+HV]=gv.astype(BF)
        gq=nn(gs[h],kg[h])+cat([nt(goi[h][tt[b]],bef_ref[b,h]) for b in range(nb)])
        gk=tn(gs[h],qg[h])
        gkc=cat([nt(v[tt[b]],sbs[h][b]) for b in range(nb)])*reachf
        av1,av2=split(gq*qs[h]-gk*ks[h])
        c1,c2=split(gkc*kd[h])
        endr=cat([jnp.broadcast_to(p,(BL,HK)) for p in p_end[h]])
        gd=nn(upb,av1)+nn(upb,av2)+nn(lsb,c1)+nn(lsb,c2)+endr
        g_ref[:,CQ+HK*h:CQ+HK*h+HK]=(gq*eg[:,a]*SCALE).astype(BF)
        g_ref[:,CK+HK*h:CK+HK*h+HK]=(gk*es[:,a]+gkc*ec[:,a]).astype(BF)
        dp=dp_ref[:,a]
        gpre=(gd*(1.0/16.0)*(1.0/(1.0+jnp.exp(dp)))).astype(BF)
        db_ref[:,a]+=jnp.sum(gpre.astype(F32).reshape(-1,8,HK),axis=0)
        dwd_ref[:,a]+=tn(rank_ref[...],gpre)
        gr=nt(gpre,wdec_ref[:,a])
        grank=gr if h==0 else grank+gr
    g_ref[:,CR:CR+128]=grank.astype(BF)
    g_ref[:,GW:]=jnp.zeros((T,128),BF)


def bwd_call(seq,before_g,deps,st,gmix,w,wdec,hg,q,k,cum,dp,v,gp,o,bef,rank,T=256):
    n,d=gmix.shape; NT=LEN//T; sd=jax.ShapeDtypeStruct; top=seq*NT+NT-1
    row=lambda a: pl.BlockSpec((T,a.shape[1]),lambda i,s:(top-i,0))
    const=lambda a: pl.BlockSpec(a.shape,lambda i,s:(0,0),pipeline_mode=pl.Buffered(1))
    hbm=pl.BlockSpec(memory_space=pl.ANY)
    nb=T//BL
    acc=lambda s: pl.BlockSpec(s,lambda i,_:(0,0))
    more=list(deps)+([before_g] if before_g is not None else [])
    return pl.pallas_call(functools.partial(bwd_kernel,NT,seq),
        grid_spec=pltpu.PrefetchScalarGridSpec(num_scalar_prefetch=1,grid=(NT,),
            in_specs=[row(gmix),const(w),const(wdec),const(hg),row(q),row(k),row(cum),row(dp),row(v),row(gp),row(o),pl.BlockSpec((nb,H,HK,HV),lambda i,s:(top-i,0,0,0)),row(rank)]+[hbm]*len(more),
            out_specs=[pl.BlockSpec((T,GW+128),lambda i,s:(top-i,0)),acc((128,DK)),acc((8,DK)),acc((8,HV))],
            scratch_shapes=[pltpu.VMEM((H,HK,HV),F32)]),
        input_output_aliases={} if before_g is None else {13+len(more):0},
        out_shape=[sd((n,GW+128),BF),sd((128,DK),F32),sd((8,DK),F32),sd((8,HV),F32)],
        name="mixer_bwd",**params())(st,gmix,w,wdec,hg,q,k,cum,dp,v,gp,o,bef,rank,*more)


def dx_kernel(g_ref,w_ref,tok_ref,gain_ref,gres_ref,*rest):
    gt_ref=rest[-1]
    gm=nt(g_ref[:,:GW],w_ref[...])
    x=tok_ref[...].astype(F32)
    r=lax.rsqrt(jnp.mean(x*x,axis=-1,keepdims=True)+EPS)
    sc=gm*gain_ref[...]
    inner=jnp.mean(sc*x,axis=-1,keepdims=True)
    gt_ref[...]=gres_ref[...]+r*sc-x*(r*r*r*inner)


def dx_call(part,parts,begun,g,w,tok,gain,gres,deps,flops=1,T=256):
    n,d=tok.shape; sd=jax.ShapeDtypeStruct; steps=n//T//parts; first=part*steps
    row=lambda a: pl.BlockSpec((T,a.shape[1]),lambda i:(first+i,0))
    const=lambda a: pl.BlockSpec(a.shape,lambda i:(0,0),pipeline_mode=pl.Buffered(1))
    hbm=pl.BlockSpec(memory_space=pl.ANY)
    more=list(deps)+([] if begun is None else [begun])
    return pl.pallas_call(dx_kernel,grid=(steps,),in_specs=[row(g),const(w),row(tok),const(gain),row(gres)]+[hbm]*len(more),
        out_specs=row(gres),out_shape=sd((n,d),F32),input_output_aliases={} if begun is None else {4+len(more):0},
        name="mixer_dx",**params(flops))(g,w,tok,gain,gres,*more)


def load_w(w_hbm,w_ref,sems,stacks):
    blocks,mlps,_,_=w_hbm.shape
    hid=w_ref.shape[1]//mlps
    copies=[pltpu.make_async_copy(w_hbm.at[r,m,pl.ds(s*hid,hid)],w_ref.at[i,pl.ds(m*hid,hid),pl.ds(r*128,128)],sems.at[i,r,m]) for i,s in enumerate(stacks) for m in range(mlps) for r in range(blocks)]
    for c in copies: c.start()
    for c in copies: c.wait()


def mlp_kernel(chunk,tok_ref,mix_ref,cot_ref,gain_ref,wo_ref,w_hbm,res_ref,n_ref,hid_ref,gg_ref,gu_ref,gres_ref,gmix_ref,gn_ref,w_ref,sems):
    @pl.when(pl.program_id(0)==0)
    def _(): load_w(w_hbm,w_ref,sems,(0,1,2))
    wg_ref,wu_ref,wd_ref=w_ref.at[0],w_ref.at[1],w_ref.at[2]
    res=tok_ref[...].astype(F32)+nt(mix_ref[...],wo_ref[...])
    res_ref[...]=res
    gain=gain_ref[...]
    r=lax.rsqrt(jnp.mean(res*res,axis=-1,keepdims=True)+EPS)
    n_ref[...]=(res*r*gain).astype(BF)
    ff=wg_ref.shape[0]
    for c in range(ff//chunk):
        sl=slice(c*chunk,(c+1)*chunk)
        n=n_ref[...]
        gp=nt(n,wg_ref[sl,:]); up=nt(n,wu_ref[sl,:]); gh=nt(cot_ref[...],wd_ref[sl,:])
        s=sigmoid(gp)
        si=gp*s
        hid_ref[:,sl]=(si*up).astype(BF)
        gu_ref[:,sl]=(gh*si).astype(BF)
        gg_ref[:,sl]=(gh*up*(s+si*(1.0-s))).astype(BF)
    gm=nn(gg_ref[...],wg_ref[...])+nn(gu_ref[...],wu_ref[...])
    res=res_ref[...]
    sc=gm*gain
    inner=jnp.mean(sc*res,axis=-1,keepdims=True)
    gi=r*sc-res*(r*r*r*inner)
    gres=cot_ref[...].astype(F32)+gi
    gres_ref[...]=gres
    gmix_ref[...]=gres.astype(BF)
    part=jnp.sum((gm*res*r).reshape(-1,8,gm.shape[1]),axis=0)
    @pl.when(pl.program_id(0)==0)
    def _(): gn_ref[...]=part
    @pl.when(pl.program_id(0)>0)
    def _(): gn_ref[...]+=part


def mlp_call(tok,mix,cot,gain,wo,w,ff,T=256,chunk=256):
    n,d=tok.shape
    row=lambda w: pl.BlockSpec((T,w),lambda i:(i,0))
    const=lambda a: pl.BlockSpec(a.shape,lambda i:(0,0),pipeline_mode=pl.Buffered(1))
    sd=jax.ShapeDtypeStruct
    return pl.pallas_call(functools.partial(mlp_kernel,chunk),grid=(n//T,),
        in_specs=[row(d),row(d),row(d),const(gain),const(wo),pl.BlockSpec(memory_space=pl.ANY)],
        out_specs=[row(d),row(d),row(ff),row(ff),row(ff),row(d),row(d),pl.BlockSpec((8,d),lambda i:(0,0))],
        out_shape=[sd((n,d),F32),sd((n,d),BF),sd((n,ff),BF),sd((n,ff),BF),sd((n,ff),BF),sd((n,d),F32),sd((n,d),BF),sd((8,d),F32)],
        scratch_shapes=[pltpu.VMEM((3,ff,d),BF),pltpu.SemaphoreType.DMA((3,)+w.shape[:2])],
        name="mlp",**params())(tok,mix,cot,gain,wo,w)


def down_kernel(res_ref,hid_ref,w_hbm,*rest):
    o_ref,w_ref,sems=rest[-3:]
    @pl.when(pl.program_id(0)==0)
    def _(): load_w(w_hbm,w_ref,sems,(2,))
    o_ref[...]=(res_ref[...]+nn(hid_ref[...],w_ref[0])).astype(BF)


def down_call(part,parts,begun,res,hid,w,deps,T=256):
    n,d=res.shape; ff=hid.shape[1]; steps=n//T//parts; first=part*steps
    row=lambda w: pl.BlockSpec((T,w),lambda i:(first+i,0))
    hbm=pl.BlockSpec(memory_space=pl.ANY)
    more=list(deps)+([] if begun is None else [begun])
    return pl.pallas_call(down_kernel,grid=(steps,),in_specs=[row(d),row(ff),hbm]+[hbm]*len(more),out_specs=row(d),
        out_shape=jax.ShapeDtypeStruct((n,d),BF),input_output_aliases={} if begun is None else {2+len(more):0},
        scratch_shapes=[pltpu.VMEM((1,ff,d),BF),pltpu.SemaphoreType.DMA((1,)+w.shape[:2])],
        name="mlp_down",**params())(res,hid,w,*more)


def dw_kernel(count,wide,extra,sel_ref,*rest):
    g_refs=rest[:count]; x_hbm=rest[count]
    outs=rest[-2*count-2:-2]; xp,sems=rest[-2:]
    i=pl.program_id(0); steps=pl.num_programs(0)//count
    @pl.when(i==0)
    def _():
        copies=[]
        for p in range(2):
            for j in range(4):
                at=pl.multiple_of((2*j+(1-sel_ref[0] if p==0 else sel_ref[0]))*128,128)
                copies.append(pltpu.make_async_copy(x_hbm.at[:,pl.ds(at,128)],xp.at[:,pl.ds(512*p+128*j,128)],sems.at[p,j]))
        for c in copies: c.start()
        for c in copies: c.wait()
    for s in range(count):
        @pl.when(i//steps==s)
        def _():
            o=tn(g_refs[s][...],xp[...]) if wide else tn(xp[...],g_refs[s][...])
            for p in range(2):
                for j in range(4):
                    b=slice(512*p+128*j,512*p+128*j+128)
                    outs[2*s+p][j]=(o[:,b] if wide else o[b,:]).astype(BF)
    if extra:
        @pl.when(i==pl.num_programs(0)-1)
        def _():
            for p in range(2):
                for j in range(4): outs[p][j,:,-128:]=rest[count+1][...]


def dw_call(gs,x,sel,deps,chunk,wide=True,extra=None):
    n,ff=gs[0].shape
    d=x.shape[1]; steps=ff//chunk; count=len(gs)
    hbm=pl.BlockSpec(memory_space=pl.ANY)
    spot=lambda i,s: jnp.clip(i-s*steps,0,steps-1)
    def out(s):
        return pl.BlockSpec((4,chunk,128),lambda i,_:(0,spot(i,s),0)) if wide else pl.BlockSpec((4,128,chunk),lambda i,_:(0,0,spot(i,s)))
    more=[] if extra is None else [pl.BlockSpec((128,128),lambda i,_:(0,0))]
    def inp(s):
        return pl.BlockSpec((n,chunk),lambda i,_:(0,spot(i,s)))
    return pl.pallas_call(functools.partial(dw_kernel,count,wide,extra is not None),
        grid_spec=pltpu.PrefetchScalarGridSpec(num_scalar_prefetch=1,grid=(steps*count,),
            in_specs=[inp(s) for s in range(count)]+[hbm]+more+[hbm]*len(deps),
            out_specs=[out(s) for s in range(count) for _ in range(2)],
            scratch_shapes=[pltpu.VMEM((n,d),BF),pltpu.SemaphoreType.DMA((2,4))]),
        out_shape=[jax.ShapeDtypeStruct((4,ff,128) if wide else (4,128,ff),BF)]*(2*count),
        name="grad_w",**params(10**11 if wide else 1))(sel,*gs,x,*([] if extra is None else [extra]),*deps)


def plane_kernel(count,at_ref,*rest):
    ins,outs=rest[:2*count],rest[-4:]
    for j in range(4):
        row=0
        for t in range(count):
            keep,came=ins[2*t],ins[2*t+1]
            rows=keep.shape[1]
            outs[j][0,row:row+rows]=keep[at_ref[j]]+came[at_ref[j]]
            row+=rows


def plane_call(pairs,at,deps,steps=8):
    each=[p[0].shape[1]//steps for p in pairs]
    return pl.pallas_call(functools.partial(plane_kernel,len(pairs)),
        grid_spec=pltpu.PrefetchScalarGridSpec(num_scalar_prefetch=1,grid=(steps,),
            in_specs=[pl.BlockSpec((4,r,128),lambda i,_:(0,i,0)) for r in each for _ in range(2)]+[pl.BlockSpec(memory_space=pl.ANY)]*len(deps),
            out_specs=[pl.BlockSpec((1,sum(each),128),lambda i,_:(i,0,0))]*4),
        out_shape=[jax.ShapeDtypeStruct((steps,sum(each),128),BF)]*4,name="plane",**params())(at,*[x for p in pairs for x in p],*deps)


def line_kernel(*refs):
    ins=refs[:4]
    out,scr,turned=refs[-3:]
    steps,rows,_=ins[0].shape
    main=rows-128
    for i in range(steps):
        v=functools.reduce(jnp.add,[x[i].astype(F32) for x in ins])
        scr[i]=v[:main].astype(BF)
        turned[i]=v[main:].T.astype(BF)
    each=steps//4; size=each*main+32*steps
    for k in range(4):
        for e in range(each):
            out[k*size+e*main:k*size+(e+1)*main]=scr[k*each+e]
        for i in range(steps):
            at=k*size+each*main+32*i
            out[at:at+32]=turned[i,32*k:32*k+32]


def line_call(parts,deps):
    steps,rows,_=parts[0].shape
    shape=(4*(steps//4*(rows-128)+steps*32),128)
    full=pl.BlockSpec(parts[0].shape,lambda i:(0,0,0))
    return pl.pallas_call(line_kernel,grid=(1,),
        in_specs=[full]*4+[pl.BlockSpec(memory_space=pl.ANY)]*len(deps),out_specs=pl.BlockSpec(shape,lambda i:(0,0)),
        scratch_shapes=[pltpu.VMEM((steps,rows-128,128),BF),pltpu.VMEM((steps,128,128),BF)],
        out_shape=jax.ShapeDtypeStruct(shape,BF),name="line",**params())(*parts,*deps)


def stack_kernel(*refs):
    out=refs[-1]
    v=functools.reduce(jnp.add,[r[...].astype(F32) for r in refs[:4]]).astype(BF)
    out[:,:GW]=v[:,:GW]
    for m in range(4):
        for j in range(4): out[32*m:32*m+32,GW+128*j:GW+128*j+128]=v[32*j:32*j+32,GW:]


def stack_call(parts,deps):
    shape=(128,GW+512)
    spec=pl.BlockSpec(parts[0].shape,lambda i:(0,0))
    return pl.pallas_call(stack_kernel,grid=(1,),
        in_specs=[spec]*4+[pl.BlockSpec(memory_space=pl.ANY)]*len(deps),out_specs=pl.BlockSpec(shape,lambda i:(0,0)),
        out_shape=jax.ShapeDtypeStruct(shape,BF),name="stack",**params())(*parts,*deps)


def spread_kernel(sizes,count,at_ref,*rest):
    outs=rest[-count:]
    for j in range(count):
        first=k=0
        for stacks,parts in sizes:
            for t in range(stacks):
                v=rest[k][t,at_ref[j]].astype(F32)
                for p in range(1,parts): v=v+rest[k+p][t,at_ref[j]].astype(F32)
                outs[j][first+t]=v.astype(BF)
            first+=stacks; k+=parts


def spread(groups,at,axis,chunk,deps):
    _,count,rows,cols=groups[0][0].shape
    size=[rows,cols]; size[axis]=chunk
    place=(lambda i: (i,0)) if axis==0 else (lambda i: (0,i))
    stacks=sum(g[0].shape[0] for g in groups)
    return pl.pallas_call(functools.partial(spread_kernel,[(g[0].shape[0],len(g)) for g in groups],count),
        grid_spec=pltpu.PrefetchScalarGridSpec(num_scalar_prefetch=1,grid=((rows,cols)[axis]//chunk,),
            in_specs=[pl.BlockSpec((g[0].shape[0],count,*size),lambda i,_:(0,0,*place(i))) for g in groups for p in g]+[pl.BlockSpec(memory_space=pl.ANY)]*len(deps),
            out_specs=[pl.BlockSpec((stacks,*size),lambda i,_:(0,*place(i)))]*count),
        out_shape=[jax.ShapeDtypeStruct((stacks,rows,cols),BF)]*count,name="spread",**params())(at,*[p for g in groups for p in g],*deps)


def swap(x, axis, bit, count):
    return lax.ppermute(x, axis, [(i, i ^ (1 << bit)) for i in range(count)])


def bit_of(axis, bit):
    return (lax.axis_index(axis) >> bit) & 1


def halve(x, dim, bit, count):
    place = bit_of("rows", bit)
    send = lax.dynamic_index_in_dim(x, 1 - place, dim, keepdims=False)
    keep = lax.dynamic_index_in_dim(x, place, dim, keepdims=False)
    return keep.astype(F32) + swap(send.astype(BF), "rows", bit, count).astype(F32)


def total(parts):
    return functools.reduce(jnp.add, [p.astype(F32) for p in parts])


def send_blocks(blocks, low, count):
    return [blocks[0]] + [
        lax.ppermute(blocks[j], "rows", [(i, i ^ (j << (low + 1))) for i in range(count)]) for j in range(1, 4)
    ]


def send_line(blocks, count):
    return [blocks[0]] + [
        lax.ppermute(blocks[j], "mlp", [(i, (i + j) % count) for i in range(count)]) for j in range(1, count)
    ]


def gather_pieces(x, low, mlps):
    half = x.shape[1] // 256 * 128
    line = [x] + [lax.ppermute(x, "mlp", [(i, (i + step) % mlps) for i in range(mlps)]) for step in range(1, mlps)]
    pieces = []
    for first, cols, bits in ((0, slice(0, half), (1, 2)), (half, slice(half, None), (2, 1))):
        held = [(jnp.concatenate([p[:, cols] for p in line], axis=0), 0)]
        for bit in bits + (0,):
            held = held + [(swap(p, "rows", bit, 8), at ^ (1 << bit)) for p, at in held]
        pieces += [(p, at, first) for p, at in held]
    return pieces


def body(
    tokens,
    doc_lengths,
    cotangent,
    norm_gain_mix,
    w_query,
    w_key,
    w_value,
    w_outgate,
    w_rank,
    w_decay,
    decay_bias,
    head_gain,
    w_output,
    norm_gain_mlp,
    w_gate,
    w_up,
    w_down,
):
    rows = lax.axis_size("rows")
    mlps = lax.axis_size("mlp")
    low = rows.bit_length() - 4
    shard = w_query.shape[0]
    hid, wide = w_down.shape
    lens = doc_lengths.reshape(-1)
    mixer_local = jnp.concatenate(
        [
            w_query, w_key, w_value, w_outgate, w_rank,
            norm_gain_mix[:, None], norm_gain_mlp[:, None], jnp.zeros((shard, 110), BF), w_output.T,
        ],
        axis=1,
    )
    mlp_local = jnp.concatenate([w_gate.T, w_up.T, w_down], axis=0)
    here = lax.axis_index("rows")
    if low == 0:
        mlp_all = lax.all_gather(mlp_local, ("rows", "mlp"), axis=0).reshape(rows, mlps, 3 * hid, 128)
        pieces = gather_pieces(mixer_local, low, mlps)
        at = jnp.concatenate([jnp.arange(8) ^ here, (lax.axis_index("mlp") - jnp.arange(mlps)) % mlps])
    else:
        mlp_all = lax.all_gather(mlp_local, ("rows", "mlp"), axis=0)
        mlp_all = mlp_all.reshape(8, rows // 8, mlps, 3 * hid, wide).transpose(0, 2, 3, 1, 4)
        mlp_all = mlp_all.reshape(8, mlps, 3 * hid, 128)
        whole = lax.all_gather(mixer_local, ("rows", "mlp"), axis=0, tiled=True)
        pieces = [(whole[128 * b : 128 * b + 128], b, 0) for b in range(8)]
        at = jnp.concatenate([jnp.arange(8), jnp.arange(4)])
    decay_wide = jnp.concatenate([w_decay, jnp.zeros((112, DK), BF)], axis=0)
    head_row = head_gain.astype(F32)[None]
    normed_in, q, k, cum, dp, v, gp, o, before, mixed, rank, gains, w_in, w_out = fwd_call(
        lens, at.astype(jnp.int32), tokens, pieces, decay_wide, decay_bias.astype(F32)[None], head_row
    )
    gain_mix, gain_mlp = gains[:1], gains[1:2]
    residual, normed_mid, hidden, grad_gate, grad_up, grad_res, grad_mixed, gain_mlp_part = mlp_call(
        tokens, mixed, cotangent, gain_mlp, w_out, mlp_all, mlps * hid
    )
    mine = bit_of("rows", low).astype(jnp.int32)[None]

    def with_other_core(send, keep):
        return [keep, swap(send, "rows", low, rows)]

    def within(parts, dim):
        if not low:
            return parts
        x = total(parts)
        x = x.reshape(x.shape[:dim] + (2,) * low + (x.shape[dim] >> low,) + x.shape[dim + 1 :])
        for bit in reversed(range(low)):
            x = halve(x, dim, bit, rows)
        return [x.astype(BF)]

    in_plane = ((here >> (low + 1)) ^ jnp.arange(4)).astype(jnp.int32)
    in_line = ((lax.axis_index("mlp") + jnp.arange(mlps)) % mlps).astype(jnp.int32)
    down_send, down_keep = dw_call([hidden], cotangent, mine, [normed_mid], 1408)
    down = with_other_core(down_send, down_keep)
    gate_send, gate_keep, up_send, up_keep = dw_call([grad_gate, grad_up], normed_mid, mine, [down_keep], 1408)
    gate = with_other_core(gate_send, gate_keep)
    up = with_other_core(up_send, up_keep)
    out_send, out_keep = dw_call([mixed], grad_mixed, mine, [gate_keep, down[1]], 512)
    out = with_other_core(out_send, out_keep)
    blocks = plane_call([gate, up, down, out], in_plane, [])
    common = (lens, grad_mixed, w_out, decay_wide, head_row, q, k, cum, dp, v, gp, o, before, rank)
    grads, small, deps = None, None, list(blocks)
    for seq in reversed(range(doc_lengths.shape[0])):
        grads, *sums = bwd_call(seq, grads, deps, *common)
        small = sums if small is None else [a + b for a, b in zip(small, sums)]
        deps = []
    small = jnp.concatenate(
        [small[0][:16].reshape(-1), small[1].sum(0), small[2].sum(0), gain_mlp_part.sum(0)]
    )
    count = small.shape[0]
    if low:
        small_sum = lax.all_gather(small.reshape(-1, 256), ("rows", "mlp"), axis=0).sum(0).reshape(-1)
    small = jnp.concatenate([small, jnp.zeros((128 * 128 - count,), F32)]).reshape(128, 128).astype(BF)
    in_send, in_keep = dw_call([grads], normed_in, mine, [], 1664, wide=False, extra=small)
    inner = with_other_core(in_send, in_keep)
    grad_tokens = dx_call(0, 2, None, grads, w_in, tokens, gain_mix, grad_res, [in_keep], 5 * 10**10)
    inner = spread([[p[None] for p in inner]], in_plane, 1, 1664, [grad_tokens])
    blocks = send_blocks(blocks, low, rows)
    if low:
        blocks = total(blocks)
        main = blocks[:, :-128].reshape(8, 3, -1, 128).transpose(1, 0, 2, 3).reshape(3, mlps, hid, 128)
        main = within([main], 3)[0]
        out = within([blocks[:, -128:].reshape(-1, 128)], 1)[0].reshape(DV, mlps, shard)
        main = send_line([jnp.take(main, in_line[j], axis=1) for j in range(mlps)], mlps)
        out = send_line([jnp.take(out, in_line[j], axis=1) for j in range(mlps)], mlps)
        deps = list(inner)
    else:
        blocks = line_call(blocks, list(inner))
        main = lax.psum_scatter(blocks, "mlp", scatter_dimension=0, tiled=True)
        deps = [blocks]
    blocks = inner
    grad_tokens = dx_call(1, 2, grad_tokens, grads, w_in, tokens, gain_mix, grad_res, deps)
    block_out = down_call(0, 2, None, residual, hidden, mlp_all, [grad_tokens])
    blocks = within(send_blocks(blocks, low, rows), 1)
    if low:
        blocks = total([b[0] for b in blocks]).astype(BF).reshape(mlps, shard, GW + 128)
    else:
        blocks = stack_call([b[0] for b in blocks], [block_out]).reshape(mlps, shard, GW + 512)
    in_grads = lax.all_to_all(blocks, "mlp", 0, 0, tiled=True)
    block_out = down_call(1, 2, block_out, residual, hidden, mlp_all, [blocks])
    in_grads = total([in_grads[j] for j in range(mlps)])
    if low:
        small = small_sum
    else:
        small = in_grads[:, GW:].reshape(shard, 4, 128).transpose(1, 0, 2).reshape(-1)[:count]
    in_grads = in_grads[:, :GW]
    if low:
        mlp_grads, out_grads = total(main), total(out)
    else:
        main = main.astype(F32)
        mlp_grads = main[: 3 * hid].reshape(2, 3, hid // 2, 128).transpose(1, 0, 2, 3).reshape(3, hid, 128)
        out_grads = main[3 * hid :].reshape(8, shard, 128).transpose(0, 2, 1).reshape(DV, shard)
    gain_mix_grad = jnp.sum(in_grads * mixer_local[:, :GW].astype(F32), axis=1) / norm_gain_mix.astype(F32)
    at = 16 * DK + DK + HV + (here * mlps + lax.axis_index("mlp")) * shard
    return (
        block_out,
        grad_tokens,
        gain_mix_grad,
        in_grads[:, CQ : CQ + DK],
        in_grads[:, CK : CK + DK],
        in_grads[:, CV : CV + DV],
        in_grads[:, CG : CG + DV],
        in_grads[:, CR : CR + 16],
        small[: 16 * DK].reshape(16, DK),
        small[16 * DK : 17 * DK],
        small[17 * DK : 17 * DK + HV],
        out_grads,
        lax.dynamic_slice_in_dim(small, at, shard),
        mlp_grads[0].T,
        mlp_grads[1].T,
        mlp_grads[2],
    )


def solution(mesh):
    in_specs = (
        P(("rows", "mlp"), None),
        P(("rows", "mlp"), None),
        P(("rows", "mlp"), None),
        P(("rows", "mlp")),
        P(("rows", "mlp"), None),
        P(("rows", "mlp"), None),
        P(("rows", "mlp"), None),
        P(("rows", "mlp"), None),
        P(("rows", "mlp"), None),
        P(),
        P(),
        P(),
        P(None, ("rows", "mlp")),
        P(("rows", "mlp")),
        P("rows", "mlp"),
        P("rows", "mlp"),
        P("mlp", "rows"),
    )
    out_specs = (
        P(("rows", "mlp"), None),
        P(("rows", "mlp"), None),
        P(("rows", "mlp")),
        P(("rows", "mlp"), None),
        P(("rows", "mlp"), None),
        P(("rows", "mlp"), None),
        P(("rows", "mlp"), None),
        P(("rows", "mlp"), None),
        P(),
        P(),
        P(),
        P(None, ("rows", "mlp")),
        P(("rows", "mlp")),
        P("rows", "mlp"),
        P("rows", "mlp"),
        P("mlp", "rows"),
    )
    return jax.shard_map(body, mesh=mesh, in_specs=in_specs, out_specs=out_specs, check_vma=False)
```

```python
import functools

import jax
import jax.numpy as jnp
from jax import lax
from jax.experimental import pallas as pl
from jax.experimental.pallas import tpu as pltpu
from jax.sharding import PartitionSpec as P

F32 = jnp.float32
BF = jnp.bfloat16
EPS = 1e-5
LEN = 1024
BL = 64
H = 4
HK = 128
HV = 256
DK = 512
DV = 1024
CQ, CK, CV, CG, CR, CO = 0, 512, 1024, 2048, 3072, 3200
GW = 3200
SCALE = HK**-0.5
VMEM = 60 * 1024 * 1024


def nn(a,b): return lax.dot_general(a,b,(((1,),(0,)),((),())),preferred_element_type=F32)


def nt(a,b): return lax.dot_general(a,b,(((1,),(1,)),((),())),preferred_element_type=F32)


def tn(a,b): return lax.dot_general(a,b,(((0,),(0,)),((),())),preferred_element_type=F32)


def sigmoid(v): return 1.0/(1.0+jnp.exp(-v))


def softminus(x): return jnp.minimum(x,0.0)-jnp.log1p(jnp.exp(-jnp.abs(x)))


def split(x):
    hi=x.astype(BF); return hi,(x-hi.astype(F32)).astype(BF)


def doc_of(p,starts):
    out=(p>=starts[0]).astype(jnp.int32)
    for s in starts[1:]: out=out+(p>=s).astype(jnp.int32)
    return out


def tile_masks(base,T,starts):
    tc=lax.broadcasted_iota(jnp.int32,(T,1),0); tr=lax.broadcasted_iota(jnp.int32,(1,T),1)
    dc=doc_of(tc+base,starts); dr=doc_of(tr+base,starts)
    first=(tc & ~(BL-1))+base
    prior=jnp.where(first>0,doc_of(first-1,starts),-1)
    last=doc_of(first+(BL-1),starts)
    inter=(dc==prior); reach=(dc==last)
    same=(tc>>6)==(tr>>6)
    low=same&(tc>=tr)
    return inter,reach,same,low,low&(dc==dr)


def keep_of(first,starts):
    return jnp.where(first>0,(doc_of(first-1,starts)==doc_of(first+BL-1,starts)).astype(F32),0.0)


def starts_of(len_ref, seq):
    first = len_ref[seq * 4]
    second = first + len_ref[seq * 4 + 1]
    return [first, second, second + len_ref[seq * 4 + 2]]


def params(flops=1):
    return dict(
        compiler_params=pltpu.CompilerParams(vmem_limit_bytes=VMEM),
        cost_estimate=pl.CostEstimate(flops=flops, bytes_accessed=1, transcendentals=0),
    )


def fwd_kernel(NT,cuts,st_ref,at_ref,tok_ref,wdec_ref,bias_ref,hg_ref,*rest):
    pieces=rest[:len(cuts)]
    n_ref,q_ref,k_ref,cum_ref,dp_ref,v_ref,gp_ref,o_ref,bef_ref,mix_ref,rank_ref,gains_ref,win_ref,wout_ref,state,w_ref,sems,save_sems=rest[len(cuts):]
    T=tok_ref.shape[0]; nb=T//BL
    i=pl.program_id(0); seq=i//NT; tile=i%NT; base=tile*T
    starts=starts_of(st_ref,seq)
    inter,reach,same,low,intra=tile_masks(base,T,starts)
    @pl.when(tile==0)
    def _(): state[...]=jnp.zeros_like(state)
    saves=[pltpu.make_async_copy(w_ref.at[:,pl.ds(0,GW)],win_ref,save_sems.at[0]),pltpu.make_async_copy(w_ref.at[:,pl.ds(GW,DV)],wout_ref,save_sems.at[1])]
    @pl.when(i==0)
    def _():
        copies=[]
        for j,(block,first,width) in enumerate(cuts):
            for z in range(4):
                rows=pl.ds(pl.multiple_of(at_ref[block]*128+at_ref[8+z]*32,32),32)
                copies.append(pltpu.make_async_copy(pieces[j].at[pl.ds(32*z,32)],w_ref.at[rows,pl.ds(first,width)],sems.at[j,z]))
        for c in copies: c.start()
        for c in copies: c.wait()
        for c in saves: c.start()
        gains_ref[...]=w_ref[:,CR:CR+128].astype(F32).T[16:24]
    @pl.when(i==pl.num_programs(0)-1)
    def _():
        for c in saves: c.wait()
    x=tok_ref[...].astype(F32)
    r=lax.rsqrt(jnp.mean(x*x,axis=-1,keepdims=True)+EPS)
    n_ref[...]=(x*r*gains_ref[0:1]).astype(BF)
    n=n_ref[...]
    rank=nn(n,w_ref[:,CR:CR+128]).astype(BF)
    rank_ref[...]=rank
    dp=nn(rank,wdec_ref[...])+bias_ref[...]
    dp_ref[...]=dp
    q_ref[...]=nn(n_ref[...],w_ref[:,CQ:CQ+DK])*SCALE
    k_ref[...]=nn(n_ref[...],w_ref[:,CK:CK+DK])
    dhi,dlo=split(softminus(dp)*(1.0/16.0))
    lowb=low.astype(BF)
    cum=nn(lowb,dhi)+nn(lowb,dlo)
    cum_ref[...]=cum
    heads=range(H)
    sa=[slice(HK*h,HK*h+HK) for h in heads]; sv=[slice(HV*h,HV*h+HV) for h in heads]
    blocks=[slice(BL*b,BL*b+BL) for b in range(nb)]
    for h in heads: v_ref[:,sv[h]]=nn(n_ref[...],w_ref[:,CV+HV*h:CV+HV*h+HV]).astype(BF)
    interf=inter.astype(F32)
    ends=[cum[BL*b+BL-1:BL*b+BL,:] for b in range(nb)]
    endb=jnp.concatenate([jnp.broadcast_to(e,(BL,DK)) for e in ends],axis=0)
    keeps=jnp.concatenate([jnp.exp(ends[b])*keep_of(base+BL*b,starts) for b in range(nb)]+[jnp.zeros((8-nb,DK),F32)],axis=0)
    qgi=[None]*H; kc=[None]*H; s=[None]*H
    for h in heads:
        a=sa[h]; c=cum[:,a]
        qf=q_ref[:,a]*jnp.exp(c); kf=k_ref[:,a]
        qgi[h]=(qf*interf).astype(BF)
        kc[h]=(kf*jnp.exp(endb[:,a]-c)).astype(BF)
        s[h]=jnp.where(intra,nt(qf.astype(BF),(kf*jnp.exp(-c)).astype(BF)),0.0).astype(BF)
    for h in heads: gp_ref[:,sv[h]]=nn(n_ref[...],w_ref[:,CG+HV*h:CG+HV*h+HV]).astype(BF)
    vk=[jnp.where(reach,v_ref[:,sv[h]],jnp.zeros((T,HV),BF)) for h in heads]
    upd=[[tn(kc[h][t],vk[h][t]) for t in blocks] for h in heads]
    kt=[keeps[:,sa[h]].T for h in heads]
    cur=[state[h] for h in heads]
    parts=[[None]*nb for h in heads]
    for b in range(nb):
        for h in heads:
            sb=cur[h].astype(BF)
            bef_ref[b,h]=sb
            parts[h][b]=nn(qgi[h][blocks[b]],sb)
            cur[h]=cur[h]*kt[h][:,b:b+1]+upd[h][b]
    for h in heads: state[h]=cur[h]
    for h in heads:
        c=sv[h]
        o=nn(s[h],v_ref[:,c])+jnp.concatenate(parts[h],axis=0)
        o_ref[:,c]=o
        sc=lax.rsqrt(jnp.maximum(jnp.mean(o*o,axis=-1,keepdims=True),1.0))
        gp=gp_ref[:,c].astype(F32)
        mix_ref[:,c]=(o*sc*hg_ref[...]*(gp*sigmoid(gp))).astype(BF)


def fwd_call(st,at,tok,pieces,wdec,bias,hg,T=256):
    n,d=tok.shape; NT=LEN//T; sd=jax.ShapeDtypeStruct
    row=lambda x: pl.BlockSpec((T,x),lambda i,*s:(i,0))
    const=lambda a: pl.BlockSpec(a.shape,lambda i,*s:(0,0),pipeline_mode=pl.Buffered(1))
    hbm=pl.BlockSpec(memory_space=pl.ANY)
    nb=T//BL
    outs=[(d,BF),(DK,F32),(DK,F32),(DK,F32),(DK,F32),(DV,BF),(DV,BF),(DV,F32),None,(DV,BF),(128,BF)]
    specs=[row(o[0]) if o else pl.BlockSpec((nb,H,HK,HV),lambda i,*s:(i,0,0,0)) for o in outs]
    shapes=[sd((n,o[0]),o[1]) if o else sd((n//BL,H,HK,HV),BF) for o in outs]
    cuts=[(p[1],p[2],p[0].shape[1]) for p in pieces]
    return pl.pallas_call(functools.partial(fwd_kernel,NT,cuts),
        grid_spec=pltpu.PrefetchScalarGridSpec(num_scalar_prefetch=2,grid=(n//T,),
            in_specs=[row(d),const(wdec),const(bias),const(hg)]+[hbm]*len(pieces),out_specs=specs+[pl.BlockSpec((8,d),lambda i,*s:(0,0)),hbm,hbm],
            scratch_shapes=[pltpu.VMEM((H,HK,HV),F32),pltpu.VMEM((d,GW+DV),BF),pltpu.SemaphoreType.DMA((len(pieces),4)),pltpu.SemaphoreType.DMA((2,))]),
        out_shape=shapes+[sd((8,d),F32),sd((d,GW),BF),sd((d,DV),BF)],name="mixer_fwd",**params())(st,at,tok,wdec,bias,hg,*[p[0] for p in pieces])


def bwd_kernel(NT,seq,st_ref,gmix_ref,w_ref,wdec_ref,hg_ref,q_ref,k_ref,cum_ref,dp_ref,v_ref,gp_ref,o_ref,bef_ref,rank_ref,*rest):
    g_ref,dwd_ref,db_ref,dhg_ref,state=rest[-5:]
    T=q_ref.shape[0]; nb=T//BL
    step=pl.program_id(0); tile=NT-1-step; base=tile*T
    starts=starts_of(st_ref,seq)
    inter,reach,same,low,intra=tile_masks(base,T,starts)
    @pl.when(tile==NT-1)
    def _(): state[...]=jnp.zeros_like(state)
    @pl.when(step==0)
    def _():
        dwd_ref[...]=jnp.zeros_like(dwd_ref); db_ref[...]=jnp.zeros_like(db_ref); dhg_ref[...]=jnp.zeros_like(dhg_ref)
    cum=cum_ref[...]
    ends=[cum[BL*b+BL-1:BL*b+BL,:] for b in range(nb)]
    endb=jnp.concatenate([jnp.broadcast_to(e,(BL,DK)) for e in ends],axis=0)
    eg=jnp.exp(cum); es=jnp.exp(-cum); ec=jnp.exp(endb-cum)
    kend=jnp.concatenate([jnp.exp(ends[b])*keep_of(base+BL*b,starts) for b in range(nb)]+[jnp.zeros((8-nb,DK),F32)],axis=0)
    interb=inter.astype(F32).astype(BF); reachf=reach.astype(F32)
    tc=lax.broadcasted_iota(jnp.int32,(T,1),0); tr=lax.broadcasted_iota(jnp.int32,(1,T),1)
    upb=(same&(tc<=tr)).astype(BF); lsb=(same&(tc>tr)).astype(BF)
    hg=hg_ref[...]
    ones=jnp.ones((8,HV),BF)
    heads=range(H)
    sa=[slice(HK*h,HK*h+HK) for h in heads]; sc_=[slice(HV*h,HV*h+HV) for h in heads]
    go=[None]*H; goi=[None]*H
    qs=[q_ref[:,sa[h]]*eg[:,sa[h]] for h in heads]; ks=[k_ref[:,sa[h]]*es[:,sa[h]] for h in heads]; kd=[k_ref[:,sa[h]]*ec[:,sa[h]] for h in heads]
    qg=[x.astype(BF) for x in qs]; kg=[x.astype(BF) for x in ks]; kc=[x.astype(BF) for x in kd]
    sco=[jnp.where(intra,nt(qg[h],kg[h]),0.0).astype(BF) for h in heads]
    for h in heads:
        c=sc_[h]
        gi=nn(gmix_ref[...],w_ref[:,c])
        o=o_ref[:,c]; gp=gp_ref[:,c].astype(F32)
        ms=jnp.mean(o*o,axis=-1,keepdims=True)
        sc=lax.rsqrt(jnp.maximum(ms,1.0))
        hn0=o*sc
        s=sigmoid(gp); si=gp*s
        g_ref[:,CG+HV*h:CG+HV*h+HV]=(gi*hn0*hg*(s+si*(1.0-s))).astype(BF)
        G=gi*si
        dhg_ref[...]+=jnp.sum((G*hn0).reshape(-1,8,HV),axis=0)
        G=G*hg
        innr=jnp.mean(G*o,axis=-1,keepdims=True)*jnp.where(ms>1.0,1.0,0.0)
        go[h]=(sc*G-o*(sc*sc*sc*innr)).astype(BF)
        goi[h]=go[h]*interb
    gs=[jnp.where(intra,nt(go[h],v_ref[:,sc_[h]]),0.0).astype(BF) for h in heads]
    loc=[[tn(qg[h][BL*b:BL*b+BL],goi[h][BL*b:BL*b+BL]) for b in range(nb)] for h in heads]
    kt=[kend[:,sa[h]].T for h in heads]
    sbs=[[None]*nb for h in heads]
    p_end=[[None]*nb for h in heads]
    for b in reversed(range(nb)):
        for h in heads:
            st=state[h] if b==nb-1 else cur[h]
            sbs[h][b]=st.astype(BF)
            m1,m2=split(st*bef_ref[b,h].astype(F32))
            p_end[h][b]=(nt(ones,m1)+nt(ones,m2))[0:1]*kend[b:b+1,sa[h]]
            st=(loc[h][b]+kt[h][:,b:b+1]*st).astype(BF).astype(F32)
            if b==nb-1:
                if h==0: cur=[None]*H
            cur[h]=st
    for h in heads: state[h]=cur[h]
    cat=lambda p: jnp.concatenate(p,axis=0)
    for h in heads:
        a=sa[h]; c=sc_[h]; v=v_ref[:,c]
        tt=[slice(BL*b,BL*b+BL) for b in range(nb)]
        gv=tn(sco[h],go[h])+cat([nn(kc[h][tt[b]],sbs[h][b]) for b in range(nb)])*reachf
        g_ref[:,CV+HV*h:CV+HV*h+HV]=gv.astype(BF)
        gq=nn(gs[h],kg[h])+cat([nt(goi[h][tt[b]],bef_ref[b,h]) for b in range(nb)])
        gk=tn(gs[h],qg[h])
        gkc=cat([nt(v[tt[b]],sbs[h][b]) for b in range(nb)])*reachf
        av1,av2=split(gq*qs[h]-gk*ks[h])
        c1,c2=split(gkc*kd[h])
        endr=cat([jnp.broadcast_to(p,(BL,HK)) for p in p_end[h]])
        gd=nn(upb,av1)+nn(upb,av2)+nn(lsb,c1)+nn(lsb,c2)+endr
        g_ref[:,CQ+HK*h:CQ+HK*h+HK]=(gq*eg[:,a]*SCALE).astype(BF)
        g_ref[:,CK+HK*h:CK+HK*h+HK]=(gk*es[:,a]+gkc*ec[:,a]).astype(BF)
        dp=dp_ref[:,a]
        gpre=(gd*(1.0/16.0)*(1.0/(1.0+jnp.exp(dp)))).astype(BF)
        db_ref[:,a]+=jnp.sum(gpre.astype(F32).reshape(-1,8,HK),axis=0)
        dwd_ref[:,a]+=tn(rank_ref[...],gpre)
        gr=nt(gpre,wdec_ref[:,a])
        grank=gr if h==0 else grank+gr
    g_ref[:,CR:CR+128]=grank.astype(BF)
    g_ref[:,GW:]=jnp.zeros((T,128),BF)


def bwd_call(seq,before_g,deps,st,gmix,w,wdec,hg,q,k,cum,dp,v,gp,o,bef,rank,T=256):
    n,d=gmix.shape; NT=LEN//T; sd=jax.ShapeDtypeStruct; top=seq*NT+NT-1
    row=lambda a: pl.BlockSpec((T,a.shape[1]),lambda i,s:(top-i,0))
    const=lambda a: pl.BlockSpec(a.shape,lambda i,s:(0,0),pipeline_mode=pl.Buffered(1))
    hbm=pl.BlockSpec(memory_space=pl.ANY)
    nb=T//BL
    acc=lambda s: pl.BlockSpec(s,lambda i,_:(0,0))
    more=list(deps)+([before_g] if before_g is not None else [])
    return pl.pallas_call(functools.partial(bwd_kernel,NT,seq),
        grid_spec=pltpu.PrefetchScalarGridSpec(num_scalar_prefetch=1,grid=(NT,),
            in_specs=[row(gmix),const(w),const(wdec),const(hg),row(q),row(k),row(cum),row(dp),row(v),row(gp),row(o),pl.BlockSpec((nb,H,HK,HV),lambda i,s:(top-i,0,0,0)),row(rank)]+[hbm]*len(more),
            out_specs=[pl.BlockSpec((T,GW+128),lambda i,s:(top-i,0)),acc((128,DK)),acc((8,DK)),acc((8,HV))],
            scratch_shapes=[pltpu.VMEM((H,HK,HV),F32)]),
        input_output_aliases={} if before_g is None else {13+len(more):0},
        out_shape=[sd((n,GW+128),BF),sd((128,DK),F32),sd((8,DK),F32),sd((8,HV),F32)],
        name="mixer_bwd",**params())(st,gmix,w,wdec,hg,q,k,cum,dp,v,gp,o,bef,rank,*more)


def dx_kernel(g_ref,w_ref,tok_ref,gain_ref,gres_ref,*rest):
    gt_ref=rest[-1]
    gm=nt(g_ref[:,:GW],w_ref[...])
    x=tok_ref[...].astype(F32)
    r=lax.rsqrt(jnp.mean(x*x,axis=-1,keepdims=True)+EPS)
    sc=gm*gain_ref[...]
    inner=jnp.mean(sc*x,axis=-1,keepdims=True)
    gt_ref[...]=gres_ref[...]+r*sc-x*(r*r*r*inner)


def dx_call(part,parts,begun,g,w,tok,gain,gres,deps,flops=1,T=256):
    n,d=tok.shape; sd=jax.ShapeDtypeStruct; steps=n//T//parts; first=part*steps
    row=lambda a: pl.BlockSpec((T,a.shape[1]),lambda i:(first+i,0))
    const=lambda a: pl.BlockSpec(a.shape,lambda i:(0,0),pipeline_mode=pl.Buffered(1))
    hbm=pl.BlockSpec(memory_space=pl.ANY)
    more=list(deps)+([] if begun is None else [begun])
    return pl.pallas_call(dx_kernel,grid=(steps,),in_specs=[row(g),const(w),row(tok),const(gain),row(gres)]+[hbm]*len(more),
        out_specs=row(gres),out_shape=sd((n,d),F32),input_output_aliases={} if begun is None else {4+len(more):0},
        name="mixer_dx",**params(flops))(g,w,tok,gain,gres,*more)


def load_w(w_hbm,w_ref,sems,stacks):
    blocks,mlps,_,_=w_hbm.shape
    hid=w_ref.shape[1]//mlps
    copies=[pltpu.make_async_copy(w_hbm.at[r,m,pl.ds(s*hid,hid)],w_ref.at[i,pl.ds(m*hid,hid),pl.ds(r*128,128)],sems.at[i,r,m]) for i,s in enumerate(stacks) for m in range(mlps) for r in range(blocks)]
    for c in copies: c.start()
    for c in copies: c.wait()


def mlp_kernel(chunk,tok_ref,mix_ref,cot_ref,gain_ref,wo_ref,w_hbm,res_ref,n_ref,hid_ref,gg_ref,gu_ref,gres_ref,gmix_ref,gn_ref,w_ref,sems):
    @pl.when(pl.program_id(0)==0)
    def _(): load_w(w_hbm,w_ref,sems,(0,1,2))
    wg_ref,wu_ref,wd_ref=w_ref.at[0],w_ref.at[1],w_ref.at[2]
    res=tok_ref[...].astype(F32)+nt(mix_ref[...],wo_ref[...])
    res_ref[...]=res
    gain=gain_ref[...]
    r=lax.rsqrt(jnp.mean(res*res,axis=-1,keepdims=True)+EPS)
    n_ref[...]=(res*r*gain).astype(BF)
    ff=wg_ref.shape[0]
    for c in range(ff//chunk):
        sl=slice(c*chunk,(c+1)*chunk)
        n=n_ref[...]
        gp=nt(n,wg_ref[sl,:]); up=nt(n,wu_ref[sl,:]); gh=nt(cot_ref[...],wd_ref[sl,:])
        s=sigmoid(gp)
        si=gp*s
        hid_ref[:,sl]=(si*up).astype(BF)
        gu_ref[:,sl]=(gh*si).astype(BF)
        gg_ref[:,sl]=(gh*up*(s+si*(1.0-s))).astype(BF)
    gm=nn(gg_ref[...],wg_ref[...])+nn(gu_ref[...],wu_ref[...])
    res=res_ref[...]
    sc=gm*gain
    inner=jnp.mean(sc*res,axis=-1,keepdims=True)
    gi=r*sc-res*(r*r*r*inner)
    gres=cot_ref[...].astype(F32)+gi
    gres_ref[...]=gres
    gmix_ref[...]=gres.astype(BF)
    part=jnp.sum((gm*res*r).reshape(-1,8,gm.shape[1]),axis=0)
    @pl.when(pl.program_id(0)==0)
    def _(): gn_ref[...]=part
    @pl.when(pl.program_id(0)>0)
    def _(): gn_ref[...]+=part


def mlp_call(tok,mix,cot,gain,wo,w,ff,T=256,chunk=256):
    n,d=tok.shape
    row=lambda w: pl.BlockSpec((T,w),lambda i:(i,0))
    const=lambda a: pl.BlockSpec(a.shape,lambda i:(0,0),pipeline_mode=pl.Buffered(1))
    sd=jax.ShapeDtypeStruct
    return pl.pallas_call(functools.partial(mlp_kernel,chunk),grid=(n//T,),
        in_specs=[row(d),row(d),row(d),const(gain),const(wo),pl.BlockSpec(memory_space=pl.ANY)],
        out_specs=[row(d),row(d),row(ff),row(ff),row(ff),row(d),row(d),pl.BlockSpec((8,d),lambda i:(0,0))],
        out_shape=[sd((n,d),F32),sd((n,d),BF),sd((n,ff),BF),sd((n,ff),BF),sd((n,ff),BF),sd((n,d),F32),sd((n,d),BF),sd((8,d),F32)],
        scratch_shapes=[pltpu.VMEM((3,ff,d),BF),pltpu.SemaphoreType.DMA((3,)+w.shape[:2])],
        name="mlp",**params())(tok,mix,cot,gain,wo,w)


def down_kernel(res_ref,hid_ref,w_hbm,*rest):
    o_ref,w_ref,sems=rest[-3:]
    @pl.when(pl.program_id(0)==0)
    def _(): load_w(w_hbm,w_ref,sems,(2,))
    o_ref[...]=(res_ref[...]+nn(hid_ref[...],w_ref[0])).astype(BF)


def down_call(part,parts,begun,res,hid,w,deps,T=256):
    n,d=res.shape; ff=hid.shape[1]; steps=n//T//parts; first=part*steps
    row=lambda w: pl.BlockSpec((T,w),lambda i:(first+i,0))
    hbm=pl.BlockSpec(memory_space=pl.ANY)
    more=list(deps)+([] if begun is None else [begun])
    return pl.pallas_call(down_kernel,grid=(steps,),in_specs=[row(d),row(ff),hbm]+[hbm]*len(more),out_specs=row(d),
        out_shape=jax.ShapeDtypeStruct((n,d),BF),input_output_aliases={} if begun is None else {2+len(more):0},
        scratch_shapes=[pltpu.VMEM((1,ff,d),BF),pltpu.SemaphoreType.DMA((1,)+w.shape[:2])],
        name="mlp_down",**params())(res,hid,w,*more)


def small_block(refs):
    *parts,gain=refs
    v=[functools.reduce(jnp.add,[p[...] for p in parts[t::3]]) for t in range(3)]+[gain[...]]
    rows=[v[0][:16,128*j:128*j+128] for j in range(4)]
    for x in v[1:]:
        x=jnp.sum(x,axis=0,keepdims=True)
        rows+=[x[:,128*j:128*j+128] for j in range(x.shape[1]//128)]
    rows.append(jnp.zeros((128-64-4-2-8,128),F32))
    return jnp.concatenate(rows,axis=0).astype(BF)


def dw_kernel(count,wide,extra,sel_ref,*rest):
    g_refs=rest[:count]; x_hbm=rest[count]
    outs=rest[-2*count-2:-2]; xp,sems=rest[-2:]
    i=pl.program_id(0); steps=pl.num_programs(0)//count
    @pl.when(i==0)
    def _():
        copies=[]
        for p in range(2):
            for j in range(4):
                at=pl.multiple_of((2*j+(1-sel_ref[0] if p==0 else sel_ref[0]))*128,128)
                copies.append(pltpu.make_async_copy(x_hbm.at[:,pl.ds(at,128)],xp.at[:,pl.ds(512*p+128*j,128)],sems.at[p,j]))
        for c in copies: c.start()
        for c in copies: c.wait()
    for s in range(count):
        @pl.when(i//steps==s)
        def _():
            o=tn(g_refs[s][...],xp[...]) if wide else tn(xp[...],g_refs[s][...])
            for p in range(2):
                for j in range(4):
                    b=slice(512*p+128*j,512*p+128*j+128)
                    outs[2*s+p][j]=(o[:,b] if wide else o[b,:]).astype(BF)
    if extra:
        @pl.when(i==pl.num_programs(0)-1)
        def _():
            for p in range(2):
                for j in range(4): outs[p][j,:,-128:]=small_block(rest[count+1:count+1+extra])


def dw_call(gs,x,sel,deps,chunk,wide=True,extra=()):
    n,ff=gs[0].shape
    d=x.shape[1]; steps=ff//chunk; count=len(gs)
    hbm=pl.BlockSpec(memory_space=pl.ANY)
    spot=lambda i,s: jnp.clip(i-s*steps,0,steps-1)
    def out(s):
        return pl.BlockSpec((4,chunk,128),lambda i,_:(0,spot(i,s),0)) if wide else pl.BlockSpec((4,128,chunk),lambda i,_:(0,0,spot(i,s)))
    more=[pl.BlockSpec(e.shape,lambda i,_:(0,0)) for e in extra]
    def inp(s):
        return pl.BlockSpec((n,chunk),lambda i,_:(0,spot(i,s)))
    return pl.pallas_call(functools.partial(dw_kernel,count,wide,len(extra)),
        grid_spec=pltpu.PrefetchScalarGridSpec(num_scalar_prefetch=1,grid=(steps*count,),
            in_specs=[inp(s) for s in range(count)]+[hbm]+more+[hbm]*len(deps),
            out_specs=[out(s) for s in range(count) for _ in range(2)],
            scratch_shapes=[pltpu.VMEM((n,d),BF),pltpu.SemaphoreType.DMA((2,4))]),
        out_shape=[jax.ShapeDtypeStruct((4,ff,128) if wide else (4,128,ff),BF)]*(2*count),
        name="grad_w",**params(10**11 if wide else 1))(sel,*gs,x,*extra,*deps)


def plane_kernel(count,at_ref,*rest):
    ins,outs=rest[:2*count],rest[-4:]
    for j in range(4):
        row=0
        for t in range(count):
            keep,came=ins[2*t],ins[2*t+1]
            rows=keep.shape[1]
            outs[j][0,row:row+rows]=keep[at_ref[j]]+came[at_ref[j]]
            row+=rows


def plane_call(pairs,at,deps,steps=8):
    each=[p[0].shape[1]//steps for p in pairs]
    return pl.pallas_call(functools.partial(plane_kernel,len(pairs)),
        grid_spec=pltpu.PrefetchScalarGridSpec(num_scalar_prefetch=1,grid=(steps,),
            in_specs=[pl.BlockSpec((4,r,128),lambda i,_:(0,i,0)) for r in each for _ in range(2)]+[pl.BlockSpec(memory_space=pl.ANY)]*len(deps),
            out_specs=[pl.BlockSpec((1,sum(each),128),lambda i,_:(i,0,0))]*4),
        out_shape=[jax.ShapeDtypeStruct((steps,sum(each),128),BF)]*4,name="plane",**params())(at,*[x for p in pairs for x in p],*deps)


def line_kernel(*refs):
    ins=refs[:4]
    out,scr,turned=refs[-3:]
    steps,rows,_=ins[0].shape
    main=rows-128
    for i in range(steps):
        v=functools.reduce(jnp.add,[x[i].astype(F32) for x in ins])
        scr[i]=v[:main].astype(BF)
        turned[i]=v[main:].T.astype(BF)
    each=steps//4; size=each*main+32*steps
    for k in range(4):
        for e in range(each):
            out[k*size+e*main:k*size+(e+1)*main]=scr[k*each+e]
        for i in range(steps):
            at=k*size+each*main+32*i
            out[at:at+32]=turned[i,32*k:32*k+32]


def line_call(parts,deps):
    steps,rows,_=parts[0].shape
    shape=(4*(steps//4*(rows-128)+steps*32),128)
    full=pl.BlockSpec(parts[0].shape,lambda i:(0,0,0))
    return pl.pallas_call(line_kernel,grid=(1,),
        in_specs=[full]*4+[pl.BlockSpec(memory_space=pl.ANY)]*len(deps),out_specs=pl.BlockSpec(shape,lambda i:(0,0)),
        scratch_shapes=[pltpu.VMEM((steps,rows-128,128),BF),pltpu.VMEM((steps,128,128),BF)],
        out_shape=jax.ShapeDtypeStruct(shape,BF),name="line",**params())(*parts,*deps)


def stack_kernel(*refs):
    out=refs[-1]
    v=functools.reduce(jnp.add,[r[...].astype(F32) for r in refs[:4]]).astype(BF)
    out[:,:GW]=v[:,:GW]
    for m in range(4):
        for j in range(4): out[32*m:32*m+32,GW+128*j:GW+128*j+128]=v[32*j:32*j+32,GW:]


def stack_call(parts,deps):
    shape=(128,GW+512)
    spec=pl.BlockSpec(parts[0].shape,lambda i:(0,0))
    return pl.pallas_call(stack_kernel,grid=(1,),
        in_specs=[spec]*4+[pl.BlockSpec(memory_space=pl.ANY)]*len(deps),out_specs=pl.BlockSpec(shape,lambda i:(0,0)),
        out_shape=jax.ShapeDtypeStruct(shape,BF),name="stack",**params())(*parts,*deps)


def spread_kernel(sizes,count,at_ref,*rest):
    outs=rest[-count:]
    for j in range(count):
        first=k=0
        for stacks,parts in sizes:
            for t in range(stacks):
                v=rest[k][t,at_ref[j]].astype(F32)
                for p in range(1,parts): v=v+rest[k+p][t,at_ref[j]].astype(F32)
                outs[j][first+t]=v.astype(BF)
            first+=stacks; k+=parts


def spread(groups,at,axis,chunk,deps):
    _,count,rows,cols=groups[0][0].shape
    size=[rows,cols]; size[axis]=chunk
    place=(lambda i: (i,0)) if axis==0 else (lambda i: (0,i))
    stacks=sum(g[0].shape[0] for g in groups)
    return pl.pallas_call(functools.partial(spread_kernel,[(g[0].shape[0],len(g)) for g in groups],count),
        grid_spec=pltpu.PrefetchScalarGridSpec(num_scalar_prefetch=1,grid=((rows,cols)[axis]//chunk,),
            in_specs=[pl.BlockSpec((g[0].shape[0],count,*size),lambda i,_:(0,0,*place(i))) for g in groups for p in g]+[pl.BlockSpec(memory_space=pl.ANY)]*len(deps),
            out_specs=[pl.BlockSpec((stacks,*size),lambda i,_:(0,*place(i)))]*count),
        out_shape=[jax.ShapeDtypeStruct((stacks,rows,cols),BF)]*count,name="spread",**params())(at,*[p for g in groups for p in g],*deps)


def swap(x, axis, bit, count):
    return lax.ppermute(x, axis, [(i, i ^ (1 << bit)) for i in range(count)])


def bit_of(axis, bit):
    return (lax.axis_index(axis) >> bit) & 1


def halve(x, dim, bit, count):
    place = bit_of("rows", bit)
    send = lax.dynamic_index_in_dim(x, 1 - place, dim, keepdims=False)
    keep = lax.dynamic_index_in_dim(x, place, dim, keepdims=False)
    return keep.astype(F32) + swap(send.astype(BF), "rows", bit, count).astype(F32)


def total(parts):
    return functools.reduce(jnp.add, [p.astype(F32) for p in parts])


def send_blocks(blocks, low, count):
    return [blocks[0]] + [
        lax.ppermute(blocks[j], "rows", [(i, i ^ (j << (low + 1))) for i in range(count)]) for j in range(1, 4)
    ]


def send_line(blocks, count):
    return [blocks[0]] + [
        lax.ppermute(blocks[j], "mlp", [(i, (i + j) % count) for i in range(count)]) for j in range(1, count)
    ]


def gather_pieces(x, low, mlps):
    half = x.shape[1] // 256 * 128
    line = [x] + [lax.ppermute(x, "mlp", [(i, (i + step) % mlps) for i in range(mlps)]) for step in range(1, mlps)]
    pieces = []
    for first, cols, bits in ((0, slice(0, half), (1, 2)), (half, slice(half, None), (2, 1))):
        held = [(jnp.concatenate([p[:, cols] for p in line], axis=0), 0)]
        for bit in bits + (0,):
            held = held + [(swap(p, "rows", bit, 8), at ^ (1 << bit)) for p, at in held]
        pieces += [(p, at, first) for p, at in held]
    return pieces


def body(
    tokens,
    doc_lengths,
    cotangent,
    norm_gain_mix,
    w_query,
    w_key,
    w_value,
    w_outgate,
    w_rank,
    w_decay,
    decay_bias,
    head_gain,
    w_output,
    norm_gain_mlp,
    w_gate,
    w_up,
    w_down,
):
    rows = lax.axis_size("rows")
    mlps = lax.axis_size("mlp")
    low = rows.bit_length() - 4
    shard = w_query.shape[0]
    hid, wide = w_down.shape
    lens = doc_lengths.reshape(-1)
    mixer_local = jnp.concatenate(
        [
            w_query, w_key, w_value, w_outgate, w_rank,
            norm_gain_mix[:, None], norm_gain_mlp[:, None], jnp.zeros((shard, 110), BF), w_output.T,
        ],
        axis=1,
    )
    mlp_local = jnp.concatenate([w_gate.T, w_up.T, w_down], axis=0)
    here = lax.axis_index("rows")
    if low == 0:
        mlp_all = lax.all_gather(mlp_local, ("rows", "mlp"), axis=0).reshape(rows, mlps, 3 * hid, 128)
        pieces = gather_pieces(mixer_local, low, mlps)
        at = jnp.concatenate([jnp.arange(8) ^ here, (lax.axis_index("mlp") - jnp.arange(mlps)) % mlps])
    else:
        mlp_all = lax.all_gather(mlp_local, ("rows", "mlp"), axis=0)
        mlp_all = mlp_all.reshape(8, rows // 8, mlps, 3 * hid, wide).transpose(0, 2, 3, 1, 4)
        mlp_all = mlp_all.reshape(8, mlps, 3 * hid, 128)
        whole = lax.all_gather(mixer_local, ("rows", "mlp"), axis=0, tiled=True)
        pieces = [(whole[128 * b : 128 * b + 128], b, 0) for b in range(8)]
        at = jnp.concatenate([jnp.arange(8), jnp.arange(4)])
    decay_wide = jnp.concatenate([w_decay, jnp.zeros((112, DK), BF)], axis=0)
    head_row = head_gain.astype(F32)[None]
    normed_in, q, k, cum, dp, v, gp, o, before, mixed, rank, gains, w_in, w_out = fwd_call(
        lens, at.astype(jnp.int32), tokens, pieces, decay_wide, decay_bias.astype(F32)[None], head_row
    )
    gain_mix, gain_mlp = gains[:1], gains[1:2]
    residual, normed_mid, hidden, grad_gate, grad_up, grad_res, grad_mixed, gain_mlp_part = mlp_call(
        tokens, mixed, cotangent, gain_mlp, w_out, mlp_all, mlps * hid
    )
    mine = bit_of("rows", low).astype(jnp.int32)[None]

    def with_other_core(send, keep):
        return [keep, swap(send, "rows", low, rows)]

    def within(parts, dim):
        if not low:
            return parts
        x = total(parts)
        x = x.reshape(x.shape[:dim] + (2,) * low + (x.shape[dim] >> low,) + x.shape[dim + 1 :])
        for bit in reversed(range(low)):
            x = halve(x, dim, bit, rows)
        return [x.astype(BF)]

    in_plane = ((here >> (low + 1)) ^ jnp.arange(4)).astype(jnp.int32)
    in_line = ((lax.axis_index("mlp") + jnp.arange(mlps)) % mlps).astype(jnp.int32)
    down_send, down_keep = dw_call([hidden], cotangent, mine, [normed_mid], 1408)
    down = with_other_core(down_send, down_keep)
    gate_send, gate_keep, up_send, up_keep = dw_call([grad_gate, grad_up], normed_mid, mine, [down_keep], 1408)
    gate = with_other_core(gate_send, gate_keep)
    up = with_other_core(up_send, up_keep)
    out_send, out_keep = dw_call([mixed], grad_mixed, mine, [gate_keep, down[1]], 512)
    out = with_other_core(out_send, out_keep)
    blocks = plane_call([gate, up, down, out], in_plane, [])
    common = (lens, grad_mixed, w_out, decay_wide, head_row, q, k, cum, dp, v, gp, o, before, rank)
    grads, small, deps = None, [], list(blocks)
    for seq in reversed(range(doc_lengths.shape[0])):
        grads, *sums = bwd_call(seq, grads, deps, *common)
        small += sums
        deps = []
    in_send, in_keep = dw_call([grads], normed_in, mine, [], 1664, wide=False, extra=small + [gain_mlp_part])
    if low:
        small = [total(small[t::3]) for t in range(3)]
        small = jnp.concatenate(
            [small[0][:16].reshape(16, 4, 128).transpose(1, 0, 2).reshape(-1)]
            + [p.sum(0) for p in (small[1], small[2], gain_mlp_part)]
        ).reshape(-1, 128)
        small = lax.all_gather(small, ("rows", "mlp"), axis=0).sum(0)
    inner = with_other_core(in_send, in_keep)
    grad_tokens = dx_call(0, 2, None, grads, w_in, tokens, gain_mix, grad_res, [in_keep], 5 * 10**10)
    inner = spread([[p[None] for p in inner]], in_plane, 1, 1664, [grad_tokens])
    blocks = send_blocks(blocks, low, rows)
    if low:
        blocks = total(blocks)
        main = blocks[:, :-128].reshape(8, 3, -1, 128).transpose(1, 0, 2, 3).reshape(3, mlps, hid, 128)
        main = within([main], 3)[0]
        out = within([blocks[:, -128:].reshape(-1, 128)], 1)[0].reshape(DV, mlps, shard)
        main = send_line([jnp.take(main, in_line[j], axis=1) for j in range(mlps)], mlps)
        out = send_line([jnp.take(out, in_line[j], axis=1) for j in range(mlps)], mlps)
        deps = list(inner)
    else:
        blocks = line_call(blocks, list(inner))
        main = lax.psum_scatter(blocks, "mlp", scatter_dimension=0, tiled=True)
        deps = [blocks]
    blocks = inner
    grad_tokens = dx_call(1, 2, grad_tokens, grads, w_in, tokens, gain_mix, grad_res, deps)
    block_out = down_call(0, 2, None, residual, hidden, mlp_all, [grad_tokens])
    blocks = within(send_blocks(blocks, low, rows), 1)
    if low:
        blocks = total([b[0] for b in blocks]).astype(BF).reshape(mlps, shard, GW + 128)
    else:
        blocks = stack_call([b[0] for b in blocks], [block_out]).reshape(mlps, shard, GW + 512)
    in_grads = lax.all_to_all(blocks, "mlp", 0, 0, tiled=True)
    block_out = down_call(1, 2, block_out, residual, hidden, mlp_all, [blocks])
    in_grads = total([in_grads[j] for j in range(mlps)])
    if not low:
        small = in_grads[:, GW:].reshape(shard, 4, 128).transpose(1, 0, 2).reshape(128, 128)
    in_grads = in_grads[:, :GW]
    if low:
        mlp_grads, out_grads = total(main), total(out)
    else:
        main = main.astype(F32)
        mlp_grads = main[: 3 * hid].reshape(2, 3, hid // 2, 128).transpose(1, 0, 2, 3).reshape(3, hid, 128)
        out_grads = main[3 * hid :].reshape(8, shard, 128).transpose(0, 2, 1).reshape(DV, shard)
    gain_mix_grad = jnp.sum(in_grads * mixer_local[:, :GW].astype(F32), axis=1) / norm_gain_mix.astype(F32)
    at = (here * mlps + lax.axis_index("mlp")) * shard
    return (
        block_out,
        grad_tokens,
        gain_mix_grad,
        in_grads[:, CQ : CQ + DK],
        in_grads[:, CK : CK + DK],
        in_grads[:, CV : CV + DV],
        in_grads[:, CG : CG + DV],
        in_grads[:, CR : CR + 16],
        small[:64].reshape(4, 16, 128).transpose(1, 0, 2).reshape(16, DK),
        small[64:68].reshape(-1),
        small[68:70].reshape(-1),
        out_grads,
        lax.dynamic_slice_in_dim(small[70:78].reshape(-1), at, shard),
        mlp_grads[0].T,
        mlp_grads[1].T,
        mlp_grads[2],
    )


def solution(mesh):
    in_specs = (
        P(("rows", "mlp"), None),
        P(("rows", "mlp"), None),
        P(("rows", "mlp"), None),
        P(("rows", "mlp")),
        P(("rows", "mlp"), None),
        P(("rows", "mlp"), None),
        P(("rows", "mlp"), None),
        P(("rows", "mlp"), None),
        P(("rows", "mlp"), None),
        P(),
        P(),
        P(),
        P(None, ("rows", "mlp")),
        P(("rows", "mlp")),
        P("rows", "mlp"),
        P("rows", "mlp"),
        P("mlp", "rows"),
    )
    out_specs = (
        P(("rows", "mlp"), None),
        P(("rows", "mlp"), None),
        P(("rows", "mlp")),
        P(("rows", "mlp"), None),
        P(("rows", "mlp"), None),
        P(("rows", "mlp"), None),
        P(("rows", "mlp"), None),
        P(("rows", "mlp"), None),
        P(),
        P(),
        P(),
        P(None, ("rows", "mlp")),
        P(("rows", "mlp")),
        P("rows", "mlp"),
        P("rows", "mlp"),
        P("mlp", "rows"),
    )
    return jax.shard_map(body, mesh=mesh, in_specs=in_specs, out_specs=out_specs, check_vma=False)
```

```python
import functools

import jax
import jax.numpy as jnp
from jax import lax
from jax.experimental import pallas as pl
from jax.experimental.pallas import tpu as pltpu
from jax.sharding import PartitionSpec as P

F32 = jnp.float32
BF = jnp.bfloat16
EPS = 1e-5
LEN = 1024
BL = 64
H = 4
HK = 128
HV = 256
DK = 512
DV = 1024
CQ, CK, CV, CG, CR, CO = 0, 512, 1024, 2048, 3072, 3200
GW = 3200
SCALE = HK**-0.5
VMEM = 60 * 1024 * 1024


def nn(a,b): return lax.dot_general(a,b,(((1,),(0,)),((),())),preferred_element_type=F32)


def nt(a,b): return lax.dot_general(a,b,(((1,),(1,)),((),())),preferred_element_type=F32)


def tn(a,b): return lax.dot_general(a,b,(((0,),(0,)),((),())),preferred_element_type=F32)


def sigmoid(v): return 1.0/(1.0+jnp.exp(-v))


def softminus(x): return jnp.minimum(x,0.0)-jnp.log1p(jnp.exp(-jnp.abs(x)))


def split(x):
    hi=x.astype(BF); return hi,(x-hi.astype(F32)).astype(BF)


def doc_of(p,starts):
    out=(p>=starts[0]).astype(jnp.int32)
    for s in starts[1:]: out=out+(p>=s).astype(jnp.int32)
    return out


def tile_masks(base,T,starts):
    tc=lax.broadcasted_iota(jnp.int32,(T,1),0); tr=lax.broadcasted_iota(jnp.int32,(1,T),1)
    dc=doc_of(tc+base,starts); dr=doc_of(tr+base,starts)
    first=(tc & ~(BL-1))+base
    prior=jnp.where(first>0,doc_of(first-1,starts),-1)
    last=doc_of(first+(BL-1),starts)
    inter=(dc==prior); reach=(dc==last)
    same=(tc>>6)==(tr>>6)
    low=same&(tc>=tr)
    return inter,reach,same,low,low&(dc==dr)


def keep_of(first,starts):
    return jnp.where(first>0,(doc_of(first-1,starts)==doc_of(first+BL-1,starts)).astype(F32),0.0)


def starts_of(len_ref, seq):
    first = len_ref[seq * 4]
    second = first + len_ref[seq * 4 + 1]
    return [first, second, second + len_ref[seq * 4 + 2]]


def params(flops=1):
    return dict(
        compiler_params=pltpu.CompilerParams(vmem_limit_bytes=VMEM),
        cost_estimate=pl.CostEstimate(flops=flops, bytes_accessed=1, transcendentals=0),
    )


def fwd_kernel(NT,cuts,st_ref,at_ref,tok_ref,wdec_ref,bias_ref,hg_ref,*rest):
    pieces=rest[:len(cuts)]
    n_ref,q_ref,k_ref,cum_ref,dp_ref,v_ref,gp_ref,o_ref,bef_ref,mix_ref,rank_ref,gains_ref,win_ref,wout_ref,state,w_ref,sems,save_sems=rest[len(cuts):]
    T=tok_ref.shape[0]; nb=T//BL
    i=pl.program_id(0); seq=i//NT; tile=i%NT; base=tile*T
    starts=starts_of(st_ref,seq)
    inter,reach,same,low,intra=tile_masks(base,T,starts)
    @pl.when(tile==0)
    def _(): state[...]=jnp.zeros_like(state)
    saves=[pltpu.make_async_copy(w_ref.at[:,pl.ds(0,GW)],win_ref,save_sems.at[0]),pltpu.make_async_copy(w_ref.at[:,pl.ds(GW,DV)],wout_ref,save_sems.at[1])]
    @pl.when(i==0)
    def _():
        copies=[]
        for j,(block,first,width) in enumerate(cuts):
            for z in range(4):
                rows=pl.ds(pl.multiple_of(at_ref[block]*128+at_ref[8+z]*32,32),32)
                copies.append(pltpu.make_async_copy(pieces[j].at[pl.ds(32*z,32)],w_ref.at[rows,pl.ds(first,width)],sems.at[j,z]))
        for c in copies: c.start()
        for c in copies: c.wait()
        for c in saves: c.start()
        gains_ref[...]=w_ref[:,CR:CR+128].astype(F32).T[16:24]
    @pl.when(i==pl.num_programs(0)-1)
    def _():
        for c in saves: c.wait()
    x=tok_ref[...].astype(F32)
    r=lax.rsqrt(jnp.mean(x*x,axis=-1,keepdims=True)+EPS)
    n_ref[...]=(x*r*gains_ref[0:1]).astype(BF)
    n=n_ref[...]
    rank=nn(n,w_ref[:,CR:CR+128]).astype(BF)
    rank_ref[...]=rank
    dp=nn(rank,wdec_ref[...])+bias_ref[...]
    dp_ref[...]=dp
    q_ref[...]=nn(n_ref[...],w_ref[:,CQ:CQ+DK])*SCALE
    k_ref[...]=nn(n_ref[...],w_ref[:,CK:CK+DK])
    dhi,dlo=split(softminus(dp)*(1.0/16.0))
    lowb=low.astype(BF)
    cum=nn(lowb,dhi)+nn(lowb,dlo)
    cum_ref[...]=cum
    heads=range(H)
    sa=[slice(HK*h,HK*h+HK) for h in heads]; sv=[slice(HV*h,HV*h+HV) for h in heads]
    blocks=[slice(BL*b,BL*b+BL) for b in range(nb)]
    for h in heads: v_ref[:,sv[h]]=nn(n_ref[...],w_ref[:,CV+HV*h:CV+HV*h+HV]).astype(BF)
    interf=inter.astype(F32)
    ends=[cum[BL*b+BL-1:BL*b+BL,:] for b in range(nb)]
    endb=jnp.concatenate([jnp.broadcast_to(e,(BL,DK)) for e in ends],axis=0)
    keeps=jnp.concatenate([jnp.exp(ends[b])*keep_of(base+BL*b,starts) for b in range(nb)]+[jnp.zeros((8-nb,DK),F32)],axis=0)
    qgi=[None]*H; kc=[None]*H; s=[None]*H
    for h in heads:
        a=sa[h]; c=cum[:,a]
        qf=q_ref[:,a]*jnp.exp(c); kf=k_ref[:,a]
        qgi[h]=(qf*interf).astype(BF)
        kc[h]=(kf*jnp.exp(endb[:,a]-c)).astype(BF)
        s[h]=jnp.where(intra,nt(qf.astype(BF),(kf*jnp.exp(-c)).astype(BF)),0.0).astype(BF)
    for h in heads: gp_ref[:,sv[h]]=nn(n_ref[...],w_ref[:,CG+HV*h:CG+HV*h+HV]).astype(BF)
    vk=[jnp.where(reach,v_ref[:,sv[h]],jnp.zeros((T,HV),BF)) for h in heads]
    upd=[[tn(kc[h][t],vk[h][t]) for t in blocks] for h in heads]
    kt=[keeps[:,sa[h]].T for h in heads]
    cur=[state[h] for h in heads]
    parts=[[None]*nb for h in heads]
    for b in range(nb):
        for h in heads:
            sb=cur[h].astype(BF)
            bef_ref[b,h]=sb
            parts[h][b]=nn(qgi[h][blocks[b]],sb)
            cur[h]=cur[h]*kt[h][:,b:b+1]+upd[h][b]
    for h in heads: state[h]=cur[h]
    for h in heads:
        c=sv[h]
        o=nn(s[h],v_ref[:,c])+jnp.concatenate(parts[h],axis=0)
        o_ref[:,c]=o
        sc=lax.rsqrt(jnp.maximum(jnp.mean(o*o,axis=-1,keepdims=True),1.0))
        gp=gp_ref[:,c].astype(F32)
        mix_ref[:,c]=(o*sc*hg_ref[...]*(gp*sigmoid(gp))).astype(BF)


def fwd_call(st,at,tok,pieces,wdec,bias,hg,T=256):
    n,d=tok.shape; NT=LEN//T; sd=jax.ShapeDtypeStruct
    row=lambda x: pl.BlockSpec((T,x),lambda i,*s:(i,0))
    const=lambda a: pl.BlockSpec(a.shape,lambda i,*s:(0,0),pipeline_mode=pl.Buffered(1))
    hbm=pl.BlockSpec(memory_space=pl.ANY)
    nb=T//BL
    outs=[(d,BF),(DK,F32),(DK,F32),(DK,F32),(DK,F32),(DV,BF),(DV,BF),(DV,F32),None,(DV,BF),(128,BF)]
    specs=[row(o[0]) if o else pl.BlockSpec((nb,H,HK,HV),lambda i,*s:(i,0,0,0)) for o in outs]
    shapes=[sd((n,o[0]),o[1]) if o else sd((n//BL,H,HK,HV),BF) for o in outs]
    cuts=[(p[1],p[2],p[0].shape[1]) for p in pieces]
    return pl.pallas_call(functools.partial(fwd_kernel,NT,cuts),
        grid_spec=pltpu.PrefetchScalarGridSpec(num_scalar_prefetch=2,grid=(n//T,),
            in_specs=[row(d),const(wdec),const(bias),const(hg)]+[hbm]*len(pieces),out_specs=specs+[pl.BlockSpec((8,d),lambda i,*s:(0,0)),hbm,hbm],
            scratch_shapes=[pltpu.VMEM((H,HK,HV),F32),pltpu.VMEM((d,GW+DV),BF),pltpu.SemaphoreType.DMA((len(pieces),4)),pltpu.SemaphoreType.DMA((2,))]),
        out_shape=shapes+[sd((8,d),F32),sd((d,GW),BF),sd((d,DV),BF)],name="mixer_fwd",**params())(st,at,tok,wdec,bias,hg,*[p[0] for p in pieces])


def bwd_kernel(NT,seq,st_ref,gmix_ref,w_ref,wdec_ref,hg_ref,q_ref,k_ref,cum_ref,dp_ref,v_ref,gp_ref,o_ref,bef_ref,rank_ref,*rest):
    g_ref,dwd_ref,db_ref,dhg_ref,state=rest[-5:]
    T=q_ref.shape[0]; nb=T//BL
    step=pl.program_id(0); tile=NT-1-step; base=tile*T
    starts=starts_of(st_ref,seq)
    inter,reach,same,low,intra=tile_masks(base,T,starts)
    @pl.when(tile==NT-1)
    def _(): state[...]=jnp.zeros_like(state)
    @pl.when(step==0)
    def _():
        dwd_ref[...]=jnp.zeros_like(dwd_ref); db_ref[...]=jnp.zeros_like(db_ref); dhg_ref[...]=jnp.zeros_like(dhg_ref)
    cum=cum_ref[...]
    ends=[cum[BL*b+BL-1:BL*b+BL,:] for b in range(nb)]
    endb=jnp.concatenate([jnp.broadcast_to(e,(BL,DK)) for e in ends],axis=0)
    eg=jnp.exp(cum); es=jnp.exp(-cum); ec=jnp.exp(endb-cum)
    kend=jnp.concatenate([jnp.exp(ends[b])*keep_of(base+BL*b,starts) for b in range(nb)]+[jnp.zeros((8-nb,DK),F32)],axis=0)
    interb=inter.astype(F32).astype(BF); reachf=reach.astype(F32)
    tc=lax.broadcasted_iota(jnp.int32,(T,1),0); tr=lax.broadcasted_iota(jnp.int32,(1,T),1)
    upb=(same&(tc<=tr)).astype(BF); lsb=(same&(tc>tr)).astype(BF)
    hg=hg_ref[...]
    ones=jnp.ones((8,HV),BF)
    heads=range(H)
    sa=[slice(HK*h,HK*h+HK) for h in heads]; sc_=[slice(HV*h,HV*h+HV) for h in heads]
    go=[None]*H; goi=[None]*H
    qs=[q_ref[:,sa[h]]*eg[:,sa[h]] for h in heads]; ks=[k_ref[:,sa[h]]*es[:,sa[h]] for h in heads]; kd=[k_ref[:,sa[h]]*ec[:,sa[h]] for h in heads]
    qg=[x.astype(BF) for x in qs]; kg=[x.astype(BF) for x in ks]; kc=[x.astype(BF) for x in kd]
    sco=[jnp.where(intra,nt(qg[h],kg[h]),0.0).astype(BF) for h in heads]
    for h in heads:
        c=sc_[h]
        gi=nn(gmix_ref[...],w_ref[:,c])
        o=o_ref[:,c]; gp=gp_ref[:,c].astype(F32)
        ms=jnp.mean(o*o,axis=-1,keepdims=True)
        sc=lax.rsqrt(jnp.maximum(ms,1.0))
        hn0=o*sc
        s=sigmoid(gp); si=gp*s
        g_ref[:,CG+HV*h:CG+HV*h+HV]=(gi*hn0*hg*(s+si*(1.0-s))).astype(BF)
        G=gi*si
        dhg_ref[...]+=jnp.sum((G*hn0).reshape(-1,8,HV),axis=0)
        G=G*hg
        innr=jnp.mean(G*o,axis=-1,keepdims=True)*jnp.where(ms>1.0,1.0,0.0)
        go[h]=(sc*G-o*(sc*sc*sc*innr)).astype(BF)
        goi[h]=go[h]*interb
    gs=[jnp.where(intra,nt(go[h],v_ref[:,sc_[h]]),0.0).astype(BF) for h in heads]
    loc=[[tn(qg[h][BL*b:BL*b+BL],goi[h][BL*b:BL*b+BL]) for b in range(nb)] for h in heads]
    kt=[kend[:,sa[h]].T for h in heads]
    sbs=[[None]*nb for h in heads]
    p_end=[[None]*nb for h in heads]
    for b in reversed(range(nb)):
        for h in heads:
            st=state[h] if b==nb-1 else cur[h]
            sbs[h][b]=st.astype(BF)
            m1,m2=split(st*bef_ref[b,h].astype(F32))
            p_end[h][b]=(nt(ones,m1)+nt(ones,m2))[0:1]*kend[b:b+1,sa[h]]
            st=(loc[h][b]+kt[h][:,b:b+1]*st).astype(BF).astype(F32)
            if b==nb-1:
                if h==0: cur=[None]*H
            cur[h]=st
    for h in heads: state[h]=cur[h]
    cat=lambda p: jnp.concatenate(p,axis=0)
    for h in heads:
        a=sa[h]; c=sc_[h]; v=v_ref[:,c]
        tt=[slice(BL*b,BL*b+BL) for b in range(nb)]
        gv=tn(sco[h],go[h])+cat([nn(kc[h][tt[b]],sbs[h][b]) for b in range(nb)])*reachf
        g_ref[:,CV+HV*h:CV+HV*h+HV]=gv.astype(BF)
        gq=nn(gs[h],kg[h])+cat([nt(goi[h][tt[b]],bef_ref[b,h]) for b in range(nb)])
        gk=tn(gs[h],qg[h])
        gkc=cat([nt(v[tt[b]],sbs[h][b]) for b in range(nb)])*reachf
        av1,av2=split(gq*qs[h]-gk*ks[h])
        c1,c2=split(gkc*kd[h])
        endr=cat([jnp.broadcast_to(p,(BL,HK)) for p in p_end[h]])
        gd=nn(upb,av1)+nn(upb,av2)+nn(lsb,c1)+nn(lsb,c2)+endr
        g_ref[:,CQ+HK*h:CQ+HK*h+HK]=(gq*eg[:,a]*SCALE).astype(BF)
        g_ref[:,CK+HK*h:CK+HK*h+HK]=(gk*es[:,a]+gkc*ec[:,a]).astype(BF)
        dp=dp_ref[:,a]
        gpre=(gd*(1.0/16.0)*(1.0/(1.0+jnp.exp(dp)))).astype(BF)
        db_ref[:,a]+=jnp.sum(gpre.astype(F32).reshape(-1,8,HK),axis=0)
        dwd_ref[:,a]+=tn(rank_ref[...],gpre)
        gr=nt(gpre,wdec_ref[:,a])
        grank=gr if h==0 else grank+gr
    g_ref[:,CR:CR+128]=grank.astype(BF)
    g_ref[:,GW:]=jnp.zeros((T,128),BF)


def bwd_call(seq,before_g,deps,st,gmix,w,wdec,hg,q,k,cum,dp,v,gp,o,bef,rank,T=256):
    n,d=gmix.shape; NT=LEN//T; sd=jax.ShapeDtypeStruct; top=seq*NT+NT-1
    row=lambda a: pl.BlockSpec((T,a.shape[1]),lambda i,s:(top-i,0))
    const=lambda a: pl.BlockSpec(a.shape,lambda i,s:(0,0),pipeline_mode=pl.Buffered(1))
    hbm=pl.BlockSpec(memory_space=pl.ANY)
    nb=T//BL
    acc=lambda s: pl.BlockSpec(s,lambda i,_:(0,0))
    more=list(deps)+([before_g] if before_g is not None else [])
    return pl.pallas_call(functools.partial(bwd_kernel,NT,seq),
        grid_spec=pltpu.PrefetchScalarGridSpec(num_scalar_prefetch=1,grid=(NT,),
            in_specs=[row(gmix),const(w),const(wdec),const(hg),row(q),row(k),row(cum),row(dp),row(v),row(gp),row(o),pl.BlockSpec((nb,H,HK,HV),lambda i,s:(top-i,0,0,0)),row(rank)]+[hbm]*len(more),
            out_specs=[pl.BlockSpec((T,GW+128),lambda i,s:(top-i,0)),acc((128,DK)),acc((8,DK)),acc((8,HV))],
            scratch_shapes=[pltpu.VMEM((H,HK,HV),F32)]),
        input_output_aliases={} if before_g is None else {13+len(more):0},
        out_shape=[sd((n,GW+128),BF),sd((128,DK),F32),sd((8,DK),F32),sd((8,HV),F32)],
        name="mixer_bwd",**params())(st,gmix,w,wdec,hg,q,k,cum,dp,v,gp,o,bef,rank,*more)


def dx_kernel(g_ref,w_ref,tok_ref,gain_ref,gres_ref,*rest):
    gt_ref=rest[-1]
    gm=nt(g_ref[:,:GW],w_ref[...])
    x=tok_ref[...].astype(F32)
    r=lax.rsqrt(jnp.mean(x*x,axis=-1,keepdims=True)+EPS)
    sc=gm*gain_ref[...]
    inner=jnp.mean(sc*x,axis=-1,keepdims=True)
    gt_ref[...]=gres_ref[...]+r*sc-x*(r*r*r*inner)


def dx_call(part,parts,begun,g,w,tok,gain,gres,deps,flops=1,T=512):
    n,d=tok.shape; sd=jax.ShapeDtypeStruct; steps=n//T//parts; first=part*steps
    row=lambda a: pl.BlockSpec((T,a.shape[1]),lambda i:(first+i,0))
    const=lambda a: pl.BlockSpec(a.shape,lambda i:(0,0),pipeline_mode=pl.Buffered(1))
    hbm=pl.BlockSpec(memory_space=pl.ANY)
    more=list(deps)+([] if begun is None else [begun])
    return pl.pallas_call(dx_kernel,grid=(steps,),in_specs=[row(g),const(w),row(tok),const(gain),row(gres)]+[hbm]*len(more),
        out_specs=row(gres),out_shape=sd((n,d),F32),input_output_aliases={} if begun is None else {4+len(more):0},
        name="mixer_dx",**params(flops))(g,w,tok,gain,gres,*more)


def load_w(w_hbm,w_ref,sems,stacks):
    blocks,mlps,_,_=w_hbm.shape
    hid=w_ref.shape[1]//mlps
    copies=[pltpu.make_async_copy(w_hbm.at[r,m,pl.ds(s*hid,hid)],w_ref.at[i,pl.ds(m*hid,hid),pl.ds(r*128,128)],sems.at[i,r,m]) for i,s in enumerate(stacks) for m in range(mlps) for r in range(blocks)]
    for c in copies: c.start()
    for c in copies: c.wait()


def mlp_kernel(chunk,tok_ref,mix_ref,cot_ref,gain_ref,wo_ref,w_hbm,res_ref,n_ref,hid_ref,gg_ref,gu_ref,gres_ref,gmix_ref,gn_ref,w_ref,sems):
    @pl.when(pl.program_id(0)==0)
    def _(): load_w(w_hbm,w_ref,sems,(0,1,2))
    wg_ref,wu_ref,wd_ref=w_ref.at[0],w_ref.at[1],w_ref.at[2]
    res=tok_ref[...].astype(F32)+nt(mix_ref[...],wo_ref[...])
    res_ref[...]=res
    gain=gain_ref[...]
    r=lax.rsqrt(jnp.mean(res*res,axis=-1,keepdims=True)+EPS)
    n_ref[...]=(res*r*gain).astype(BF)
    ff=wg_ref.shape[0]
    for c in range(ff//chunk):
        sl=slice(c*chunk,(c+1)*chunk)
        n=n_ref[...]
        gp=nt(n,wg_ref[sl,:]); up=nt(n,wu_ref[sl,:]); gh=nt(cot_ref[...],wd_ref[sl,:])
        s=sigmoid(gp)
        si=gp*s
        hid_ref[:,sl]=(si*up).astype(BF)
        gu_ref[:,sl]=(gh*si).astype(BF)
        gg_ref[:,sl]=(gh*up*(s+si*(1.0-s))).astype(BF)
    gm=nn(gg_ref[...],wg_ref[...])+nn(gu_ref[...],wu_ref[...])
    res=res_ref[...]
    sc=gm*gain
    inner=jnp.mean(sc*res,axis=-1,keepdims=True)
    gi=r*sc-res*(r*r*r*inner)
    gres=cot_ref[...].astype(F32)+gi
    gres_ref[...]=gres
    gmix_ref[...]=gres.astype(BF)
    part=jnp.sum((gm*res*r).reshape(-1,8,gm.shape[1]),axis=0)
    @pl.when(pl.program_id(0)==0)
    def _(): gn_ref[...]=part
    @pl.when(pl.program_id(0)>0)
    def _(): gn_ref[...]+=part


def mlp_call(tok,mix,cot,gain,wo,w,ff,T=256,chunk=256):
    n,d=tok.shape
    row=lambda w: pl.BlockSpec((T,w),lambda i:(i,0))
    const=lambda a: pl.BlockSpec(a.shape,lambda i:(0,0),pipeline_mode=pl.Buffered(1))
    sd=jax.ShapeDtypeStruct
    return pl.pallas_call(functools.partial(mlp_kernel,chunk),grid=(n//T,),
        in_specs=[row(d),row(d),row(d),const(gain),const(wo),pl.BlockSpec(memory_space=pl.ANY)],
        out_specs=[row(d),row(d),row(ff),row(ff),row(ff),row(d),row(d),pl.BlockSpec((8,d),lambda i:(0,0))],
        out_shape=[sd((n,d),F32),sd((n,d),BF),sd((n,ff),BF),sd((n,ff),BF),sd((n,ff),BF),sd((n,d),F32),sd((n,d),BF),sd((8,d),F32)],
        scratch_shapes=[pltpu.VMEM((3,ff,d),BF),pltpu.SemaphoreType.DMA((3,)+w.shape[:2])],
        name="mlp",**params())(tok,mix,cot,gain,wo,w)


def down_kernel(res_ref,hid_ref,w_hbm,*rest):
    o_ref,w_ref,sems=rest[-3:]
    @pl.when(pl.program_id(0)==0)
    def _(): load_w(w_hbm,w_ref,sems,(2,))
    o_ref[...]=(res_ref[...]+nn(hid_ref[...],w_ref[0])).astype(BF)


def down_call(part,parts,begun,res,hid,w,deps,T=256):
    n,d=res.shape; ff=hid.shape[1]; steps=n//T//parts; first=part*steps
    row=lambda w: pl.BlockSpec((T,w),lambda i:(first+i,0))
    hbm=pl.BlockSpec(memory_space=pl.ANY)
    more=list(deps)+([] if begun is None else [begun])
    return pl.pallas_call(down_kernel,grid=(steps,),in_specs=[row(d),row(ff),hbm]+[hbm]*len(more),out_specs=row(d),
        out_shape=jax.ShapeDtypeStruct((n,d),BF),input_output_aliases={} if begun is None else {2+len(more):0},
        scratch_shapes=[pltpu.VMEM((1,ff,d),BF),pltpu.SemaphoreType.DMA((1,)+w.shape[:2])],
        name="mlp_down",**params())(res,hid,w,*more)


def small_block(refs):
    *parts,gain=refs
    v=[functools.reduce(jnp.add,[p[...] for p in parts[t::3]]) for t in range(3)]+[gain[...]]
    rows=[v[0][:16,128*j:128*j+128] for j in range(4)]
    for x in v[1:]:
        x=jnp.sum(x,axis=0,keepdims=True)
        rows+=[x[:,128*j:128*j+128] for j in range(x.shape[1]//128)]
    rows.append(jnp.zeros((128-64-4-2-8,128),F32))
    return jnp.concatenate(rows,axis=0).astype(BF)


def dw_kernel(count,wide,extra,sel_ref,*rest):
    g_refs=rest[:count]; x_hbm=rest[count]
    outs=rest[-2*count-2:-2]; xp,sems=rest[-2:]
    i=pl.program_id(0); steps=pl.num_programs(0)//count
    @pl.when(i==0)
    def _():
        copies=[]
        for p in range(2):
            for j in range(4):
                at=pl.multiple_of((2*j+(1-sel_ref[0] if p==0 else sel_ref[0]))*128,128)
                copies.append(pltpu.make_async_copy(x_hbm.at[:,pl.ds(at,128)],xp.at[:,pl.ds(512*p+128*j,128)],sems.at[p,j]))
        for c in copies: c.start()
        for c in copies: c.wait()
    for s in range(count):
        @pl.when(i//steps==s)
        def _():
            o=tn(g_refs[s][...],xp[...]) if wide else tn(xp[...],g_refs[s][...])
            for p in range(2):
                for j in range(4):
                    b=slice(512*p+128*j,512*p+128*j+128)
                    outs[2*s+p][j]=(o[:,b] if wide else o[b,:]).astype(BF)
    if extra:
        @pl.when(i==pl.num_programs(0)-1)
        def _():
            for p in range(2):
                for j in range(4): outs[p][j,:,-128:]=small_block(rest[count+1:count+1+extra])


def dw_call(gs,x,sel,deps,chunk,wide=True,extra=()):
    n,ff=gs[0].shape
    d=x.shape[1]; steps=ff//chunk; count=len(gs)
    hbm=pl.BlockSpec(memory_space=pl.ANY)
    spot=lambda i,s: jnp.clip(i-s*steps,0,steps-1)
    def out(s):
        return pl.BlockSpec((4,chunk,128),lambda i,_:(0,spot(i,s),0)) if wide else pl.BlockSpec((4,128,chunk),lambda i,_:(0,0,spot(i,s)))
    more=[pl.BlockSpec(e.shape,lambda i,_:(0,0)) for e in extra]
    def inp(s):
        return pl.BlockSpec((n,chunk),lambda i,_:(0,spot(i,s)))
    return pl.pallas_call(functools.partial(dw_kernel,count,wide,len(extra)),
        grid_spec=pltpu.PrefetchScalarGridSpec(num_scalar_prefetch=1,grid=(steps*count,),
            in_specs=[inp(s) for s in range(count)]+[hbm]+more+[hbm]*len(deps),
            out_specs=[out(s) for s in range(count) for _ in range(2)],
            scratch_shapes=[pltpu.VMEM((n,d),BF),pltpu.SemaphoreType.DMA((2,4))]),
        out_shape=[jax.ShapeDtypeStruct((4,ff,128) if wide else (4,128,ff),BF)]*(2*count),
        name="grad_w",**params(10**11 if wide else 1))(sel,*gs,x,*extra,*deps)


def plane_kernel(count,at_ref,*rest):
    ins,outs=rest[:2*count],rest[-4:]
    for j in range(4):
        row=0
        for t in range(count):
            keep,came=ins[2*t],ins[2*t+1]
            rows=keep.shape[1]
            outs[j][0,row:row+rows]=keep[at_ref[j]]+came[at_ref[j]]
            row+=rows


def plane_call(pairs,at,deps,steps=8):
    each=[p[0].shape[1]//steps for p in pairs]
    return pl.pallas_call(functools.partial(plane_kernel,len(pairs)),
        grid_spec=pltpu.PrefetchScalarGridSpec(num_scalar_prefetch=1,grid=(steps,),
            in_specs=[pl.BlockSpec((4,r,128),lambda i,_:(0,i,0)) for r in each for _ in range(2)]+[pl.BlockSpec(memory_space=pl.ANY)]*len(deps),
            out_specs=[pl.BlockSpec((1,sum(each),128),lambda i,_:(i,0,0))]*4),
        out_shape=[jax.ShapeDtypeStruct((steps,sum(each),128),BF)]*4,name="plane",**params())(at,*[x for p in pairs for x in p],*deps)


def line_kernel(*refs):
    ins=refs[:4]
    out,scr,turned=refs[-3:]
    steps,rows,_=ins[0].shape
    main=rows-128
    for i in range(steps):
        v=functools.reduce(jnp.add,[x[i].astype(F32) for x in ins])
        scr[i]=v[:main].astype(BF)
        turned[i]=v[main:].T.astype(BF)
    each=steps//4; size=each*main+32*steps
    for k in range(4):
        for e in range(each):
            out[k*size+e*main:k*size+(e+1)*main]=scr[k*each+e]
        for i in range(steps):
            at=k*size+each*main+32*i
            out[at:at+32]=turned[i,32*k:32*k+32]


def line_call(parts,deps):
    steps,rows,_=parts[0].shape
    shape=(4*(steps//4*(rows-128)+steps*32),128)
    full=pl.BlockSpec(parts[0].shape,lambda i:(0,0,0))
    return pl.pallas_call(line_kernel,grid=(1,),
        in_specs=[full]*4+[pl.BlockSpec(memory_space=pl.ANY)]*len(deps),out_specs=pl.BlockSpec(shape,lambda i:(0,0)),
        scratch_shapes=[pltpu.VMEM((steps,rows-128,128),BF),pltpu.VMEM((steps,128,128),BF)],
        out_shape=jax.ShapeDtypeStruct(shape,BF),name="line",**params())(*parts,*deps)


def stack_kernel(*refs):
    out=refs[-1]
    v=functools.reduce(jnp.add,[r[...].astype(F32) for r in refs[:4]]).astype(BF)
    out[:,:GW]=v[:,:GW]
    for m in range(4):
        for j in range(4): out[32*m:32*m+32,GW+128*j:GW+128*j+128]=v[32*j:32*j+32,GW:]


def stack_call(parts,deps):
    shape=(128,GW+512)
    spec=pl.BlockSpec(parts[0].shape,lambda i:(0,0))
    return pl.pallas_call(stack_kernel,grid=(1,),
        in_specs=[spec]*4+[pl.BlockSpec(memory_space=pl.ANY)]*len(deps),out_specs=pl.BlockSpec(shape,lambda i:(0,0)),
        out_shape=jax.ShapeDtypeStruct(shape,BF),name="stack",**params())(*parts,*deps)


def spread_kernel(sizes,count,at_ref,*rest):
    outs=rest[-count:]
    for j in range(count):
        first=k=0
        for stacks,parts in sizes:
            for t in range(stacks):
                v=rest[k][t,at_ref[j]].astype(F32)
                for p in range(1,parts): v=v+rest[k+p][t,at_ref[j]].astype(F32)
                outs[j][first+t]=v.astype(BF)
            first+=stacks; k+=parts


def spread(groups,at,axis,chunk,deps):
    _,count,rows,cols=groups[0][0].shape
    size=[rows,cols]; size[axis]=chunk
    place=(lambda i: (i,0)) if axis==0 else (lambda i: (0,i))
    stacks=sum(g[0].shape[0] for g in groups)
    return pl.pallas_call(functools.partial(spread_kernel,[(g[0].shape[0],len(g)) for g in groups],count),
        grid_spec=pltpu.PrefetchScalarGridSpec(num_scalar_prefetch=1,grid=((rows,cols)[axis]//chunk,),
            in_specs=[pl.BlockSpec((g[0].shape[0],count,*size),lambda i,_:(0,0,*place(i))) for g in groups for p in g]+[pl.BlockSpec(memory_space=pl.ANY)]*len(deps),
            out_specs=[pl.BlockSpec((stacks,*size),lambda i,_:(0,*place(i)))]*count),
        out_shape=[jax.ShapeDtypeStruct((stacks,rows,cols),BF)]*count,name="spread",**params())(at,*[p for g in groups for p in g],*deps)


def swap(x, axis, bit, count):
    return lax.ppermute(x, axis, [(i, i ^ (1 << bit)) for i in range(count)])


def bit_of(axis, bit):
    return (lax.axis_index(axis) >> bit) & 1


def halve(x, dim, bit, count):
    place = bit_of("rows", bit)
    send = lax.dynamic_index_in_dim(x, 1 - place, dim, keepdims=False)
    keep = lax.dynamic_index_in_dim(x, place, dim, keepdims=False)
    return keep.astype(F32) + swap(send.astype(BF), "rows", bit, count).astype(F32)


def total(parts):
    return functools.reduce(jnp.add, [p.astype(F32) for p in parts])


def send_blocks(blocks, low, count):
    return [blocks[0]] + [
        lax.ppermute(blocks[j], "rows", [(i, i ^ (j << (low + 1))) for i in range(count)]) for j in range(1, 4)
    ]


def send_line(blocks, count):
    return [blocks[0]] + [
        lax.ppermute(blocks[j], "mlp", [(i, (i + j) % count) for i in range(count)]) for j in range(1, count)
    ]


def gather_pieces(x, low, mlps):
    half = x.shape[1] // 256 * 128
    line = [x] + [lax.ppermute(x, "mlp", [(i, (i + step) % mlps) for i in range(mlps)]) for step in range(1, mlps)]
    pieces = []
    for first, cols, bits in ((0, slice(0, half), (1, 2)), (half, slice(half, None), (2, 1))):
        held = [(jnp.concatenate([p[:, cols] for p in line], axis=0), 0)]
        for bit in bits + (0,):
            held = held + [(swap(p, "rows", bit, 8), at ^ (1 << bit)) for p, at in held]
        pieces += [(p, at, first) for p, at in held]
    return pieces


def body(
    tokens,
    doc_lengths,
    cotangent,
    norm_gain_mix,
    w_query,
    w_key,
    w_value,
    w_outgate,
    w_rank,
    w_decay,
    decay_bias,
    head_gain,
    w_output,
    norm_gain_mlp,
    w_gate,
    w_up,
    w_down,
):
    rows = lax.axis_size("rows")
    mlps = lax.axis_size("mlp")
    low = rows.bit_length() - 4
    shard = w_query.shape[0]
    hid, wide = w_down.shape
    lens = doc_lengths.reshape(-1)
    mixer_local = jnp.concatenate(
        [
            w_query, w_key, w_value, w_outgate, w_rank,
            norm_gain_mix[:, None], norm_gain_mlp[:, None], jnp.zeros((shard, 110), BF), w_output.T,
        ],
        axis=1,
    )
    mlp_local = jnp.concatenate([w_gate.T, w_up.T, w_down], axis=0)
    here = lax.axis_index("rows")
    if low == 0:
        mlp_all = lax.all_gather(mlp_local, ("rows", "mlp"), axis=0).reshape(rows, mlps, 3 * hid, 128)
        pieces = gather_pieces(mixer_local, low, mlps)
        at = jnp.concatenate([jnp.arange(8) ^ here, (lax.axis_index("mlp") - jnp.arange(mlps)) % mlps])
    else:
        mlp_all = lax.all_gather(mlp_local, ("rows", "mlp"), axis=0)
        mlp_all = mlp_all.reshape(8, rows // 8, mlps, 3 * hid, wide).transpose(0, 2, 3, 1, 4)
        mlp_all = mlp_all.reshape(8, mlps, 3 * hid, 128)
        whole = lax.all_gather(mixer_local, ("rows", "mlp"), axis=0, tiled=True)
        pieces = [(whole[128 * b : 128 * b + 128], b, 0) for b in range(8)]
        at = jnp.concatenate([jnp.arange(8), jnp.arange(4)])
    decay_wide = jnp.concatenate([w_decay, jnp.zeros((112, DK), BF)], axis=0)
    head_row = head_gain.astype(F32)[None]
    normed_in, q, k, cum, dp, v, gp, o, before, mixed, rank, gains, w_in, w_out = fwd_call(
        lens, at.astype(jnp.int32), tokens, pieces, decay_wide, decay_bias.astype(F32)[None], head_row
    )
    gain_mix, gain_mlp = gains[:1], gains[1:2]
    residual, normed_mid, hidden, grad_gate, grad_up, grad_res, grad_mixed, gain_mlp_part = mlp_call(
        tokens, mixed, cotangent, gain_mlp, w_out, mlp_all, mlps * hid
    )
    mine = bit_of("rows", low).astype(jnp.int32)[None]

    def with_other_core(send, keep):
        return [keep, swap(send, "rows", low, rows)]

    def within(parts, dim):
        if not low:
            return parts
        x = total(parts)
        x = x.reshape(x.shape[:dim] + (2,) * low + (x.shape[dim] >> low,) + x.shape[dim + 1 :])
        for bit in reversed(range(low)):
            x = halve(x, dim, bit, rows)
        return [x.astype(BF)]

    in_plane = ((here >> (low + 1)) ^ jnp.arange(4)).astype(jnp.int32)
    in_line = ((lax.axis_index("mlp") + jnp.arange(mlps)) % mlps).astype(jnp.int32)
    down_send, down_keep = dw_call([hidden], cotangent, mine, [normed_mid], 1408)
    down = with_other_core(down_send, down_keep)
    gate_send, gate_keep, up_send, up_keep = dw_call([grad_gate, grad_up], normed_mid, mine, [down_keep], 1408)
    gate = with_other_core(gate_send, gate_keep)
    up = with_other_core(up_send, up_keep)
    out_send, out_keep = dw_call([mixed], grad_mixed, mine, [gate_keep, down[1]], 512)
    out = with_other_core(out_send, out_keep)
    blocks = plane_call([gate, up, down, out], in_plane, [])
    common = (lens, grad_mixed, w_out, decay_wide, head_row, q, k, cum, dp, v, gp, o, before, rank)
    grads, small, deps = None, [], list(blocks)
    for seq in reversed(range(doc_lengths.shape[0])):
        grads, *sums = bwd_call(seq, grads, deps, *common)
        small += sums
        deps = []
    in_send, in_keep = dw_call([grads], normed_in, mine, [], 1664, wide=False, extra=small + [gain_mlp_part])
    if low:
        small = [total(small[t::3]) for t in range(3)]
        small = jnp.concatenate(
            [small[0][:16].reshape(16, 4, 128).transpose(1, 0, 2).reshape(-1)]
            + [p.sum(0) for p in (small[1], small[2], gain_mlp_part)]
        ).reshape(-1, 128)
        small = lax.all_gather(small, ("rows", "mlp"), axis=0).sum(0)
    inner = with_other_core(in_send, in_keep)
    grad_tokens = dx_call(0, 2, None, grads, w_in, tokens, gain_mix, grad_res, [in_keep], 5 * 10**10)
    inner = spread([[p[None] for p in inner]], in_plane, 1, 1664, [grad_tokens])
    blocks = send_blocks(blocks, low, rows)
    if low:
        blocks = total(blocks)
        main = blocks[:, :-128].reshape(8, 3, -1, 128).transpose(1, 0, 2, 3).reshape(3, mlps, hid, 128)
        main = within([main], 3)[0]
        out = within([blocks[:, -128:].reshape(-1, 128)], 1)[0].reshape(DV, mlps, shard)
        main = send_line([jnp.take(main, in_line[j], axis=1) for j in range(mlps)], mlps)
        out = send_line([jnp.take(out, in_line[j], axis=1) for j in range(mlps)], mlps)
        deps = list(inner)
    else:
        blocks = line_call(blocks, list(inner))
        main = lax.psum_scatter(blocks, "mlp", scatter_dimension=0, tiled=True)
        deps = [blocks]
    blocks = inner
    grad_tokens = dx_call(1, 2, grad_tokens, grads, w_in, tokens, gain_mix, grad_res, deps)
    block_out = down_call(0, 2, None, residual, hidden, mlp_all, [grad_tokens])
    blocks = within(send_blocks(blocks, low, rows), 1)
    if low:
        blocks = total([b[0] for b in blocks]).astype(BF).reshape(mlps, shard, GW + 128)
    else:
        blocks = stack_call([b[0] for b in blocks], [block_out]).reshape(mlps, shard, GW + 512)
    in_grads = lax.all_to_all(blocks, "mlp", 0, 0, tiled=True)
    block_out = down_call(1, 2, block_out, residual, hidden, mlp_all, [blocks])
    in_grads = total([in_grads[j] for j in range(mlps)])
    if not low:
        small = in_grads[:, GW:].reshape(shard, 4, 128).transpose(1, 0, 2).reshape(128, 128)
    in_grads = in_grads[:, :GW]
    if low:
        mlp_grads, out_grads = total(main), total(out)
    else:
        main = main.astype(F32)
        mlp_grads = main[: 3 * hid].reshape(2, 3, hid // 2, 128).transpose(1, 0, 2, 3).reshape(3, hid, 128)
        out_grads = main[3 * hid :].reshape(8, shard, 128).transpose(0, 2, 1).reshape(DV, shard)
    gain_mix_grad = jnp.sum(in_grads * mixer_local[:, :GW].astype(F32), axis=1) / norm_gain_mix.astype(F32)
    at = (here * mlps + lax.axis_index("mlp")) * shard
    return (
        block_out,
        grad_tokens,
        gain_mix_grad,
        in_grads[:, CQ : CQ + DK],
        in_grads[:, CK : CK + DK],
        in_grads[:, CV : CV + DV],
        in_grads[:, CG : CG + DV],
        in_grads[:, CR : CR + 16],
        small[:64].reshape(4, 16, 128).transpose(1, 0, 2).reshape(16, DK),
        small[64:68].reshape(-1),
        small[68:70].reshape(-1),
        out_grads,
        lax.dynamic_slice_in_dim(small[70:78].reshape(-1), at, shard),
        mlp_grads[0].T,
        mlp_grads[1].T,
        mlp_grads[2],
    )


def solution(mesh):
    in_specs = (
        P(("rows", "mlp"), None),
        P(("rows", "mlp"), None),
        P(("rows", "mlp"), None),
        P(("rows", "mlp")),
        P(("rows", "mlp"), None),
        P(("rows", "mlp"), None),
        P(("rows", "mlp"), None),
        P(("rows", "mlp"), None),
        P(("rows", "mlp"), None),
        P(),
        P(),
        P(),
        P(None, ("rows", "mlp")),
        P(("rows", "mlp")),
        P("rows", "mlp"),
        P("rows", "mlp"),
        P("mlp", "rows"),
    )
    out_specs = (
        P(("rows", "mlp"), None),
        P(("rows", "mlp"), None),
        P(("rows", "mlp")),
        P(("rows", "mlp"), None),
        P(("rows", "mlp"), None),
        P(("rows", "mlp"), None),
        P(("rows", "mlp"), None),
        P(("rows", "mlp"), None),
        P(),
        P(),
        P(),
        P(None, ("rows", "mlp")),
        P(("rows", "mlp")),
        P("rows", "mlp"),
        P("rows", "mlp"),
        P("mlp", "rows"),
    )
    return jax.shard_map(body, mesh=mesh, in_specs=in_specs, out_specs=out_specs, check_vma=False)
```
